128 devices in a mesh: fsdp: 8 (over x, y_lo), seq: 16 (over y_hi, z, core).
Axes of the slice: x: 4, y: 4 (y_hi: 2, y_lo: 2; y = y_hi * 2 + y_lo), z: 4, core: 2. Of those that a mesh axis runs over, the one named last changes fastest.
Arguments:
- inputs: bfloat16 [20480, 1024], P(('fsdp', 'seq')), may hold values from -6 to 6
- image_ids: int32 [20480], P('fsdp'), may hold values from 0 to 3, as said below
- ln1_gain: bfloat16 [1024], P(('fsdp', 'seq')), may hold values from 0.5 to 1.5
- ln1_shift: bfloat16 [1024], P(('fsdp', 'seq')), may hold values from -1.796875 to 1.796875
- qkv_weight: bfloat16 [1024, 3072], P(('fsdp', 'seq')), may hold values from -0.1875 to 0.1875
- query_bias: bfloat16 [1024], P(('fsdp', 'seq')), may hold values from -1.796875 to 1.796875
- value_bias: bfloat16 [1024], P(('fsdp', 'seq')), may hold values from -0.1796875 to 0.1796875
- out_weight: bfloat16 [1024, 1024], P(('fsdp', 'seq')), may hold values from -6 to 6
- out_bias: bfloat16 [1024], P(('fsdp', 'seq')), may hold values from -1.796875 to 1.796875
- ln2_gain: bfloat16 [1024], P(('fsdp', 'seq')), may hold values from 0.5 to 1.5
- ln2_shift: bfloat16 [1024], P(('fsdp', 'seq')), may hold values from -1.796875 to 1.796875
- fc1_weight: bfloat16 [1024, 4096], P(('fsdp', 'seq')), may hold values from -0.1875 to 0.1875
- fc1_bias: bfloat16 [4096], P(('fsdp', 'seq')), may hold values from -1.796875 to 1.796875
- fc2_weight: bfloat16 [4096, 1024], P(('fsdp', 'seq')), may hold values from -0.09375 to 0.09375
- fc2_bias: bfloat16 [1024], P(('fsdp', 'seq')), may hold values from -1.796875 to 1.796875
- out_grad: bfloat16 [20480, 1024], P(('fsdp', 'seq')), may hold values from -6 to 6
Outputs:
- block_output: bfloat16 [20480, 1024], P(('fsdp', 'seq'))
- input_grad: bfloat16 [20480, 1024], P(('fsdp', 'seq'))
- ln1_gain_grad: float32 [1024], P(('fsdp', 'seq'))
- ln1_shift_grad: float32 [1024], P(('fsdp', 'seq'))
- qkv_weight_grad: float32 [1024, 3072], P(('fsdp', 'seq'))
- query_bias_grad: float32 [1024], P(('fsdp', 'seq'))
- value_bias_grad: float32 [1024], P(('fsdp', 'seq'))
- out_weight_grad: float32 [1024, 1024], P(('fsdp', 'seq'))
- out_bias_grad: float32 [1024], P(('fsdp', 'seq'))
- ln2_gain_grad: float32 [1024], P(('fsdp', 'seq'))
- ln2_shift_grad: float32 [1024], P(('fsdp', 'seq'))
- fc1_weight_grad: float32 [1024, 4096], P(('fsdp', 'seq'))
- fc1_bias_grad: float32 [4096], P(('fsdp', 'seq'))
- fc2_weight_grad: float32 [4096, 1024], P(('fsdp', 'seq'))
- fc2_bias_grad: float32 [1024], P(('fsdp', 'seq'))
The draws below stay inside these ranges and needn't reach their ends.
Inputs may be any that keep to these rules, and one draw needn't show every extreme that they name: Within each group of 2560 tokens image_ids never falls along the tokens; tokens with one number form one image; in every group one image starts among the group's first 160 tokens and ends among its last 160.
All inputs are finite; a program needn't handle non-finite values.
Results may differ from the reference program's by a relative error of at most 0.01225.
Values may be sent and summed in bfloat16 or wider, within the bound.
No kernel may reach another device: no remote copies, remote signals or barrier semaphores. Data moves between devices by JAX's collectives and lax.ppermute only.
A program may use at most 256 MiB of HBM per device.

```python
import jax
import jax.numpy as jnp
from jax import lax

D = 1024
FF = 4096
HEADS = 16
HEAD_DIM = 64
TOK_DEV = 160
GROUP = 2560
TOKENS = 20480
N_FSDP = 8
N_SEQ = 16


def draw_image_ids(key, part):
    key = jax.random.fold_in(key, 7)
    group_rows = N_SEQ * TOK_DEV
    first_key, second_key, third_key = jax.random.split(key, 3)
    first = jax.random.randint(first_key, (N_FSDP, 1), 0, TOK_DEV)
    second = jax.random.randint(second_key, (N_FSDP, 1), (N_SEQ - 1) * TOK_DEV + 1, group_rows + 1)
    extra = jax.random.randint(third_key, (N_FSDP, 1), 0, group_rows + 1)
    third = jnp.maximum(second, extra)
    places = jnp.arange(group_rows, dtype=jnp.int32)[None, :]
    numbers = (places >= first).astype(jnp.int32) + (places >= second).astype(jnp.int32)
    numbers = numbers + (places >= third).astype(jnp.int32)
    return numbers.reshape(-1)


def levels(stream_key, shape, cuts, least, top_value):
    level = 1.0
    for dim, shards_of in cuts:
        draws = jax.random.uniform(jax.random.fold_in(jax.random.fold_in(stream_key, 6), dim), (shards_of,), jnp.float32, least / len(cuts), top_value / len(cuts))
        level = level * jnp.repeat(jnp.exp(draws), shape[dim] // shards_of).reshape((-1,) + (1,) * (len(shape) - 1 - dim))
    return level


def noise(own_key, dims, scale, most, cuts=(), held_as=jnp.bfloat16):
    result = scale * jax.random.normal(own_key, dims, jnp.float32)
    if cuts:
        result = result * levels(own_key, dims, cuts, -0.22, 0.18)
    return jnp.clip(result, -most, most).astype(held_as)


def setup_inputs(seed: int = 0) -> dict:
    arg_keys = jax.random.split(jax.random.key(seed), 17)
    return {
        "inputs": noise(arg_keys[0], (TOKENS, D), 1.0, 6.0, ((0, 128),)),
        "image_ids": draw_image_ids(jax.random.fold_in(arg_keys[16], 71), 0),
        "ln1_gain": jnp.clip(1.0 + 0.1 * jax.random.normal(arg_keys[2], (D,), jnp.float32), 0.5, 1.5).astype(jnp.bfloat16),
        "ln1_shift": noise(arg_keys[3], (D,), 0.3, 1.796875, ((0, 128),)),
        "qkv_weight": noise(arg_keys[4], (D, 3 * D), D ** -0.5, 0.1875, ((0, 128),)),
        "query_bias": noise(arg_keys[5], (D,), 0.3, 1.796875, ((0, 128),)),
        "value_bias": noise(arg_keys[6], (D,), 0.03, 0.1796875, ((0, 128),)),
        "out_weight": noise(arg_keys[7], (D, D), (max(1, D * 4 // GROUP)) ** -0.5, 6.0, ((0, 128),)),
        "out_bias": noise(arg_keys[8], (D,), 0.3, 1.796875, ((0, 128),)),
        "ln2_gain": jnp.clip(1.0 + 0.1 * jax.random.normal(arg_keys[9], (D,), jnp.float32), 0.5, 1.5).astype(jnp.bfloat16),
        "ln2_shift": noise(arg_keys[10], (D,), 0.3, 1.796875, ((0, 128),)),
        "fc1_weight": noise(arg_keys[11], (D, FF), D ** -0.5, 0.1875, ((0, 128),)),
        "fc1_bias": noise(arg_keys[12], (FF,), 0.3, 1.796875, ((0, 128),)),
        "fc2_weight": noise(arg_keys[13], (FF, D), FF ** -0.5, 0.09375, ((0, 128),)),
        "fc2_bias": noise(arg_keys[14], (D,), 0.3, 1.796875, ((0, 128),)),
        "out_grad": noise(arg_keys[15], (TOKENS, D), 1.0, 6.0, ((0, 128),)),
    }


EPSILON = 1e-06
NEGATIVE = -1e+30
HIGHEST = lax.Precision.HIGHEST

@jax.custom_vjp
def low(v):
    return lax.optimization_barrier(v.astype(jnp.bfloat16)).astype(jnp.float32)

@jax.custom_vjp
def low_back(v):
    return v

def low_keep(v):
    return (low(v), None)

def low_pass(kept, grad):
    return (grad,)

def back_keep(v):
    return (v, None)

def back_low(kept, grad):
    return (low(grad),)
low.defvjp(low_keep, low_pass)
low_back.defvjp(back_keep, back_low)

def layer_norm(values, gain, shift):
    center = values - lax.optimization_barrier(jnp.mean(values, -1, keepdims=True))
    spread = lax.optimization_barrier(jnp.mean(center * center, -1, keepdims=True))
    return center * lax.rsqrt(spread + EPSILON) * gain + shift

def matmul(left, right):
    return jnp.dot(left, right, precision=HIGHEST, preferred_element_type=jnp.float32)

def attention(queries, key_rows, value_rows, group_ids):
    scale = HEAD_DIM ** (-0.5)
    query_block = min(512, GROUP)
    heads_q = queries.reshape(GROUP // query_block, query_block, HEADS, HEAD_DIM)
    heads_k = key_rows.reshape(GROUP, HEADS, HEAD_DIM)
    heads_v = value_rows.reshape(GROUP, HEADS, HEAD_DIM)
    ids_q = group_ids.reshape(GROUP // query_block, query_block)

    def one_block(pieces):
        block_q, block_ids = pieces
        raw = jnp.einsum('qhe,khe->hqk', block_q, heads_k, precision=HIGHEST)
        keep = (block_ids[:, None] == group_ids[None, :])[None]
        scores = jnp.where(keep, low_back(raw) * scale, NEGATIVE)
        row_top = lax.optimization_barrier(jnp.max(scores, -1, keepdims=True))
        row_total = lax.optimization_barrier(jnp.sum(jnp.where(keep, jnp.exp(scores - row_top), 0.0), -1, keepdims=True))
        log_total = row_top + jnp.log(row_total)
        weights = low(jnp.where(keep, jnp.exp(scores - log_total), 0.0))
        return jnp.einsum('hqk,khe->qhe', weights, heads_v, precision=HIGHEST)
    outputs = lax.map(jax.checkpoint(one_block), (heads_q, ids_q))
    return outputs.reshape(GROUP, HEADS * HEAD_DIM)

def group_layer(params, group_x, group_ids):
    gain_one, shift_one, w_qkv, bias_q, bias_v, w_out, bias_out, gain_two, shift_two, w_fc1, bias_fc1, w_fc2, bias_fc2 = params
    normed_one = low(layer_norm(group_x, gain_one, shift_one))
    combined = matmul(normed_one, w_qkv)
    queries = low(low_back(combined[:, :D] + bias_q))
    key_rows = low(low_back(combined[:, D:2 * D]))
    value_rows = low(low_back(combined[:, 2 * D:] + bias_v))
    attended = low(low_back(attention(queries, key_rows, value_rows, group_ids)))
    branch = low_back(matmul(attended, w_out) + bias_out)
    resid = group_x + branch
    normed_two = low(layer_norm(resid, gain_two, shift_two))
    hidden_pre = low_back(matmul(normed_two, w_fc1) + bias_fc1)
    hidden = low(jax.nn.gelu(hidden_pre, approximate=False))
    return resid + matmul(hidden, w_fc2) + bias_fc2

def forward(params, inputs, image_ids):

    def advance(state, pieces):
        return (state, jax.checkpoint(group_layer)(params, pieces[0], pieces[1]))
    _, outputs = lax.scan(advance, jnp.zeros((), jnp.float32), (inputs.reshape(-1, GROUP, D), image_ids.reshape(-1, GROUP)))
    return outputs.reshape(TOKENS, D)

def reference(inputs, image_ids, ln1_gain, ln1_shift, qkv_weight, query_bias, value_bias, out_weight, out_bias, ln2_gain, ln2_shift, fc1_weight, fc1_bias, fc2_weight, fc2_bias, out_grad):
    params = (ln1_gain, ln1_shift, qkv_weight, query_bias, value_bias, out_weight, out_bias, ln2_gain, ln2_shift, fc1_weight, fc1_bias, fc2_weight, fc2_bias)
    params = tuple((item.astype(jnp.float32) for item in params))

    def whole(prm, values):
        return forward(prm, values, image_ids)
    outputs, pullback = jax.vjp(whole, params, inputs.astype(jnp.float32))
    grads, input_grad = pullback(out_grad.astype(jnp.float32))
    return (outputs.astype(jnp.bfloat16), input_grad.astype(jnp.bfloat16), grads[0], grads[1], grads[2], grads[3], grads[4], grads[5], grads[6], grads[7], grads[8], grads[9], grads[10], grads[11], grads[12])
```

```python
import functools

import jax
import jax.numpy as jnp
from jax import lax
from jax.experimental import pallas as pl
from jax.experimental.pallas import tpu as pltpu
from jax.sharding import Mesh
from jax.sharding import PartitionSpec as P

HEADS = 16
HEAD_DIM = 64
D = 1024
FF = 4096
TOK = 160
GROUP = 2560
HALF = 1280
EPSILON = 1e-06
NEGATIVE = -1e30
TILE = 256
TILES = GROUP // TILE
ALL = ("x", "yl", "yh", "z", "c")
TP = ("z", "c")
XY = ("x", "yl", "yh")
SEQ = ("yh", "z", "c")
BF = jnp.bfloat16
F32 = jnp.float32
VMEM = 48 * 1024 * 1024


def dot(left, right, dims=((1,), (0,))):
    return lax.dot_general(left, right, (dims, ((), ())), preferred_element_type=F32)


def params():
    return pltpu.CompilerParams(vmem_limit_bytes=VMEM)


def along(value, axis, by):
    size = 4 if axis in ("x", "z") else 2
    return lax.ppermute(value, axis, [(i, (i + by) % size) for i in range(size)])


def along_y(value, by):
    pairs = []
    for yl in range(2):
        for yh in range(2):
            to = (yh * 2 + yl + by) % 4
            pairs.append((yl * 2 + yh, (to % 2) * 2 + to // 2))
    return lax.ppermute(value, ("yl", "yh"), pairs)


def ring(value, shift):
    return [value, shift(value, -1), shift(value, 2), shift(value, 1)]


def in_order(blocks, place):
    both = jnp.stack(blocks + blocks)
    return lax.dynamic_slice_in_dim(both, (4 - place) % 4, 4)


def project_kernel(at, xo, xc, w, sv, qb, vb, ids_row, ids_col, n1, q_out, k_out, v_out, att, o_out, lse_out, wh, kt):
    step = pl.program_id(0)
    yh, core, head = at[0], at[2], at[3]

    @pl.when(step == 0)
    def _():
        wh[...] = jnp.where(yh == 0, w[:, 0:192], w[:, 192:384])

    @pl.when(step < 8)
    def _():
        rows = jnp.concatenate([xo[0, 0], xc[0, 0]], 0).astype(F32)
        center = rows - jnp.mean(rows, -1, keepdims=True)
        spread = jnp.mean(center * center, -1, keepdims=True)
        gain = sv[0:1, :].astype(F32)
        shift = sv[1:2, :].astype(F32)
        normed = (center * lax.rsqrt(spread + EPSILON) * gain + shift).astype(BF)
        mixed = dot(normed, wh[...])
        queries = (mixed[:, 0:64] + qb[head]).astype(BF) * jnp.asarray(0.125, BF)
        keys = mixed[:, 64:128].astype(BF)
        values = (mixed[:, 128:192] + vb[head]).astype(BF)
        half = (step // 4 + yh) % 2
        for part in range(2):
            which = core if part == 0 else 1 - core
            here = slice(part * TOK, part * TOK + TOK)
            n1[0, 0, pl.ds(which, 1)] = normed[here][None]
            at_row = pl.multiple_of(half * HALF + (step % 4) * 2 * TOK + which * TOK, TOK)
            q_out[pl.ds(at_row, TOK), :] = queries[here]
            k_out[pl.ds(at_row, TOK), :] = keys[here]
            v_out[pl.ds(at_row, TOK), :] = values[here]

    @pl.when(step == 8)
    def _():
        kt[...] = v_out[...].T

    @pl.when(step >= 8)
    def _():
        tile = step - 8
        queries = q_out[pl.ds(pl.multiple_of(tile * TILE, TILE), TILE), :]
        scores = dot(k_out[...], queries, ((1,), (1,)))
        scores = jnp.where(ids_col[...] == ids_row[...], scores, NEGATIVE)
        top = jnp.max(scores, 0, keepdims=True)
        parts = jnp.exp(scores - top)
        total = jnp.sum(parts, 0, keepdims=True)
        out = dot(kt[...], parts.astype(BF)) / total
        o_out[...] = out
        att[...] = out.T.astype(BF)
        lse_out[0] = top + jnp.log(total)


def project(at, xo, xc, weights, sv, qb, vb, ids):
    late = lambda i: jnp.maximum(i - 8, 0)
    early = lambda i: jnp.minimum(i, 7)
    whole = lambda shape: pl.BlockSpec(shape, lambda i, at: (0,) * len(shape))
    turned = lambda i, at: ((late(i) + (TILES // 2) * at[0]) % TILES, 0)
    x_spec = pl.BlockSpec((1, 1, TOK, D), lambda i, at: (early(i) % 4, early(i) // 4, 0, 0))
    return pl.pallas_call(
        project_kernel,
        out_shape=(
            jax.ShapeDtypeStruct((2, 4, 2, TOK, D), BF),
            jax.ShapeDtypeStruct((GROUP, HEAD_DIM), BF),
            jax.ShapeDtypeStruct((GROUP, HEAD_DIM), BF),
            jax.ShapeDtypeStruct((GROUP, HEAD_DIM), BF),
            jax.ShapeDtypeStruct((GROUP, HEAD_DIM), BF),
            jax.ShapeDtypeStruct((HEAD_DIM, GROUP), F32),
            jax.ShapeDtypeStruct((TILES, 1, TILE), F32),
        ),
        grid_spec=pltpu.PrefetchScalarGridSpec(
            num_scalar_prefetch=1,
            grid=(8 + TILES,),
            in_specs=[
                x_spec,
                x_spec,
                pl.BlockSpec((D, 512), lambda i, at: (0, 0)),
                whole((8, D)),
                whole((HEADS, 1, HEAD_DIM)),
                whole((HEADS, 1, HEAD_DIM)),
                pl.BlockSpec((1, TILE), lambda i, at: (0, late(i))),
                whole((GROUP, 1)),
            ],
            out_specs=[
                pl.BlockSpec((1, 1, 2, TOK, D), lambda i, at: ((early(i) // 4 + at[0]) % 2, early(i) % 4, 0, 0, 0)),
                whole((GROUP, HEAD_DIM)),
                whole((GROUP, HEAD_DIM)),
                whole((GROUP, HEAD_DIM)),
                pl.BlockSpec((TILE, HEAD_DIM), turned),
                pl.BlockSpec((HEAD_DIM, TILE), lambda i, at: (0, late(i))),
                pl.BlockSpec((1, 1, TILE), lambda i, at: (late(i), 0, 0)),
            ],
            scratch_shapes=[pltpu.VMEM((D, 192), BF), pltpu.VMEM((HEAD_DIM, GROUP), BF)],
        ),
        compiler_params=params(),
        name="project_attend",
    )(at, xo, xc, weights, sv, qb, vb, ids[None, :], ids[:, None])


def attend_back_kernel(q, k, v, do, o, lse, ids_row, ids_col, g, kt, dk, dv):
    tile = pl.program_id(0)

    @pl.when(tile == 0)
    def _():
        kt[...] = k[...].T
        dk[...] = jnp.zeros_like(dk)
        dv[...] = jnp.zeros_like(dv)

    rows = pl.ds(pl.multiple_of(tile * TILE, TILE), TILE)
    queries = q[rows, :]
    grads = do[rows, :]
    scores = dot(k[...], queries, ((1,), (1,)))
    probs = jnp.where(ids_col[...] == ids_row[...], jnp.exp(scores - lse[0]), 0.0)
    probs_grad = dot(v[...], grads, ((1,), (1,)))
    delta = jnp.sum(o[...] * grads.astype(F32).T, 0, keepdims=True)
    scores_grad = (probs * (probs_grad - delta)).astype(BF)
    dk[...] += dot(scores_grad, queries)
    dv[...] += dot(probs.astype(BF), grads)
    g[rows, 0:64] = (dot(kt[...], scores_grad).T * 0.125).astype(BF)

    @pl.when(tile == TILES - 1)
    def _():
        g[:, 64:128] = dk[...].astype(BF)
        g[:, 128:192] = dv[...].astype(BF)


def attend_back(q, k, v, do, o, lse, ids):
    whole = lambda shape: pl.BlockSpec(shape, lambda i: (0,) * len(shape))
    heads = whole((GROUP, HEAD_DIM))
    return pl.pallas_call(
        attend_back_kernel,
        out_shape=jax.ShapeDtypeStruct((GROUP, 192), BF),
        grid=(TILES,),
        in_specs=[
            heads,
            heads,
            heads,
            heads,
            pl.BlockSpec((HEAD_DIM, TILE), lambda i: (0, i)),
            pl.BlockSpec((1, 1, TILE), lambda i: (i, 0, 0)),
            pl.BlockSpec((1, TILE), lambda i: (0, i)),
            whole((GROUP, 1)),
        ],
        out_specs=whole((GROUP, 192)),
        scratch_shapes=[
            pltpu.VMEM((HEAD_DIM, GROUP), BF),
            pltpu.VMEM((GROUP, HEAD_DIM), F32),
            pltpu.VMEM((GROUP, HEAD_DIM), F32),
        ],
        compiler_params=params(),
        name="attend_back",
    )(q, k, v, do, o, lse, ids[None, :], ids[:, None])


def feed_kernel(at, ao, ac, xo, xc, w_out, sv, w1, b1, w2, dy, resid_out, n2_out, hid_out, pg_out, dn2_out, b1_out, wide):
    step = pl.program_id(0)
    z, core = at[1], at[2]
    own = step >= 2
    pair = step % 2

    for src, block in ((core, ao), (1 - core, ac)):
        for s in range(4):
            lane = pl.multiple_of(s * 256 + src * 128, 128)
            wide[:, pl.ds(lane, 128)] = block[s, :, 0].reshape(2 * TOK, 128)
    x_rows = jnp.where(own, xo[:, 0], xc[:, 0]).reshape(2 * TOK, D).astype(F32)
    resid = x_rows + dot(wide[...], w_out[...]) + sv[4:5, :].astype(F32)

    @pl.when(jnp.logical_and(own, pair == z // 2))
    def _():
        resid_out[...] = jnp.where(z % 2 == 0, resid[:TOK], resid[TOK:])

    center = resid - jnp.mean(resid, -1, keepdims=True)
    spread = jnp.mean(center * center, -1, keepdims=True)
    normed = (center * lax.rsqrt(spread + EPSILON) * sv[5:6, :].astype(F32) + sv[6:7, :].astype(F32)).astype(BF)
    n2_out[:, 0] = normed.reshape(2, TOK, D)
    pre = dot(normed, w1[...]) + b1[...].astype(F32)
    cdf = 0.5 * (1.0 + lax.erf(pre * (0.5**0.5)))
    hid_out[:, 0] = (pre * cdf).astype(BF).reshape(2, TOK, 512)
    slope = cdf + pre * jnp.exp(-0.5 * pre * pre) * 0.3989422804014327
    hidden_grad = dot(dy[:, 0].reshape(2 * TOK, D), w2[...], ((1,), (1,)))
    pre_grad = (hidden_grad * slope).astype(BF)
    pg_out[:, 0] = pre_grad.reshape(2, TOK, 512)
    dn2_out[0] = dot(pre_grad, w1[...], ((1,), (1,))).astype(BF).reshape(2, TOK, D)

    @pl.when(step == 0)
    def _():
        b1_out[...] = jnp.zeros_like(b1_out)

    b1_out[...] += jnp.sum(pre_grad.astype(F32), 0, keepdims=True)


def feed(at, att_own, att_other, xo, xc, w_out, sv, weights, b1, w2, dy):
    core_of = lambda i, at: jnp.where(i >= 2, at[2], 1 - at[2])
    whole = lambda shape: pl.BlockSpec(shape, lambda i, at: (0,) * len(shape))
    a_spec = pl.BlockSpec((4, 2, 1, TOK, 128), lambda i, at: (0, i % 2, core_of(i, at), 0, 0))
    tok_spec = lambda width: pl.BlockSpec((2, 1, TOK, width), lambda i, at: (i % 2, core_of(i, at), 0, 0))
    return pl.pallas_call(
        feed_kernel,
        out_shape=(
            jax.ShapeDtypeStruct((TOK, D), F32),
            jax.ShapeDtypeStruct((4, 2, TOK, D), BF),
            jax.ShapeDtypeStruct((4, 2, TOK, 512), BF),
            jax.ShapeDtypeStruct((4, 2, TOK, 512), BF),
            jax.ShapeDtypeStruct((2, 4, TOK, D), BF),
            jax.ShapeDtypeStruct((1, 512), F32),
        ),
        grid_spec=pltpu.PrefetchScalarGridSpec(
            num_scalar_prefetch=1,
            grid=(4,),
            in_specs=[
                a_spec,
                a_spec,
                pl.BlockSpec((2, 1, TOK, D), lambda i, at: (jnp.where(i >= 2, i - 2, 0), 0, 0, 0)),
                pl.BlockSpec((2, 1, TOK, D), lambda i, at: (jnp.minimum(i, 1), 0, 0, 0)),
                whole((D, D)),
                whole((8, D)),
                pl.BlockSpec((D, 512), lambda i, at: (0, 1)),
                whole((1, 512)),
                whole((512, D)),
                tok_spec(D),
            ],
            out_specs=[
                whole((TOK, D)),
                tok_spec(D),
                tok_spec(512),
                tok_spec(512),
                pl.BlockSpec((1, 2, TOK, D), lambda i, at: (1 - i // 2, i % 2, 0, 0)),
                whole((1, 512)),
            ],
            scratch_shapes=[pltpu.VMEM((2 * TOK, D), BF)],
        ),
        compiler_params=params(),
        name="out_feed",
    )(at, att_own, att_other, xo, xc, w_out, sv, weights, b1, w2, dy)


def norm_back(values, gain, grad):
    center = values - jnp.mean(values, -1, keepdims=True)
    spread = jnp.mean(center * center, -1, keepdims=True)
    r = lax.rsqrt(spread + EPSILON)
    n = center * r
    e = grad * gain
    inner = r * (e - jnp.mean(e, -1, keepdims=True) - n * jnp.mean(e * n, -1, keepdims=True))
    return inner, jnp.sum(grad * n, 0), jnp.sum(grad, 0)


def body(
    inputs,
    image_ids,
    ln1_gain,
    ln1_shift,
    qkv_weight,
    query_bias,
    value_bias,
    out_weight,
    out_bias,
    ln2_gain,
    ln2_shift,
    fc1_weight,
    fc1_bias,
    fc2_weight,
    fc2_bias,
    out_grad,
):
    xi, yl, yh, zi, ci = (lax.axis_index(name) for name in ALL)
    yi = yh * 2 + yl
    at = jnp.stack([yh, zi, ci, yh * 8 + zi * 2 + ci]).astype(jnp.int32)
    shift_x = lambda v, by: along(v, "x", by)
    shift_z = lambda v, by: along(v, "z", by)

    pair = jnp.stack([inputs, along(inputs, "yh", 1)])
    xo = in_order(ring(pair, shift_z), zi)
    xc = along(xo, "c", 1)
    dy_all = lax.all_gather(out_grad, TP, axis=0, tiled=True).reshape(4, 2, TOK, D)

    qkv = qkv_weight.reshape(8, 3, 2, 8, HEAD_DIM).transpose(3, 0, 2, 1, 4).reshape(8, 8, 384)
    small = jnp.stack(
        [ln1_gain, ln1_shift, query_bias, value_bias, out_bias, ln2_gain, ln2_shift, fc2_bias], 1
    )
    small = jnp.broadcast_to(jnp.pad(small, ((0, 0), (0, 120)))[None], (8, 8, 128))
    fc1 = fc1_weight.reshape(8, 16, 8, 32).transpose(2, 0, 1, 3).reshape(8, 8, 512)
    columns = jnp.concatenate([qkv, small, fc1], 2)
    columns = lax.all_to_all(columns, TP, split_axis=0, concat_axis=0, tiled=True).reshape(64, 1024)
    pairs = [(((j // 8) * 8 + zc) * 8 + j % 8, j * 8 + zc) for j in range(16) for zc in range(8)]
    out_rows = lax.ppermute(out_weight, ALL, pairs)
    rows = jnp.concatenate(
        [fc2_weight, out_rows, jnp.pad(fc1_bias[None], ((0, 7), (0, D - 32)))], 0
    )

    def y_spread(blocks, buffer, index):
        for k, block in enumerate(blocks):
            y = (yi + k) % 4
            buffer = lax.dynamic_update_slice(buffer, block, index(y % 2, y // 2))
        return buffer

    col_x = in_order(ring(columns, shift_x), xi)
    col_blocks = [b.reshape(4, 1, 1, 64, 1024) for b in ring(col_x, along_y)]
    col_all = y_spread(
        col_blocks, jnp.zeros((4, 2, 2, 64, 1024), BF), lambda l, h: (0, l, h, 0, 0)
    ).reshape(1024, 1024)
    row_y = y_spread(
        [b.reshape(1, 1, 48, 1024) for b in ring(rows, along_y)],
        jnp.zeros((2, 2, 48, 1024), BF),
        lambda l, h: (l, h, 0, 0),
    )
    row_all = in_order(ring(row_y, shift_x), xi).reshape(16, 48, 1024)
    w2 = row_all[:, 0:32].reshape(512, 1024)
    w_out_part = row_all[:, 32:40].reshape(128, 1024)
    b1 = row_all[:, 40, 0:32].reshape(1, 512)
    sv = col_all[:, 384:392].T
    w_out = lax.all_gather(w_out_part, TP, axis=0, tiled=True)
    w_qkv = lax.all_gather(col_all[:, 0:384], TP, axis=0, tiled=False)

    n1, q, k, v, att, o, lse = project(
        at, xo, xc, col_all, sv, sv[2].astype(F32).reshape(HEADS, 1, HEAD_DIM), sv[3].astype(F32).reshape(HEADS, 1, HEAD_DIM), image_ids
    )

    theirs = along(att[HALF:], "yh", 1)
    first = jnp.where(yh == 0, att[:HALF], theirs)
    second = jnp.where(yh == 0, theirs, att[:HALF])
    att_two = jnp.concatenate([first, second], 1)
    att_own = in_order(ring(att_two, shift_z), zi)
    att_other = along(att_own, "c", 1)
    split = (4, 4, 2, TOK, 128)
    resid, n2, hidden, pre_grad, dn2, b1_grad = feed(
        at, att_own.reshape(split), att_other.reshape(split), xo, xc, w_out, sv, col_all, b1, w2, dy_all
    )

    def sum_tp(part_own, part_other):
        mixed = (part_own.astype(F32) + along(part_other, "c", 1).astype(F32)).astype(BF)
        pick = lambda by: lax.dynamic_index_in_dim(mixed, (zi + by) % 4, 0, keepdims=False)
        total = pick(0).astype(F32)
        for by in (1, 2, 3):
            total = total + shift_z(pick(by), by).astype(F32)
        return total

    dn2_own = sum_tp(dn2[0], dn2[1])
    out_grad_f = out_grad.astype(F32)
    gain_two = sv[5].astype(F32)
    resid_part, gain_two_grad, shift_two_grad = norm_back(resid, gain_two, dn2_own)
    resid_grad = out_grad_f + resid_part
    branch_grad = resid_grad.astype(BF)
    out_bias_grad = jnp.sum(branch_grad.astype(F32), 0)
    att_grad = dot(branch_grad, w_out, ((1,), (1,))).astype(BF)
    att_grad = att_grad.reshape(TOK, 8, 2, HEAD_DIM).transpose(2, 1, 0, 3).reshape(16, TOK, HEAD_DIM)
    do = lax.all_to_all(att_grad, SEQ, split_axis=0, concat_axis=0, tiled=True).reshape(GROUP, HEAD_DIM)
    g = attend_back(q, k, v, do, o, lse, image_ids)
    g_tok = lax.all_to_all(g.reshape(16, TOK, 192), SEQ, split_axis=0, concat_axis=0, tiled=True)

    hidden = hidden.reshape(HALF, 512)
    part = dot(hidden, w2).astype(BF)
    summed = lax.psum_scatter(part, TP, scatter_dimension=0, tiled=True)
    outputs = resid + summed.astype(F32) + sv[7].astype(F32)
    dy_rows = dy_all.reshape(HALF, D)
    fc2_grad = dot(hidden, dy_rows, ((0,), (0,))).astype(BF)
    fc1_grad = dot(n2.reshape(HALF, D), pre_grad.reshape(HALF, 512), ((0,), (0,))).astype(BF)
    fc2_grad = lax.psum_scatter(fc2_grad, XY, scatter_dimension=0, tiled=True).astype(F32)
    fc1_grad = lax.psum_scatter(fc1_grad, XY, scatter_dimension=0, tiled=True)
    fc1_grad = lax.all_to_all(fc1_grad.reshape(8, 8, 512), TP, split_axis=0, concat_axis=0, tiled=True)
    fc1_grad = fc1_grad.reshape(8, 8, 16, 32).transpose(1, 2, 0, 3).reshape(8, FF).astype(F32)
    fc1_bias_grad = lax.psum_scatter(b1_grad[0], XY, scatter_dimension=0, tiled=True)

    branch_all = lax.all_gather(branch_grad, TP, axis=0, tiled=True)
    out_w = dot(att_two, branch_all, ((0,), (0,))).astype(BF)
    out_w = lax.psum_scatter(out_w, XY, scatter_dimension=0, tiled=True)
    out_w = lax.ppermute(out_w, ALL, [(b, a) for a, b in pairs]).astype(F32)

    qkv_grad = dot(n1.reshape(GROUP, D), g, ((0,), (0,))).astype(BF)
    qkv_grad = lax.psum_scatter(qkv_grad, ("x", "yl"), scatter_dimension=0, tiled=True)
    qkv_grad = lax.all_to_all(qkv_grad.reshape(16, 8, 192), SEQ, split_axis=0, concat_axis=0, tiled=True)
    qkv_grad = qkv_grad.reshape(16, 8, 3, HEAD_DIM).transpose(1, 2, 0, 3).reshape(8, 3 * D).astype(F32)

    g_heads = g_tok.reshape(2, 8, TOK, 192).transpose(2, 1, 0, 3).reshape(TOK, 8, 384)
    normed_grad = jnp.einsum("tzn,zmn->tm", g_heads, w_qkv, preferred_element_type=F32)
    first_x = inputs.astype(F32)
    first_part, gain_one_grad, shift_one_grad = norm_back(first_x, sv[0].astype(F32), normed_grad)
    input_grad = resid_grad + first_part
    sums = jnp.sum(g_tok.astype(F32), 1)

    vectors = jnp.stack(
        [
            gain_one_grad,
            shift_one_grad,
            sums[:, 0:64].reshape(D),
            sums[:, 128:192].reshape(D),
            out_bias_grad,
            gain_two_grad,
            shift_two_grad,
            jnp.sum(out_grad_f, 0),
        ]
    )
    vectors = vectors.reshape(8, 16, 8, 8).transpose(2, 1, 0, 3).reshape(8, 16, 64)
    vectors = lax.all_to_all(vectors, TP, split_axis=0, concat_axis=0, tiled=True).sum(0)
    vectors = lax.all_to_all(vectors, XY, split_axis=0, concat_axis=0, tiled=True).sum(0).reshape(8, 8)
    return (
        outputs.astype(BF),
        input_grad.astype(BF),
        vectors[0],
        vectors[1],
        qkv_grad,
        vectors[2],
        vectors[3],
        out_w,
        vectors[4],
        vectors[5],
        vectors[6],
        fc1_grad,
        fc1_bias_grad,
        fc2_grad,
        vectors[7],
    )


def solution(mesh):
    fine = Mesh(mesh.devices.reshape(4, 2, 2, 4, 2), ALL)
    rows = P(ALL, None)
    vec = P(ALL)
    return jax.shard_map(
        body,
        mesh=fine,
        in_specs=(rows, P(("x", "yl")), vec, vec, rows, vec, vec, rows, vec, vec, vec, rows, vec, rows, vec, rows),
        out_specs=(rows, rows, vec, vec, rows, vec, vec, rows, vec, vec, vec, rows, vec, rows, vec),
        check_vma=False,
    )
```

```python
import functools

import jax
import jax.numpy as jnp
from jax import lax
from jax.experimental import pallas as pl
from jax.experimental.pallas import tpu as pltpu
from jax.sharding import Mesh
from jax.sharding import PartitionSpec as P

HEADS = 16
HEAD_DIM = 64
D = 1024
FF = 4096
TOK = 160
GROUP = 2560
HALF = 1280
EPSILON = 1e-06
NEGATIVE = -1e30
TILE = 256
TILES = GROUP // TILE
ALL = ("x", "yl", "yh", "z", "c")
TP = ("z", "c")
XY = ("x", "yl", "yh")
SEQ = ("yh", "z", "c")
BF = jnp.bfloat16
F32 = jnp.float32


def dot(left, right, dims=((1,), (0,))):
    return lax.dot_general(left, right, (dims, ((), ())), preferred_element_type=F32)


def params(mebibytes):
    return pltpu.CompilerParams(vmem_limit_bytes=mebibytes * 1024 * 1024)


def cost(micros):
    return pl.CostEstimate(flops=int(micros * 1e9), bytes_accessed=1 << 20, transcendentals=0)


def whole(*shape):
    return pl.BlockSpec(shape, lambda *_: (0,) * len(shape))


def along(value, axis, by):
    size = 4 if axis in ("x", "z") else 2
    return lax.ppermute(value, axis, [(i, (i + by) % size) for i in range(size)])


def along_y(value, by):
    pairs = []
    for yl in range(2):
        for yh in range(2):
            to = (yh * 2 + yl + by) % 4
            pairs.append((yl * 2 + yh, (to % 2) * 2 + to // 2))
    return lax.ppermute(value, ("yl", "yh"), pairs)


def from_up(value, k):
    return along(value, "z", 4 - k)


def after(value, *done):
    return lax.optimization_barrier((value, *done))[0]


def exchange(value, axes):
    return lax.all_to_all(value, axes, split_axis=0, concat_axis=0, tiled=True)


def project_rows(at, raw, sv, wh, qb, vb):
    rows = raw.astype(F32)
    center = rows - jnp.mean(rows, -1, keepdims=True)
    spread = jnp.mean(center * center, -1, keepdims=True)
    gain = sv[0:1, :].astype(F32)
    shift = sv[1:2, :].astype(F32)
    normed = (center * lax.rsqrt(spread + EPSILON) * gain + shift).astype(BF)
    mixed = dot(normed, wh[...])
    head = at[3]
    queries = (mixed[:, 0:64] + qb[head]).astype(BF) * jnp.asarray(0.125, BF)
    keys = mixed[:, 64:128].astype(BF)
    values = (mixed[:, 128:192] + vb[head]).astype(BF)
    return normed, jnp.concatenate([queries, jnp.zeros_like(queries)], 1), jnp.concatenate([keys, values], 1)


def choose_head(at, w, wh):
    @pl.when(pl.program_id(0) == 0)
    def _():
        wh[...] = jnp.where(at[0] == 0, w[:, 0:192], w[:, 192:384])


def project_near_kernel(at, *refs):
    blocks, (w, sv, qb, vb, x_out, n1, q_out, kv_out, wh) = refs[:8], refs[8:]
    core = at[2]
    choose_head(at, w, wh)

    def one(own, other):
        raw = jnp.concatenate([own[...], other[...]], 0)
        normed, queries, pairs = project_rows(at, raw, sv, wh, qb, vb)
        for part in range(2):
            which = core if part == 0 else 1 - core
            here = slice(part * TOK, part * TOK + TOK)
            for ref, value in ((x_out, raw), (n1, normed), (q_out, queries), (kv_out, pairs)):
                ref[0, pl.ds(which, 1)] = value[here][None]

    for k in range(4):
        pl.when(pl.program_id(0) == k)(functools.partial(one, blocks[k], blocks[4 + k]))


def project_far_kernel(at, x, w, sv, qb, vb, n1, q_out, kv_out, wh):
    choose_head(at, w, wh)
    raw = x[0].reshape(2 * TOK, D)
    for ref, value in zip((n1, q_out, kv_out), project_rows(at, raw, sv, wh, qb, vb), strict=True):
        ref[0] = value.reshape(2, TOK, value.shape[1])


def project(at, x, weights, sv, qb, vb):
    near = isinstance(x, list)
    placed = lambda width: pl.BlockSpec(
        (1, 2, TOK, width), lambda i, at: ((i + at[1]) % 4 if near else i, 0, 0, 0)
    )
    shape = lambda width: jax.ShapeDtypeStruct((4, 2, TOK, width), BF)
    widths = (D, D, 128, 128) if near else (D, 128, 128)
    return pl.pallas_call(
        project_near_kernel if near else project_far_kernel,
        out_shape=[shape(w) for w in widths],
        grid_spec=pltpu.PrefetchScalarGridSpec(
            num_scalar_prefetch=1,
            grid=(4,),
            in_specs=([whole(TOK, D)] * 8 if near else [placed(D)])
            + [whole(D, 512), whole(8, D), whole(HEADS, 1, HEAD_DIM), whole(HEADS, 1, HEAD_DIM)],
            out_specs=[placed(w) for w in widths],
            scratch_shapes=[pltpu.VMEM((D, 192), BF)],
        ),
        compiler_params=params(24),
        cost_estimate=cost(2),
        name="project_near" if near else "project_far",
    )(at, *(x if near else [x]), weights, sv, qb, vb)


def image_range(at, ids):
    first = jnp.zeros_like(ids)
    length = jnp.zeros_like(ids)
    for m in range(4):
        first = jnp.where(ids == m, at[4 + m], first)
        length = jnp.where(ids == m, at[5 + m] - at[4 + m], length)
    return first, length


def allowed(base, first, length, rows):
    place = lax.broadcasted_iota(jnp.int32, (rows, length.shape[1]), 0) - (first - base)
    return jnp.logical_and(place >= 0, place < length)


def attend_kernel(at, q, kv_a, kv_b, ids, att, o_out, lse_out, vt_a, vt_b):
    @pl.when(pl.program_id(0) == 0)
    def _():
        vt_a[...] = kv_a[...].T
        vt_b[...] = kv_b[...].T

    first, length = image_range(at, ids[...])
    queries = q[...]
    scores = []
    for half, keys in enumerate((kv_a, kv_b)):
        raw = dot(keys[...], queries, ((1,), (1,)))
        keep = allowed(((half + at[0]) % 2) * HALF, first, length, HALF)
        scores.append(jnp.where(keep, raw, NEGATIVE))
    top = jnp.maximum(jnp.max(scores[0], 0, keepdims=True), jnp.max(scores[1], 0, keepdims=True))
    total = 0.0
    out = 0.0
    for part, values in zip(scores, (vt_a, vt_b), strict=True):
        part = jnp.exp(part - top)
        total = total + jnp.sum(part, 0, keepdims=True)
        out = out + dot(values[64:128, :], part.astype(BF))
    out = out / total
    o_out[...] = out
    att[...] = out.T.astype(BF)
    lse_out[0] = top + jnp.log(total)


def attend(at, q, kv, ids):
    tiles = HALF // TILE
    pairs = whole(HALF, 128)
    return pl.pallas_call(
        attend_kernel,
        out_shape=(
            jax.ShapeDtypeStruct((HALF, HEAD_DIM), BF),
            jax.ShapeDtypeStruct((HEAD_DIM, HALF), F32),
            jax.ShapeDtypeStruct((tiles, 1, TILE), F32),
        ),
        grid_spec=pltpu.PrefetchScalarGridSpec(
            num_scalar_prefetch=1,
            grid=(tiles,),
            in_specs=[
                pl.BlockSpec((TILE, 128), lambda i, at: (i, 0)),
                pairs,
                pairs,
                pl.BlockSpec((1, TILE), lambda i, at: (0, i)),
            ],
            out_specs=[
                pl.BlockSpec((TILE, HEAD_DIM), lambda i, at: (i, 0)),
                pl.BlockSpec((HEAD_DIM, TILE), lambda i, at: (0, i)),
                pl.BlockSpec((1, 1, TILE), lambda i, at: (i, 0, 0)),
            ],
            scratch_shapes=[pltpu.VMEM((128, HALF), BF)] * 2,
        ),
        compiler_params=params(24),
        cost_estimate=cost(3),
        name="attend",
    )(at, q, *kv, ids)


def attend_back_kernel(at, q_a, q_b, kv_a, kv_b, do_in, o_a, o_b, lse_a, lse_b, ids_a, ids_b, g_abs, g_a, g_b, q, kv, do, kt, dq, dkv):
    tile = pl.program_id(0)
    yh = at[0]

    @pl.when(tile == 0)
    def _():
        for ref, one, two in ((q, q_a, q_b), (kv, kv_a, kv_b)):
            ref[0:HALF, :] = one[...]
            ref[HALF:GROUP, :] = two[...]
        kt[...] = kv[...].T
        for half in range(2):
            start = ((half + yh) % 2) * HALF
            for s in range(8):
                packed = do_in[half * 8 + s]
                block = jnp.concatenate([packed[:, 0:64], packed[:, 64:128]], 0)
                block = jnp.concatenate([jnp.zeros_like(block), block], 1)
                do[pl.ds(pl.multiple_of(start + s * TOK, TOK), TOK), :] = block
        dkv[...] = jnp.zeros_like(dkv)

    near = tile < TILES // 2
    first, length = image_range(at, jnp.where(near, ids_a[...], ids_b[...]))
    o_tile = jnp.where(near, o_a[...], o_b[...])
    lse = jnp.where(near, lse_a[0], lse_b[0])
    rows = pl.ds(pl.multiple_of(tile * TILE, TILE), TILE)
    queries = q[rows, :]
    grads = do[rows, :]
    delta = jnp.sum(o_tile * grads[:, 64:128].astype(F32).T, 0, keepdims=True)
    dq_tile = 0.0
    for half in range(2):
        here = slice(half * HALF, half * HALF + HALF)
        scores = dot(kv[here, :], queries, ((1,), (1,)))
        keep = allowed(((half + yh) % 2) * HALF, first, length, HALF)
        probs = jnp.where(keep, jnp.exp(scores - lse), 0.0)
        probs_grad = dot(kv[here, :], grads, ((1,), (1,)))
        scores_grad = (probs * (probs_grad - delta)).astype(BF)
        dkv[here, :] += dot(scores_grad, queries) + dot(probs.astype(BF), grads)
        dq_tile = dq_tile + dot(kt[0:64, here], scores_grad)
    dq[rows, :] = (dq_tile.T * 0.125).astype(BF)

    @pl.when(tile == TILES - 1)
    def _():
        for ref, half in ((g_a, 0), (g_b, 1)):
            here = slice(half * HALF, half * HALF + HALF)
            ref[:, 0:64] = dq[here, :]
            ref[:, 64:192] = dkv[here, :].astype(BF)
            for s in range(8):
                block = ref[s * TOK : s * TOK + TOK, :]
                to = ((half + yh) % 2) * 8 + s
                g_abs[to, 0:TOK, :] = block[:, 0:128]
                g_abs[to, TOK : TOK + 80, :] = jnp.concatenate([block[0:80, 128:192], block[80:TOK, 128:192]], 1)


def attend_back(at, q, kv, do, o, lse, ids):
    pairs = whole(HALF, 128)
    last = TILES // 2 - 1
    one = lambda i: jnp.minimum(i, last)
    two = lambda i: jnp.maximum(i - last - 1, 0)
    wide = pltpu.VMEM((GROUP, 128), BF)
    return pl.pallas_call(
        attend_back_kernel,
        out_shape=(
            jax.ShapeDtypeStruct((HEADS, 240, 128), BF),
            jax.ShapeDtypeStruct((HALF, 192), BF),
            jax.ShapeDtypeStruct((HALF, 192), BF),
        ),
        grid_spec=pltpu.PrefetchScalarGridSpec(
            num_scalar_prefetch=1,
            grid=(TILES,),
            in_specs=[pairs] * 4
            + [whole(HEADS, TOK // 2, 128)]
            + [pl.BlockSpec((HEAD_DIM, TILE), lambda i, at, f=f: (0, f(i))) for f in (one, two)]
            + [pl.BlockSpec((1, 1, TILE), lambda i, at, f=f: (f(i), 0, 0)) for f in (one, two)]
            + [pl.BlockSpec((1, TILE), lambda i, at, f=f: (0, f(i))) for f in (one, two)],
            out_specs=[whole(HEADS, 240, 128), whole(HALF, 192), whole(HALF, 192)],
            scratch_shapes=[
                wide,
                wide,
                wide,
                pltpu.VMEM((128, GROUP), BF),
                pltpu.VMEM((GROUP, HEAD_DIM), BF),
                pltpu.VMEM((GROUP, 128), F32),
            ],
        ),
        compiler_params=params(40),
        cost_estimate=cost(20),
        name="attend_back",
    )(at, *q, *kv, do, *o, *lse, *ids)


def feed_kernel(at, *refs):
    blocks, refs = refs[:8], refs[8:]
    x, w_out, sv, rows, b1, dy, resid_out, att_out, y_out, dn2_other, dn2_own, w1_out, w2_out, b1_out = refs[:14]
    wide, w1, w2, w1_grad, w2_grad = refs[14:]
    step = pl.program_id(0)
    z, core = at[1], at[2]
    own = step >= 2
    pair = step % 2

    @pl.when(step == 0)
    def _():
        for j in range(16):
            w1[j * 64 : j * 64 + 32, :] = rows[j, 0:32, 0:512]
            w1[j * 64 + 32 : j * 64 + 64, :] = rows[j, 0:32, 512:1024]
            w2[j * 32 : j * 32 + 32, :] = rows[j, 32:64, :]
        b1_out[...] = jnp.zeros_like(b1_out)
        w1_grad[...] = jnp.zeros_like(w1_grad)
        w2_grad[...] = jnp.zeros_like(w2_grad)

    for k in range(4):
        for src, block in ((core, blocks[k]), (1 - core, blocks[4 + k])):
            lane = pl.multiple_of(((z + k) % 4) * 256 + src * 128, 128)
            wide[:, pl.ds(lane, 128)] = block[:, 0].reshape(2 * TOK, 128)
    resid = x[:, 0].reshape(2 * TOK, D).astype(F32) + dot(wide[...], w_out[...]) + sv[4:5, :].astype(F32)

    @pl.when(jnp.logical_and(own, pair == z // 2))
    def _():
        resid_out[...] = jnp.where(z % 2 == 0, resid[:TOK], resid[TOK:])
        att = jnp.where(z % 2 == 0, wide[:TOK, :], wide[TOK:, :])
        for h in range(HEADS):
            lane = (h % 8) * 128 + (h // 8) * 64
            att_out[:, h * 64 : h * 64 + 64] = att[:, lane : lane + 64]

    center = resid - jnp.mean(resid, -1, keepdims=True)
    spread = jnp.mean(center * center, -1, keepdims=True)
    normed = (center * lax.rsqrt(spread + EPSILON) * sv[5:6, :].astype(F32) + sv[6:7, :].astype(F32)).astype(BF)
    pre = dot(normed, w1[...]) + b1[...].astype(F32)
    cdf = 0.5 * (1.0 + lax.erf(pre * (0.5**0.5)))
    hidden = (pre * cdf).astype(BF)
    slope = cdf + pre * jnp.exp(-0.5 * pre * pre) * 0.3989422804014327
    dy_rows = dy[:, 0].reshape(2 * TOK, D)
    hidden_grad = dot(dy_rows, w2[...], ((1,), (1,)))
    pre_grad = (hidden_grad * slope).astype(BF)
    normed_grad = dot(pre_grad, w1[...], ((1,), (1,))).astype(BF).reshape(2, TOK, D)
    y_out[:, 0] = dot(hidden, w2[...]).astype(BF).reshape(2, TOK, D)
    w2_grad[...] += dot(hidden, dy_rows, ((0,), (0,)))
    w1_grad[...] += dot(normed, pre_grad, ((0,), (0,)))
    b1_out[...] += jnp.sum(pre_grad.astype(F32), 0, keepdims=True)

    @pl.when(own)
    def _():
        dn2_own[...] = normed_grad

    @pl.when(jnp.logical_not(own))
    def _():
        dn2_other[...] = normed_grad

    @pl.when(step == 3)
    def _():
        w1_out[...] = w1_grad[...].astype(BF).reshape(128, 8, 512)
        w2_out[...] = w2_grad[...].astype(BF).reshape(16, 32, D)


def feed(at, att_own, att_other, x, w_out, sv, rows, b1, dy):
    core_of = lambda i, at: jnp.where(i >= 2, at[2], 1 - at[2])
    tok_spec = lambda width: pl.BlockSpec((2, 1, TOK, width), lambda i, at: (i % 2, core_of(i, at), 0, 0))
    return pl.pallas_call(
        feed_kernel,
        out_shape=(
            jax.ShapeDtypeStruct((TOK, D), F32),
            jax.ShapeDtypeStruct((TOK, D), BF),
            jax.ShapeDtypeStruct((4, 2, TOK, D), BF),
            jax.ShapeDtypeStruct((4, TOK, D), BF),
            jax.ShapeDtypeStruct((4, TOK, D), BF),
            jax.ShapeDtypeStruct((128, 8, 512), BF),
            jax.ShapeDtypeStruct((16, 32, D), BF),
            jax.ShapeDtypeStruct((1, 512), F32),
        ),
        grid_spec=pltpu.PrefetchScalarGridSpec(
            num_scalar_prefetch=1,
            grid=(4,),
            in_specs=[tok_spec(128)] * 8
            + [
                tok_spec(D),
                whole(D, D),
                whole(8, D),
                whole(16, 112, D),
                whole(1, 512),
                tok_spec(D),
            ],
            out_specs=[
                whole(TOK, D),
                whole(TOK, D),
                tok_spec(D),
                pl.BlockSpec((2, TOK, D), lambda i, at: (jnp.minimum(i, 1), 0, 0)),
                pl.BlockSpec((2, TOK, D), lambda i, at: (jnp.maximum(i - 2, 0), 0, 0)),
                whole(128, 8, 512),
                whole(16, 32, D),
                whole(1, 512),
            ],
            scratch_shapes=[
                pltpu.VMEM((2 * TOK, D), BF),
                pltpu.VMEM((D, 512), BF),
                pltpu.VMEM((512, D), BF),
                pltpu.VMEM((D, 512), F32),
                pltpu.VMEM((512, D), F32),
            ],
        ),
        compiler_params=params(56),
        cost_estimate=cost(20),
        name="out_feed",
    )(at, *att_own, *att_other, x, w_out, sv, rows, b1, dy)


def mix_kernel(at, own, came, *outs):
    for k in range(4):
        here = pl.ds((at[1] + k) % 4, 1)
        outs[k][...] = (own[here][0].astype(F32) + came[here][0].astype(F32)).astype(BF)


def mix(at, own, came):
    return pl.pallas_call(
        mix_kernel,
        out_shape=[jax.ShapeDtypeStruct((TOK, D), BF)] * 4,
        grid_spec=pltpu.PrefetchScalarGridSpec(
            num_scalar_prefetch=1,
            grid=(1,),
            in_specs=[whole(4, TOK, D)] * 2,
            out_specs=[whole(TOK, D)] * 4,
        ),
        compiler_params=params(12),
        cost_estimate=cost(2),
        name="mix",
    )(at, own, came)


def norm_back(values, gain, grad):
    center = values - jnp.mean(values, -1, keepdims=True)
    spread = jnp.mean(center * center, -1, keepdims=True)
    r = lax.rsqrt(spread + EPSILON)
    n = center * r
    e = grad * gain
    inner = r * (e - jnp.mean(e, -1, keepdims=True) - n * jnp.mean(e * n, -1, keepdims=True))
    return inner, jnp.sum(grad * n, 0, keepdims=True), jnp.sum(grad, 0, keepdims=True)


def middle_kernel(m0, m1, m2, m3, resid, dy, sv, w_out, resid_grad_out, branch_out, att_grad_out, sums):
    grad = m0[...].astype(F32) + m1[...].astype(F32) + m2[...].astype(F32) + m3[...].astype(F32)
    dy_f = dy[...].astype(F32)
    part, gain_grad, shift_grad = norm_back(resid[...], sv[5:6, :].astype(F32), grad)
    resid_grad = dy_f + part
    resid_grad_out[...] = resid_grad
    branch = resid_grad.astype(BF)
    branch_out[...] = branch
    sums[0:1, :] = jnp.sum(branch.astype(F32), 0, keepdims=True)
    sums[1:2, :] = gain_grad
    sums[2:3, :] = shift_grad
    sums[3:4, :] = jnp.sum(dy_f, 0, keepdims=True)
    att_grad = dot(branch, w_out[...], ((1,), (1,))).astype(BF)
    for h in range(HEADS):
        lane = (h % 8) * 128 + (h // 8) * 64
        att_grad_out[h] = jnp.concatenate(
            [att_grad[0:80, lane : lane + 64], att_grad[80:160, lane : lane + 64]], 1
        )


def middle(parts, resid, dy, sv, w_out):
    return pl.pallas_call(
        middle_kernel,
        out_shape=(
            jax.ShapeDtypeStruct((TOK, D), F32),
            jax.ShapeDtypeStruct((TOK, D), BF),
            jax.ShapeDtypeStruct((HEADS, TOK // 2, 128), BF),
            jax.ShapeDtypeStruct((4, D), F32),
        ),
        grid=(1,),
        in_specs=[whole(TOK, D)] * 6 + [whole(8, D), whole(D, D)],
        out_specs=[whole(TOK, D), whole(TOK, D), whole(HEADS, TOK // 2, 128), whole(4, D)],
        compiler_params=params(16),
        cost_estimate=cost(5),
        name="middle",
    )(*parts, resid, dy, sv, w_out)


def last_kernel(g_a, g_b, w, x, resid_grad, sv, out, sums, biases, total):
    step = pl.program_id(0)

    @pl.when(step == 0)
    def _():
        total[...] = jnp.zeros_like(total)

    pair = []
    for packed in (g_a[0], g_b[0]):
        values = jnp.concatenate([packed[160:240, 0:64], packed[160:240, 64:128]], 0)
        pair += [packed[0:160, :], values]
    pair = jnp.concatenate(pair, 1)
    total[...] += dot(pair, w[0], ((1,), (1,)))
    biases[0] = jnp.sum(pair.astype(F32), 0, keepdims=True)

    @pl.when(step == 7)
    def _():
        part, gain_grad, shift_grad = norm_back(x[...].astype(F32), sv[0:1, :].astype(F32), total[...])
        out[...] = (resid_grad[...] + part).astype(BF)
        sums[0:1, :] = gain_grad
        sums[1:2, :] = shift_grad


def last(g, w, x, resid_grad, sv):
    return pl.pallas_call(
        last_kernel,
        out_shape=(
            jax.ShapeDtypeStruct((TOK, D), BF),
            jax.ShapeDtypeStruct((2, D), F32),
            jax.ShapeDtypeStruct((8, 1, 384), F32),
        ),
        grid=(8,),
        in_specs=[
            pl.BlockSpec((1, 240, 128), lambda i: (i, 0, 0)),
            pl.BlockSpec((1, 240, 128), lambda i: (i + 8, 0, 0)),
            pl.BlockSpec((1, D, 384), lambda i: (i, 0, 0)),
            whole(TOK, D),
            whole(TOK, D),
            whole(8, D),
        ],
        out_specs=[whole(TOK, D), whole(2, D), pl.BlockSpec((1, 1, 384), lambda i: (i, 0, 0))],
        scratch_shapes=[pltpu.VMEM((TOK, D), F32)],
        compiler_params=params(48),
        cost_estimate=cost(5),
        name="last",
    )(g, g, w, x, resid_grad, sv)


def body(
    inputs,
    image_ids,
    ln1_gain,
    ln1_shift,
    qkv_weight,
    query_bias,
    value_bias,
    out_weight,
    out_bias,
    ln2_gain,
    ln2_shift,
    fc1_weight,
    fc1_bias,
    fc2_weight,
    fc2_bias,
    out_grad,
):
    xi, yl, yh, zi, ci = (lax.axis_index(name) for name in ALL)
    zc = zi * 2 + ci
    where_at = jnp.arange(16)
    starts = jnp.sum((image_ids[:, None] < where_at[None, :] - 4).astype(jnp.int32), 0)
    at = jnp.where(where_at == 0, yh, jnp.where(where_at == 1, zi, jnp.where(where_at == 2, ci, yh * 8 + zc)))
    at = jnp.where(where_at < 4, at, starts).astype(jnp.int32)

    crossed = along(inputs, "yh", 1)
    near = [inputs] + [from_up(inputs, k) for k in (1, 2, 3)]

    qkv = qkv_weight.reshape(8, 3, 2, 8, HEAD_DIM).transpose(3, 0, 2, 1, 4).reshape(8, 8, 384)
    small = jnp.stack(
        [ln1_gain, ln1_shift, query_bias, value_bias, out_bias, ln2_gain, ln2_shift, fc2_bias], 1
    )
    small = jnp.broadcast_to(jnp.pad(small, ((0, 0), (0, 120)))[None], (8, 8, 128))
    fc1 = fc1_weight.reshape(8, 16, 8, 32).transpose(2, 0, 1, 3).reshape(8, 8, 512)
    columns = exchange(jnp.concatenate([qkv, small, fc1], 2), TP)
    columns = columns.reshape(64, D)
    far = lax.all_gather(after(crossed, *near), TP, axis=0, tiled=True).reshape(4, 2, TOK, D)
    near = near + [along(v, "c", 1) for v in near]

    pairs = [(((j // 8) * 8 + s) * 8 + j % 8, j * 8 + s) for j in range(16) for s in range(8)]
    out_rows = lax.ppermute(out_weight, ALL, pairs)
    fc1 = jnp.concatenate([columns[0:32, 512:], columns[32:64, 512:]], 1)
    columns = jnp.concatenate([columns[0:32, 0:512], columns[32:64, 0:512]], 1)
    rows = [fc1, fc2_weight, jnp.pad(fc1_bias[None], ((0, 7), (0, D - 32))), out_rows, columns]
    rows = exchange(jnp.broadcast_to(jnp.concatenate(rows, 0)[None], (16, 112, D)), XY)
    b1 = rows[:, 64, 0:32].reshape(1, 512)
    w_out = lax.all_gather(rows[:, 72:80].reshape(128, D), TP, axis=0, tiled=True)
    columns = jnp.concatenate([rows[:, 80:112, 0:512], rows[:, 80:112, 512:]], 1).reshape(D, 512)
    sv = columns[:, 384:392].T
    qb = sv[2].astype(F32).reshape(HEADS, 1, HEAD_DIM)
    vb = sv[3].astype(F32).reshape(HEADS, 1, HEAD_DIM)

    x_near, n1_near, q_near, kv_near = project(at, near, after(columns, far), sv, qb, vb)
    n1_far, q_far, kv_far = project(at, far, columns, sv, qb, vb)
    flat = lambda v: v.reshape(HALF, 128)
    q, kv = ((flat(one), flat(two)) for one, two in ((q_near, q_far), (kv_near, kv_far)))
    ids = image_ids.reshape(2, 1, HALF)
    ids = jnp.where(yh == 0, ids[0], ids[1]), jnp.where(yh == 0, ids[1], ids[0])
    att_far, o_far, lse_far = attend(at, q[1], kv, ids[1])
    dy_all = lax.all_gather(after(out_grad, att_far), TP, axis=0, tiled=True).reshape(4, 2, TOK, D)
    theirs = along(att_far, "yh", 1)
    att_near, o_near, lse_near = attend(at, q[0], kv, ids[0])

    first = jnp.where(yh == 0, att_near, theirs)
    second = jnp.where(yh == 0, theirs, att_near)
    att_two = jnp.concatenate([first, second], 1)
    att_own = [att_two] + [from_up(att_two, k) for k in (1, 2, 3)]
    att_other = [along(block, "c", 1) for block in att_own]
    w_qkv = lax.all_gather(after(columns[:, 0:384], *att_other), TP, axis=0, tiled=False)
    split = lambda blocks: [block.reshape(4, 2, TOK, 128) for block in blocks]
    resid, att_tok, y_part, dn2_other, dn2_own, fc1_grad, fc2_grad, b1_grad = feed(
        at, split(att_own), split(att_other), x_near, w_out, sv, rows, b1, dy_all
    )

    mixed = mix(at, dn2_own, along(dn2_other, "c", 1))
    parts = [mixed[0]] + [along(mixed[k], "z", k) for k in (1, 2, 3)]
    fc2_grad = exchange(fc2_grad, XY)
    parts = [after(parts[0], fc2_grad)] + parts[1:]
    resid_grad, branch_grad, att_grad, mid_sums = middle(parts, resid, out_grad, sv, w_out)
    do = exchange(after(att_grad, w_qkv), SEQ)
    turn = ((0,), (0,))

    g, g_near, g_far = attend_back(
        at, q, kv, do, (o_near, o_far), (lse_near, lse_far), ids
    )

    out_w = dot(att_tok, branch_grad, turn).astype(BF)
    out_w = lax.psum_scatter(out_w, TP, scatter_dimension=0, tiled=True)

    fc1_grad = exchange(after(fc1_grad, do), ALL)
    g_tok = exchange(after(g, fc1_grad), SEQ)
    fc2_grad = jnp.sum(fc2_grad.astype(F32), 0)
    fc1_grad = jnp.sum(fc1_grad.reshape(16, 8, 8, 512).astype(F32), 0)
    fc1_grad = fc1_grad.reshape(8, 8, 16, 32).transpose(1, 2, 0, 3).reshape(8, FF)

    summed = lax.psum_scatter(after(y_part, *parts).reshape(HALF, D), TP, scatter_dimension=0, tiled=True)
    outputs = resid + summed.astype(F32) + sv[7].astype(F32)

    qkv_grad = dot(n1_near.reshape(HALF, D), g_near, turn) + dot(n1_far.reshape(HALF, D), g_far, turn)
    qkv_grad = qkv_grad.astype(BF)
    g_tok = after(g_tok, qkv_grad)
    input_grad, norm_sums, biases = last(g_tok, w_qkv, inputs, resid_grad, sv)
    biases = biases.reshape(8, 2, 3, HEAD_DIM).transpose(2, 1, 0, 3).reshape(3, D)
    vectors = jnp.concatenate([norm_sums, biases[0:1], biases[2:3], mid_sums])
    vectors = vectors.reshape(8, 128, 8).transpose(1, 0, 2)
    mine = jnp.arange(8)[None, :, None] == zc
    b1_part = jnp.where(mine, b1_grad.reshape(16, 1, 32), 0.0).reshape(128, 4, 8)
    b1_part = jnp.pad(b1_part, ((0, 0), (0, 4), (0, 0)))
    vectors = jnp.concatenate([vectors, b1_part], 2)
    high = vectors.astype(BF)
    low = (vectors - high.astype(F32)).astype(BF)

    final = jnp.concatenate([qkv_grad.reshape(128, 8, 192), high, low], 2)
    out_w = exchange(after(out_w, g_tok).reshape(16, 8, D), XY)
    final = after(final, out_w)
    out_w = jnp.sum(out_w.astype(F32), 0)
    out_w = lax.ppermute(out_w, ALL, [(j * 8 + s, (2 * s + j // 8) * 8 + j % 8) for j in range(16) for s in range(8)])
    final = exchange(final, ALL).astype(F32)
    qkv_grad = jnp.sum(final[:, :, 0:192].reshape(8, HEADS, 8, 192), 0)
    qkv_grad = qkv_grad.reshape(HEADS, 8, 3, HEAD_DIM).transpose(1, 2, 0, 3).reshape(8, 3 * D)
    vectors = jnp.sum(final[:, :, 192:208] + final[:, :, 208:224], 0)
    fc1_bias_grad = vectors[0:4, 8:16].reshape(32)
    vectors = vectors[:, 0:8]
    return (
        outputs.astype(BF),
        input_grad,
        vectors[0],
        vectors[1],
        qkv_grad,
        vectors[2],
        vectors[3],
        out_w,
        vectors[4],
        vectors[5],
        vectors[6],
        fc1_grad,
        fc1_bias_grad,
        fc2_grad,
        vectors[7],
    )


def solution(mesh):
    fine = Mesh(mesh.devices.reshape(4, 2, 2, 4, 2), ALL)
    rows = P(ALL, None)
    vec = P(ALL)
    return jax.shard_map(
        body,
        mesh=fine,
        in_specs=(rows, P(("x", "yl")), vec, vec, rows, vec, vec, rows, vec, vec, vec, rows, vec, rows, vec, rows),
        out_specs=(rows, rows, vec, vec, rows, vec, vec, rows, vec, vec, vec, rows, vec, rows, vec),
        check_vma=False,
    )
```

```python
import functools

import jax
import jax.numpy as jnp
from jax import lax
from jax.experimental import pallas as pl
from jax.experimental.pallas import tpu as pltpu
from jax.sharding import Mesh
from jax.sharding import PartitionSpec as P

HEADS = 16
HEAD_DIM = 64
D = 1024
FF = 4096
TOK = 160
GROUP = 2560
HALF = 1280
EPSILON = 1e-06
NEGATIVE = -1e30
TILE = 256
TILES = GROUP // TILE
ALL = ("x", "yl", "yh", "z", "c")
TP = ("z", "c")
XY = ("x", "yl", "yh")
SEQ = ("yh", "z", "c")
BF = jnp.bfloat16
F32 = jnp.float32


def dot(left, right, dims=((1,), (0,))):
    return lax.dot_general(left, right, (dims, ((), ())), preferred_element_type=F32)


def params(mebibytes):
    return pltpu.CompilerParams(vmem_limit_bytes=mebibytes * 1024 * 1024)


def cost(micros):
    return pl.CostEstimate(flops=int(micros * 1e9), bytes_accessed=1 << 20, transcendentals=0)


def whole(*shape):
    return pl.BlockSpec(shape, lambda *_: (0,) * len(shape))


def along(value, axis, by):
    size = 4 if axis in ("x", "z") else 2
    return lax.ppermute(value, axis, [(i, (i + by) % size) for i in range(size)])


def along_y(value, by):
    pairs = []
    for yl in range(2):
        for yh in range(2):
            to = (yh * 2 + yl + by) % 4
            pairs.append((yl * 2 + yh, (to % 2) * 2 + to // 2))
    return lax.ppermute(value, ("yl", "yh"), pairs)


def from_up(value, k):
    return along(value, "z", 4 - k)


def after(value, *done):
    return lax.optimization_barrier((value, *done))[0]


def exchange(value, axes):
    return lax.all_to_all(value, axes, split_axis=0, concat_axis=0, tiled=True)


def project_rows(at, raw, sv, wh, qb, vb):
    rows = raw.astype(F32)
    center = rows - jnp.mean(rows, -1, keepdims=True)
    spread = jnp.mean(center * center, -1, keepdims=True)
    gain = sv[0:1, :].astype(F32)
    shift = sv[1:2, :].astype(F32)
    normed = (center * lax.rsqrt(spread + EPSILON) * gain + shift).astype(BF)
    mixed = dot(normed, wh[...])
    head = at[3]
    queries = (mixed[:, 0:64] + qb[head]).astype(BF) * jnp.asarray(0.125, BF)
    keys = mixed[:, 64:128].astype(BF)
    values = (mixed[:, 128:192] + vb[head]).astype(BF)
    return normed, jnp.concatenate([queries, jnp.zeros_like(queries)], 1), jnp.concatenate([keys, values], 1)


def choose_head(at, w, wh):
    @pl.when(pl.program_id(0) == 0)
    def _():
        wh[...] = jnp.where(at[0] == 0, w[:, 0:192], w[:, 192:384])


def image_range(at, ids):
    first = jnp.zeros_like(ids)
    length = jnp.zeros_like(ids)
    for m in range(4):
        first = jnp.where(ids == m, at[4 + m], first)
        length = jnp.where(ids == m, at[5 + m] - at[4 + m], length)
    return first, length


EDGE = TOK


def masked(values, base, first, length, whole_tile, fill):
    def cut(rows, start):
        place = lax.broadcasted_iota(jnp.int32, rows.shape, 0) - (first - base - start)
        return jnp.where(jnp.logical_and(place >= 0, place < length), rows, fill)

    if whole_tile:
        return cut(values, 0)
    end = HALF - EDGE
    return jnp.concatenate([cut(values[:EDGE], 0), values[EDGE:end], cut(values[end:], end)], 0)


def by_tile(at, half, tile, run):
    at_end = tile == jnp.where((at[0] + half) % 2 == 0, 0, HALF // TILE - 1)
    pl.when(at_end)(lambda: run(True))
    pl.when(jnp.logical_not(at_end))(lambda: run(False))


def attend_tile(at, half, queries, kv, vt, ids, att, o_out, lse_out, whole_tile):
    first, length = image_range(at, ids[...])
    scores = []
    for key_half, keys in enumerate(kv):
        raw = dot(keys[...], queries, ((1,), (1,)))
        base = ((key_half + at[0]) % 2) * HALF
        scores.append(masked(raw, base, first, length, whole_tile, NEGATIVE))
    top = jnp.maximum(jnp.max(scores[0], 0, keepdims=True), jnp.max(scores[1], 0, keepdims=True))
    total = 0.0
    out = 0.0
    for part, values in zip(scores, vt, strict=True):
        part = jnp.exp(part - top)
        total = total + jnp.sum(part, 0, keepdims=True)
        out = out + dot(values[64:128, :], part.astype(BF))
    out = out / total
    o_out[...] = out
    att[...] = out.T.astype(BF)
    lse_out[0] = top + jnp.log(total)


def project_kernel(at, x_a, x_b, w, sv, qb, vb, ids, n1_a, n1_b, q_a, kv_a, q_b, kv_b, att, o_out, lse_out, wh, vt_a, vt_b):
    step = pl.program_id(0)
    choose_head(at, w, wh)

    def put(x, n1, q_out, kv_out):
        normed, queries, pairs = project_rows(at, x[0].reshape(2 * TOK, D), sv, wh, qb, vb)
        n1[0] = normed.reshape(2, TOK, D)
        rows = pl.ds(pl.multiple_of((step % 4) * 2 * TOK, 2 * TOK), 2 * TOK)
        q_out[rows, :] = queries
        kv_out[rows, :] = pairs

    pl.when(step < 4)(lambda: put(x_a, n1_a, q_a, kv_a))
    pl.when(jnp.logical_and(step >= 4, step < 8))(lambda: put(x_b, n1_b, q_b, kv_b))

    @pl.when(step == 8)
    def _():
        vt_a[...] = kv_a[...].T
        vt_b[...] = kv_b[...].T

    @pl.when(step >= 8)
    def _():
        tile = step - 8
        queries = q_b[pl.ds(pl.multiple_of(tile * TILE, TILE), TILE), :]
        run = functools.partial(attend_tile, at, 1, queries, (kv_a, kv_b), (vt_a, vt_b), ids, att, o_out, lse_out)
        by_tile(at, 1, tile, run)


def project(at, near, far, weights, sv, qb, vb, ids):
    tiles = HALF // TILE
    one = lambda i, at: (jnp.minimum(i, 3), 0, 0, 0)
    two = lambda i, at: (jnp.clip(i - 4, 0, 3), 0, 0, 0)
    late = lambda i: jnp.maximum(i - 8, 0)
    block = lambda index: pl.BlockSpec((1, 2, TOK, D), index)
    rows = jax.ShapeDtypeStruct((4, 2, TOK, D), BF)
    pairs = jax.ShapeDtypeStruct((HALF, 128), BF)
    return pl.pallas_call(
        project_kernel,
        out_shape=[rows] * 2
        + [pairs] * 4
        + [
            jax.ShapeDtypeStruct((HALF, HEAD_DIM), BF),
            jax.ShapeDtypeStruct((HEAD_DIM, HALF), F32),
            jax.ShapeDtypeStruct((tiles, 1, TILE), F32),
        ],
        grid_spec=pltpu.PrefetchScalarGridSpec(
            num_scalar_prefetch=1,
            grid=(8 + tiles,),
            in_specs=[
                block(one),
                block(two),
                whole(D, 512),
                whole(8, D),
                whole(HEADS, 1, HEAD_DIM),
                whole(HEADS, 1, HEAD_DIM),
                pl.BlockSpec((1, TILE), lambda i, at: (0, late(i))),
            ],
            out_specs=[block(one), block(two)]
            + [whole(HALF, 128)] * 4
            + [
                pl.BlockSpec((TILE, HEAD_DIM), lambda i, at: (late(i), 0)),
                pl.BlockSpec((HEAD_DIM, TILE), lambda i, at: (0, late(i))),
                pl.BlockSpec((1, 1, TILE), lambda i, at: (late(i), 0, 0)),
            ],
            scratch_shapes=[pltpu.VMEM((D, 192), BF)] + [pltpu.VMEM((128, HALF), BF)] * 2,
        ),
        compiler_params=params(60),
        cost_estimate=cost(1),
        name="project_attend",
    )(at, near, far, weights, sv, qb, vb, ids)


def attend_kernel(half, at, q, kv_a, kv_b, ids, att, o_out, lse_out, vt_a, vt_b):
    @pl.when(pl.program_id(0) == 0)
    def _():
        vt_a[...] = kv_a[...].T
        vt_b[...] = kv_b[...].T

    run = functools.partial(attend_tile, at, half, q[...], (kv_a, kv_b), (vt_a, vt_b), ids, att, o_out, lse_out)
    by_tile(at, half, pl.program_id(0), run)


def attend(at, half, q, kv, ids):
    tiles = HALF // TILE
    pairs = whole(HALF, 128)
    return pl.pallas_call(
        functools.partial(attend_kernel, half),
        out_shape=(
            jax.ShapeDtypeStruct((HALF, HEAD_DIM), BF),
            jax.ShapeDtypeStruct((HEAD_DIM, HALF), F32),
            jax.ShapeDtypeStruct((tiles, 1, TILE), F32),
        ),
        grid_spec=pltpu.PrefetchScalarGridSpec(
            num_scalar_prefetch=1,
            grid=(tiles,),
            in_specs=[
                pl.BlockSpec((TILE, 128), lambda i, at: (i, 0)),
                pairs,
                pairs,
                pl.BlockSpec((1, TILE), lambda i, at: (0, i)),
            ],
            out_specs=[
                pl.BlockSpec((TILE, HEAD_DIM), lambda i, at: (i, 0)),
                pl.BlockSpec((HEAD_DIM, TILE), lambda i, at: (0, i)),
                pl.BlockSpec((1, 1, TILE), lambda i, at: (i, 0, 0)),
            ],
            scratch_shapes=[pltpu.VMEM((128, HALF), BF)] * 2,
        ),
        compiler_params=params(60),
        cost_estimate=cost(1),
        name="attend",
    )(at, q, *kv, ids)


def attend_back_kernel(at, q_a, q_b, kv_a, kv_b, do_in, o_a, o_b, lse_a, lse_b, ids_a, ids_b, g_abs, g_a, g_b, q, kv, do, kt, dq, dkv):
    tile = pl.program_id(0)
    yh = at[0]

    @pl.when(tile == 0)
    def _():
        for ref, one, two in ((q, q_a, q_b), (kv, kv_a, kv_b)):
            ref[0:HALF, :] = one[...]
            ref[HALF:GROUP, :] = two[...]
        kt[...] = kv[...].T
        for half in range(2):
            start = ((half + yh) % 2) * HALF
            for s in range(8):
                packed = do_in[half * 8 + s]
                block = jnp.concatenate([packed[:, 0:64], packed[:, 64:128]], 0)
                block = jnp.concatenate([jnp.zeros_like(block), block], 1)
                do[pl.ds(pl.multiple_of(start + s * TOK, TOK), TOK), :] = block
        dkv[...] = jnp.zeros_like(dkv)

    near = tile < TILES // 2

    def run(whole_tile):
        first, length = image_range(at, jnp.where(near, ids_a[...], ids_b[...]))
        o_tile = jnp.where(near, o_a[...], o_b[...])
        lse = jnp.where(near, lse_a[0], lse_b[0])
        rows = pl.ds(pl.multiple_of(tile * TILE, TILE), TILE)
        queries = q[rows, :]
        grads = do[rows, :]
        delta = jnp.sum(o_tile * grads[:, 64:128].astype(F32).T, 0, keepdims=True)
        dq_tile = 0.0
        for half in range(2):
            here = slice(half * HALF, half * HALF + HALF)
            scores = dot(kv[here, :], queries, ((1,), (1,)))
            base = ((half + yh) % 2) * HALF
            probs = jnp.exp(masked(scores, base, first, length, whole_tile, NEGATIVE) - lse)
            probs_grad = dot(kv[here, :], grads, ((1,), (1,)))
            scores_grad = (probs * (probs_grad - delta)).astype(BF)
            dkv[here, :] += dot(scores_grad, queries) + dot(probs.astype(BF), grads)
            dq_tile = dq_tile + dot(kt[0:64, here], scores_grad)
        dq[rows, :] = (dq_tile.T * 0.125).astype(BF)

    place = jnp.where(near, tile, tile - TILES // 2)
    at_end = place == jnp.where((yh + jnp.where(near, 0, 1)) % 2 == 0, 0, TILES // 2 - 1)
    pl.when(at_end)(lambda: run(True))
    pl.when(jnp.logical_not(at_end))(lambda: run(False))

    @pl.when(tile == TILES - 1)
    def _():
        for ref, half in ((g_a, 0), (g_b, 1)):
            here = slice(half * HALF, half * HALF + HALF)
            ref[:, 0:64] = dq[here, :]
            ref[:, 64:192] = dkv[here, :].astype(BF)
            for s in range(8):
                block = ref[s * TOK : s * TOK + TOK, :]
                to = ((half + yh) % 2) * 8 + s
                g_abs[to, 0:TOK, :] = block[:, 0:128]
                g_abs[to, TOK : TOK + 80, :] = jnp.concatenate([block[0:80, 128:192], block[80:TOK, 128:192]], 1)


def attend_back(at, q, kv, do, o, lse, ids):
    pairs = whole(HALF, 128)
    last = TILES // 2 - 1
    one = lambda i: jnp.minimum(i, last)
    two = lambda i: jnp.maximum(i - last - 1, 0)
    wide = pltpu.VMEM((GROUP, 128), BF)
    return pl.pallas_call(
        attend_back_kernel,
        out_shape=(
            jax.ShapeDtypeStruct((HEADS, 240, 128), BF),
            jax.ShapeDtypeStruct((HALF, 192), BF),
            jax.ShapeDtypeStruct((HALF, 192), BF),
        ),
        grid_spec=pltpu.PrefetchScalarGridSpec(
            num_scalar_prefetch=1,
            grid=(TILES,),
            in_specs=[pairs] * 4
            + [whole(HEADS, TOK // 2, 128)]
            + [pl.BlockSpec((HEAD_DIM, TILE), lambda i, at, f=f: (0, f(i))) for f in (one, two)]
            + [pl.BlockSpec((1, 1, TILE), lambda i, at, f=f: (f(i), 0, 0)) for f in (one, two)]
            + [pl.BlockSpec((1, TILE), lambda i, at, f=f: (0, f(i))) for f in (one, two)],
            out_specs=[whole(HEADS, 240, 128), whole(HALF, 192), whole(HALF, 192)],
            scratch_shapes=[
                wide,
                wide,
                wide,
                pltpu.VMEM((128, GROUP), BF),
                pltpu.VMEM((GROUP, HEAD_DIM), BF),
                pltpu.VMEM((GROUP, 128), F32),
            ],
        ),
        compiler_params=params(60),
        cost_estimate=cost(20),
        name="attend_back",
    )(at, *q, *kv, do, *o, *lse, *ids)


def feed_kernel(at, *refs):
    blocks, refs = refs[:8], refs[8:]
    x, w_out, sv, rows, b1, dy, resid_out, att_out, y_out, dn2_other, dn2_own, w1_out, w2_out, b1_out = refs[:14]
    wide, w1, w2, w1_grad, w2_grad = refs[14:]
    step = pl.program_id(0)
    z, core = at[1], at[2]
    own = step >= 2
    pair = step % 2

    @pl.when(step == 0)
    def _():
        for j in range(16):
            w1[j * 64 : j * 64 + 32, :] = rows[j, 0:32, 0:512]
            w1[j * 64 + 32 : j * 64 + 64, :] = rows[j, 0:32, 512:1024]
            w2[j * 32 : j * 32 + 32, :] = rows[j, 32:64, :]
        b1_out[...] = jnp.zeros_like(b1_out)
        w1_grad[...] = jnp.zeros_like(w1_grad)
        w2_grad[...] = jnp.zeros_like(w2_grad)

    for k in range(4):
        mine, theirs = (block[:, 0].reshape(2 * TOK, 128) for block in (blocks[k], blocks[4 + k]))
        one = jnp.where(core == 0, mine, theirs)
        two = jnp.where(core == 0, theirs, mine)
        for h in range(2):
            lane = pl.multiple_of(h * 512 + ((z + k) % 4) * 128, 128)
            here = slice(h * 64, h * 64 + 64)
            wide[:, pl.ds(lane, 128)] = jnp.concatenate([one[:, here], two[:, here]], 1)
    resid = x[:, 0].reshape(2 * TOK, D).astype(F32) + dot(wide[...], w_out[...]) + sv[4:5, :].astype(F32)

    @pl.when(jnp.logical_and(own, pair == z // 2))
    def _():
        resid_out[...] = jnp.where(z % 2 == 0, resid[:TOK], resid[TOK:])
        att_out[...] = jnp.where(z % 2 == 0, wide[:TOK, :], wide[TOK:, :])

    center = resid - jnp.mean(resid, -1, keepdims=True)
    spread = jnp.mean(center * center, -1, keepdims=True)
    normed = (center * lax.rsqrt(spread + EPSILON) * sv[5:6, :].astype(F32) + sv[6:7, :].astype(F32)).astype(BF)
    pre = dot(normed, w1[...]) + b1[...].astype(F32)
    cdf = 0.5 * (1.0 + lax.erf(pre * (0.5**0.5)))
    hidden = (pre * cdf).astype(BF)
    slope = cdf + pre * jnp.exp(-0.5 * pre * pre) * 0.3989422804014327
    dy_rows = dy[:, 0].reshape(2 * TOK, D)
    hidden_grad = dot(dy_rows, w2[...], ((1,), (1,)))
    pre_grad = (hidden_grad * slope).astype(BF)
    normed_grad = dot(pre_grad, w1[...], ((1,), (1,))).astype(BF).reshape(2, TOK, D)
    y_out[:, 0] = dot(hidden, w2[...]).astype(BF).reshape(2, TOK, D)
    w2_grad[...] += dot(hidden, dy_rows, ((0,), (0,)))
    w1_grad[...] += dot(normed, pre_grad, ((0,), (0,)))
    b1_out[...] += jnp.sum(pre_grad.astype(F32), 0, keepdims=True)

    @pl.when(own)
    def _():
        dn2_own[...] = normed_grad

    @pl.when(jnp.logical_not(own))
    def _():
        dn2_other[...] = normed_grad

    @pl.when(step == 3)
    def _():
        w1_out[...] = w1_grad[...].astype(BF).reshape(128, 8, 512)
        w2_out[...] = w2_grad[...].astype(BF).reshape(16, 32, D)


def feed(at, att_own, att_other, x, w_out, sv, rows, b1, dy):
    core_of = lambda i, at: jnp.where(i >= 2, at[2], 1 - at[2])
    tok_spec = lambda width: pl.BlockSpec((2, 1, TOK, width), lambda i, at: (i % 2, core_of(i, at), 0, 0))
    return pl.pallas_call(
        feed_kernel,
        out_shape=(
            jax.ShapeDtypeStruct((TOK, D), F32),
            jax.ShapeDtypeStruct((TOK, D), BF),
            jax.ShapeDtypeStruct((4, 2, TOK, D), BF),
            jax.ShapeDtypeStruct((4, TOK, D), BF),
            jax.ShapeDtypeStruct((4, TOK, D), BF),
            jax.ShapeDtypeStruct((128, 8, 512), BF),
            jax.ShapeDtypeStruct((16, 32, D), BF),
            jax.ShapeDtypeStruct((1, 512), F32),
        ),
        grid_spec=pltpu.PrefetchScalarGridSpec(
            num_scalar_prefetch=1,
            grid=(4,),
            in_specs=[tok_spec(128)] * 8
            + [
                tok_spec(D),
                whole(D, D),
                whole(8, D),
                whole(16, 64, D),
                whole(1, 512),
                tok_spec(D),
            ],
            out_specs=[
                whole(TOK, D),
                whole(TOK, D),
                tok_spec(D),
                pl.BlockSpec((2, TOK, D), lambda i, at: (jnp.minimum(i, 1), 0, 0)),
                pl.BlockSpec((2, TOK, D), lambda i, at: (jnp.maximum(i - 2, 0), 0, 0)),
                whole(128, 8, 512),
                whole(16, 32, D),
                whole(1, 512),
            ],
            scratch_shapes=[
                pltpu.VMEM((2 * TOK, D), BF),
                pltpu.VMEM((D, 512), BF),
                pltpu.VMEM((512, D), BF),
                pltpu.VMEM((D, 512), F32),
                pltpu.VMEM((512, D), F32),
            ],
        ),
        compiler_params=params(56),
        cost_estimate=cost(20),
        name="out_feed",
    )(at, *att_own, *att_other, x, w_out, sv, rows, b1, dy)


def mix_kernel(at, own, came, *outs):
    for k in range(4):
        here = pl.ds((at[1] + k) % 4, 1)
        outs[k][...] = (own[here][0].astype(F32) + came[here][0].astype(F32)).astype(BF)


def mix(at, own, came):
    return pl.pallas_call(
        mix_kernel,
        out_shape=[jax.ShapeDtypeStruct((TOK, D), BF)] * 4,
        grid_spec=pltpu.PrefetchScalarGridSpec(
            num_scalar_prefetch=1,
            grid=(1,),
            in_specs=[whole(4, TOK, D)] * 2,
            out_specs=[whole(TOK, D)] * 4,
        ),
        compiler_params=params(60),
        cost_estimate=cost(2),
        name="mix",
    )(at, own, came)


def norm_back(values, gain, grad):
    center = values - jnp.mean(values, -1, keepdims=True)
    spread = jnp.mean(center * center, -1, keepdims=True)
    r = lax.rsqrt(spread + EPSILON)
    n = center * r
    e = grad * gain
    inner = r * (e - jnp.mean(e, -1, keepdims=True) - n * jnp.mean(e * n, -1, keepdims=True))
    return inner, jnp.sum(grad * n, 0, keepdims=True), jnp.sum(grad, 0, keepdims=True)


def middle_kernel(m0, m1, m2, m3, resid, dy, sv, w_out, resid_grad_out, branch_out, att_grad_out, sums):
    grad = m0[...].astype(F32) + m1[...].astype(F32) + m2[...].astype(F32) + m3[...].astype(F32)
    dy_f = dy[...].astype(F32)
    part, gain_grad, shift_grad = norm_back(resid[...], sv[5:6, :].astype(F32), grad)
    resid_grad = dy_f + part
    resid_grad_out[...] = resid_grad
    branch = resid_grad.astype(BF)
    branch_out[...] = branch
    sums[0:1, :] = jnp.sum(branch.astype(F32), 0, keepdims=True)
    sums[1:2, :] = gain_grad
    sums[2:3, :] = shift_grad
    sums[3:4, :] = jnp.sum(dy_f, 0, keepdims=True)
    att_grad = dot(branch, w_out[...], ((1,), (1,))).astype(BF)
    for h in range(HEADS):
        lane = h * 64
        att_grad_out[h] = jnp.concatenate(
            [att_grad[0:80, lane : lane + 64], att_grad[80:160, lane : lane + 64]], 1
        )


def middle(parts, resid, dy, sv, w_out):
    return pl.pallas_call(
        middle_kernel,
        out_shape=(
            jax.ShapeDtypeStruct((TOK, D), F32),
            jax.ShapeDtypeStruct((TOK, D), BF),
            jax.ShapeDtypeStruct((HEADS, TOK // 2, 128), BF),
            jax.ShapeDtypeStruct((4, D), F32),
        ),
        grid=(1,),
        in_specs=[whole(TOK, D)] * 6 + [whole(8, D), whole(D, D)],
        out_specs=[whole(TOK, D), whole(TOK, D), whole(HEADS, TOK // 2, 128), whole(4, D)],
        compiler_params=params(16),
        cost_estimate=cost(5),
        name="middle",
    )(*parts, resid, dy, sv, w_out)


def last_kernel(g_a, g_b, w, x, resid_grad, sv, out, sums, biases, total):
    step = pl.program_id(0)

    @pl.when(step == 0)
    def _():
        total[...] = jnp.zeros_like(total)

    pair = []
    for packed in (g_a[0], g_b[0]):
        values = jnp.concatenate([packed[160:240, 0:64], packed[160:240, 64:128]], 0)
        pair += [packed[0:160, :], values]
    pair = jnp.concatenate(pair, 1)
    total[...] += dot(pair, w[0], ((1,), (1,)))
    biases[0] = jnp.sum(pair.astype(F32), 0, keepdims=True)

    @pl.when(step == 7)
    def _():
        part, gain_grad, shift_grad = norm_back(x[...].astype(F32), sv[0:1, :].astype(F32), total[...])
        out[...] = (resid_grad[...] + part).astype(BF)
        sums[0:1, :] = gain_grad
        sums[1:2, :] = shift_grad


def last(g, w, x, resid_grad, sv):
    return pl.pallas_call(
        last_kernel,
        out_shape=(
            jax.ShapeDtypeStruct((TOK, D), BF),
            jax.ShapeDtypeStruct((2, D), F32),
            jax.ShapeDtypeStruct((8, 1, 384), F32),
        ),
        grid=(8,),
        in_specs=[
            pl.BlockSpec((1, 240, 128), lambda i: (i, 0, 0)),
            pl.BlockSpec((1, 240, 128), lambda i: (i + 8, 0, 0)),
            pl.BlockSpec((1, D, 384), lambda i: (i, 0, 0)),
            whole(TOK, D),
            whole(TOK, D),
            whole(8, D),
        ],
        out_specs=[whole(TOK, D), whole(2, D), pl.BlockSpec((1, 1, 384), lambda i: (i, 0, 0))],
        scratch_shapes=[pltpu.VMEM((TOK, D), F32)],
        compiler_params=params(48),
        cost_estimate=cost(5),
        name="last",
    )(g, g, w, x, resid_grad, sv)


def body(
    inputs,
    image_ids,
    ln1_gain,
    ln1_shift,
    qkv_weight,
    query_bias,
    value_bias,
    out_weight,
    out_bias,
    ln2_gain,
    ln2_shift,
    fc1_weight,
    fc1_bias,
    fc2_weight,
    fc2_bias,
    out_grad,
):
    xi, yl, yh, zi, ci = (lax.axis_index(name) for name in ALL)
    zc = zi * 2 + ci
    where_at = jnp.arange(16)
    starts = jnp.sum((image_ids[:, None] < where_at[None, :] - 4).astype(jnp.int32), 0)
    at = jnp.where(where_at == 0, yh, jnp.where(where_at == 1, zi, jnp.where(where_at == 2, ci, yh * 8 + zc)))
    at = jnp.where(where_at < 4, at, starts).astype(jnp.int32)

    near = lax.all_gather(inputs, TP, axis=0, tiled=True).reshape(4, 2, TOK, D)
    crossed = along(inputs, "yh", 1)

    qkv = qkv_weight.reshape(8, 3, 2, 8, HEAD_DIM).transpose(3, 0, 2, 1, 4).reshape(8, 8, 384)
    small = jnp.stack(
        [ln1_gain, ln1_shift, query_bias, value_bias, out_bias, ln2_gain, ln2_shift, fc2_bias], 1
    )
    small = jnp.broadcast_to(jnp.pad(small, ((0, 0), (0, 120)))[None], (8, 8, 128))
    fc1 = fc1_weight.reshape(8, 16, 8, 32).transpose(2, 0, 1, 3).reshape(8, 8, 512)
    columns = exchange(jnp.concatenate([qkv, small, fc1], 2), TP)
    far = lax.all_gather(after(crossed, columns), TP, axis=0, tiled=True).reshape(4, 2, TOK, D)
    dy_all = lax.all_gather(after(out_grad, crossed, columns), TP, axis=0, tiled=True).reshape(4, 2, TOK, D)
    columns = columns.reshape(64, D)

    fc1 = jnp.concatenate([columns[0:32, 512:], columns[32:64, 512:]], 1)
    columns = jnp.concatenate([columns[0:32, 0:512], columns[32:64, 0:512]], 1)
    bias = jnp.pad(fc1_bias[None], ((0, 7), (0, D - 32)))
    rows = jnp.concatenate([fc1, fc2_weight, columns, out_weight, bias], 0)
    rows = exchange(jnp.broadcast_to(rows[None], (16, 112, D)), XY)
    columns = jnp.concatenate([rows[:, 64:96, 0:512], rows[:, 64:96, 512:]], 1).reshape(D, 512)
    b1 = rows[:, 104, 0:32].reshape(1, 512)
    sv = columns[:, 384:392].T
    qb = sv[2].astype(F32).reshape(HEADS, 1, HEAD_DIM)
    vb = sv[3].astype(F32).reshape(HEADS, 1, HEAD_DIM)

    ids = image_ids.reshape(2, 1, HALF)
    ids = jnp.where(yh == 0, ids[0], ids[1]), jnp.where(yh == 0, ids[1], ids[0])
    n1_near, n1_far, q_near, kv_near, q_far, kv_far, att_far, o_far, lse_far = project(
        at, near, far, columns, sv, qb, vb, ids[1]
    )
    q, kv = (q_near, q_far), (kv_near, kv_far)
    theirs = along(att_far, "yh", 1)
    att_near, o_near, lse_near = attend(at, 0, after(q[0], att_far), kv, ids[0])
    w_out = lax.all_gather(rows[:, 96:104], TP, axis=1, tiled=True).reshape(D, D)

    att_two = jnp.where(
        yh == 0, jnp.concatenate([att_near, theirs], 1), jnp.concatenate([theirs, att_near], 1)
    )
    att_own = [att_two] + [from_up(att_two, k) for k in (1, 2, 3)]
    att_other = [along(block, "c", 1) for block in att_own]
    w_qkv = lax.all_gather(after(columns[:, 0:384], *att_other), TP, axis=0, tiled=False)
    split = lambda blocks: [block.reshape(4, 2, TOK, 128) for block in blocks]
    resid, att_tok, y_part, dn2_other, dn2_own, fc1_grad, fc2_grad, b1_grad = feed(
        at, split(att_own), split(att_other), near, w_out, sv, rows, b1, dy_all
    )

    mixed = mix(at, dn2_own, along(dn2_other, "c", 1))
    parts = [mixed[0]] + [along(mixed[k], "z", k) for k in (1, 2, 3)]
    fc2_grad = exchange(after(fc2_grad, mixed[0]), XY)
    parts = [after(parts[0], fc2_grad)] + parts[1:]
    resid_grad, branch_grad, att_grad, mid_sums = middle(parts, resid, out_grad, sv, w_out)
    do = exchange(after(att_grad, w_qkv), SEQ)
    turn = ((0,), (0,))

    g, g_near, g_far = attend_back(
        at, q, kv, do, (o_near, o_far), (lse_near, lse_far), ids
    )

    out_w = dot(att_tok, branch_grad, turn).astype(BF)
    out_w = lax.psum_scatter(out_w, TP, scatter_dimension=0, tiled=True)

    fc1_grad = exchange(after(fc1_grad, do), ALL)
    g_tok = exchange(after(g, fc1_grad), SEQ)
    fc2_grad = jnp.sum(fc2_grad.astype(F32), 0)
    fc1_grad = jnp.sum(fc1_grad.reshape(16, 8, 8, 512).astype(F32), 0)
    fc1_grad = fc1_grad.reshape(8, 8, 16, 32).transpose(1, 2, 0, 3).reshape(8, FF)

    summed = lax.psum_scatter(after(y_part, *parts).reshape(HALF, D), TP, scatter_dimension=0, tiled=True)
    outputs = resid + summed.astype(F32) + sv[7].astype(F32)

    qkv_grad = dot(n1_near.reshape(HALF, D), g_near, turn) + dot(n1_far.reshape(HALF, D), g_far, turn)
    qkv_grad = qkv_grad.astype(BF)
    pick = lambda v, axis, place: lax.dynamic_index_in_dim(v, place, axis, keepdims=False)
    out_w = after(out_w, qkv_grad).reshape(4, 2, 2, 8, D)
    total = pick(out_w, 0, xi).astype(F32)
    for k in (1, 2, 3):
        total = total + along(pick(out_w, 0, (xi + k) % 4), "x", k).astype(F32)
    out_w = total.astype(BF)
    g_tok = after(g_tok, out_w)
    input_grad, norm_sums, biases = last(g_tok, w_qkv, inputs, resid_grad, sv)
    biases = biases.reshape(8, 2, 3, HEAD_DIM).transpose(2, 1, 0, 3).reshape(3, D)
    vectors = jnp.concatenate([norm_sums, biases[0:1], biases[2:3], mid_sums])
    vectors = vectors.reshape(8, 128, 8).transpose(1, 0, 2)
    mine = jnp.arange(8)[None, :, None] == zc
    b1_part = jnp.where(mine, b1_grad.reshape(16, 1, 32), 0.0).reshape(128, 4, 8)
    b1_part = jnp.pad(b1_part, ((0, 0), (0, 4), (0, 0)))
    vectors = jnp.concatenate([vectors, b1_part], 2)
    high = vectors.astype(BF)
    low = (vectors - high.astype(F32)).astype(BF)

    final = jnp.concatenate([qkv_grad.reshape(128, 8, 192), high, low], 2)
    final = after(final, out_w)
    out_w = after(out_w, norm_sums)
    by_y = lambda y: pick(pick(out_w, 0, y % 2), 0, y // 2)
    yi = yh * 2 + yl
    total = by_y(yi).astype(F32)
    for k in (1, 2, 3):
        total = total + along_y(by_y((yi + k) % 4), k).astype(F32)
    out_w = lax.ppermute(total, ALL, [(j * 8 + s, (2 * s + j // 8) * 8 + j % 8) for j in range(16) for s in range(8)])
    final = exchange(final, ALL).astype(F32)
    qkv_grad = jnp.sum(final[:, :, 0:192].reshape(8, HEADS, 8, 192), 0)
    qkv_grad = qkv_grad.reshape(HEADS, 8, 3, HEAD_DIM).transpose(1, 2, 0, 3).reshape(8, 3 * D)
    vectors = jnp.sum(final[:, :, 192:208] + final[:, :, 208:224], 0)
    fc1_bias_grad = vectors[0:4, 8:16].reshape(32)
    vectors = vectors[:, 0:8]
    return (
        outputs.astype(BF),
        input_grad,
        vectors[0],
        vectors[1],
        qkv_grad,
        vectors[2],
        vectors[3],
        out_w,
        vectors[4],
        vectors[5],
        vectors[6],
        fc1_grad,
        fc1_bias_grad,
        fc2_grad,
        vectors[7],
    )


def solution(mesh):
    fine = Mesh(mesh.devices.reshape(4, 2, 2, 4, 2), ALL)
    rows = P(ALL, None)
    vec = P(ALL)
    return jax.shard_map(
        body,
        mesh=fine,
        in_specs=(rows, P(("x", "yl")), vec, vec, rows, vec, vec, rows, vec, vec, vec, rows, vec, rows, vec, rows),
        out_specs=(rows, rows, vec, vec, rows, vec, vec, rows, vec, vec, vec, rows, vec, rows, vec),
        check_vma=False,
    )
```

```python
import functools

import jax
import jax.numpy as jnp
from jax import lax
from jax.experimental import pallas as pl
from jax.experimental.pallas import tpu as pltpu
from jax.sharding import Mesh
from jax.sharding import PartitionSpec as P

HEADS = 16
HEAD_DIM = 64
D = 1024
FF = 4096
TOK = 160
GROUP = 2560
HALF = 1280
EPSILON = 1e-06
NEGATIVE = -1e30
TILE = 256
TILES = GROUP // TILE
ALL = ("x", "yl", "yh", "z", "c")
TP = ("z", "c")
XY = ("x", "yl", "yh")
SEQ = ("yh", "z", "c")
BF = jnp.bfloat16
F32 = jnp.float32


def dot(left, right, dims=((1,), (0,))):
    return lax.dot_general(left, right, (dims, ((), ())), preferred_element_type=F32)


def params(mebibytes):
    return pltpu.CompilerParams(vmem_limit_bytes=mebibytes * 1024 * 1024)


def cost(micros):
    return pl.CostEstimate(flops=int(micros * 1e9), bytes_accessed=1 << 20, transcendentals=0)


def whole(*shape):
    return pl.BlockSpec(shape, lambda *_: (0,) * len(shape))


def along(value, axis, by):
    size = 4 if axis in ("x", "z") else 2
    return lax.ppermute(value, axis, [(i, (i + by) % size) for i in range(size)])


def along_y(value, by):
    pairs = []
    for yl in range(2):
        for yh in range(2):
            to = (yh * 2 + yl + by) % 4
            pairs.append((yl * 2 + yh, (to % 2) * 2 + to // 2))
    return lax.ppermute(value, ("yl", "yh"), pairs)


def from_up(value, k):
    return along(value, "z", 4 - k)


def after(value, *done):
    return lax.optimization_barrier((value, *done))[0]


def exchange(value, axes):
    return lax.all_to_all(value, axes, split_axis=0, concat_axis=0, tiled=True)


def project_rows(raw, sv, wh, bias):
    rows = raw.astype(F32)
    center = rows - jnp.mean(rows, -1, keepdims=True)
    spread = jnp.mean(center * center, -1, keepdims=True)
    gain = sv[0:1, :].astype(F32)
    shift = sv[1:2, :].astype(F32)
    normed = (center * lax.rsqrt(spread + EPSILON) * gain + shift).astype(BF)
    mixed = dot(normed, wh[...])
    queries = (mixed[:, 0:64] + bias[0:1, :]).astype(BF) * jnp.asarray(0.125, BF)
    keys = mixed[:, 64:128].astype(BF)
    values = (mixed[:, 128:192] + bias[8:9, :]).astype(BF)
    return normed, jnp.concatenate([queries, jnp.zeros_like(queries)], 1), jnp.concatenate([keys, values], 1)


def choose_head(at, w, sv, heads, wh, bias):
    @pl.when(pl.program_id(0) == 0)
    def _():
        for j in range(16):
            for part in range(2):
                lane = part * 512
                rows = jnp.where(at[0] == 0, w[j, :, lane : lane + 192], w[j, :, lane + 192 : lane + 384])
                wh[j * 64 + part * 32 : j * 64 + part * 32 + 32, :] = rows
                heads[j * 64 + part * 32 : j * 64 + part * 32 + 32, :] = w[j, :, lane : lane + 384]
        for row, place in ((2, 0), (3, 8)):
            value = sv[row : row + 1, 0:64]
            for h in range(1, HEADS):
                value = jnp.where(at[3] == h, sv[row : row + 1, h * 64 : h * 64 + 64], value)
            bias[place : place + 1, :] = value.astype(F32)


def image_range(at, ids):
    first = jnp.zeros_like(ids)
    length = jnp.zeros_like(ids)
    for m in range(4):
        first = jnp.where(ids == m, at[4 + m], first)
        length = jnp.where(ids == m, at[5 + m] - at[4 + m], length)
    return first, length


EDGE = TOK


def masked(values, base, first, length, whole_tile, fill):
    def cut(rows, start):
        place = lax.broadcasted_iota(jnp.int32, rows.shape, 0) - (first - base - start)
        return jnp.where(jnp.logical_and(place >= 0, place < length), rows, fill)

    if whole_tile:
        return cut(values, 0)
    end = HALF - EDGE
    return jnp.concatenate([cut(values[:EDGE], 0), values[EDGE:end], cut(values[end:], end)], 0)


def by_tile(at, half, tile, run):
    at_end = tile == jnp.where((at[0] + half) % 2 == 0, 0, HALF // TILE - 1)
    pl.when(at_end)(lambda: run(True))
    pl.when(jnp.logical_not(at_end))(lambda: run(False))


def attend_tile(at, half, queries, kv, vt, ids, att, o_out, lse_out, whole_tile):
    first, length = image_range(at, ids[0])
    scores = []
    for key_half, keys in enumerate(kv):
        raw = dot(keys[...], queries, ((1,), (1,)))
        base = ((key_half + at[0]) % 2) * HALF
        scores.append(masked(raw, base, first, length, whole_tile, NEGATIVE))
    top = jnp.maximum(jnp.max(scores[0], 0, keepdims=True), jnp.max(scores[1], 0, keepdims=True))
    total = 0.0
    out = 0.0
    for part, values in zip(scores, vt, strict=True):
        part = jnp.exp(part - top)
        total = total + jnp.sum(part, 0, keepdims=True)
        out = out + dot(values[64:128, :], part.astype(BF))
    out = out / total
    o_out[...] = out
    att[...] = out.T.astype(BF)
    lse_out[0] = top + jnp.log(total)


def project_kernel(at, x_a, x_b, w, sv, ids, n1_a, n1_b, q_a, kv_a, q_b, kv_b, heads, att, o_out, lse_out, wh, bias, vt_a, vt_b):
    step = pl.program_id(0)
    choose_head(at, w, sv, heads, wh, bias)

    def put(x, n1, q_out, kv_out):
        normed, queries, pairs = project_rows(x[0].reshape(2 * TOK, D), sv, wh, bias)
        n1[0] = normed.reshape(2, TOK, D)
        rows = pl.ds(pl.multiple_of((step % 4) * 2 * TOK, 2 * TOK), 2 * TOK)
        q_out[rows, :] = queries
        kv_out[rows, :] = pairs

    pl.when(step < 4)(lambda: put(x_a, n1_a, q_a, kv_a))
    pl.when(jnp.logical_and(step >= 4, step < 8))(lambda: put(x_b, n1_b, q_b, kv_b))

    @pl.when(step == 8)
    def _():
        vt_a[...] = kv_a[...].T
        vt_b[...] = kv_b[...].T

    @pl.when(step >= 8)
    def _():
        tile = step - 8
        queries = q_b[pl.ds(pl.multiple_of(tile * TILE, TILE), TILE), :]
        run = functools.partial(attend_tile, at, 1, queries, (kv_a, kv_b), (vt_a, vt_b), ids, att, o_out, lse_out)
        by_tile(at, 1, tile, run)


def project(at, near, far, rows, sv, ids):
    tiles = HALF // TILE
    one = lambda i, at: (jnp.minimum(i, 3), 0, 0, 0)
    two = lambda i, at: (jnp.clip(i - 4, 0, 3), 0, 0, 0)
    late = lambda i: jnp.maximum(i - 8, 0)
    block = lambda index: pl.BlockSpec((1, 2, TOK, D), index)
    tokens = jax.ShapeDtypeStruct((4, 2, TOK, D), BF)
    pairs = jax.ShapeDtypeStruct((HALF, 128), BF)
    return pl.pallas_call(
        project_kernel,
        out_shape=[tokens] * 2
        + [pairs] * 4
        + [
            jax.ShapeDtypeStruct((D, 384), BF),
            jax.ShapeDtypeStruct((HALF, HEAD_DIM), BF),
            jax.ShapeDtypeStruct((HEAD_DIM, HALF), F32),
            jax.ShapeDtypeStruct((tiles, 1, TILE), F32),
        ],
        grid_spec=pltpu.PrefetchScalarGridSpec(
            num_scalar_prefetch=1,
            grid=(8 + tiles,),
            in_specs=[
                block(one),
                block(two),
                whole(16, 32, D),
                whole(8, D),
                pl.BlockSpec((1, 1, TILE), lambda i, at: (1 - at[0], 0, late(i))),
            ],
            out_specs=[block(one), block(two)]
            + [whole(HALF, 128)] * 4
            + [
                whole(D, 384),
                pl.BlockSpec((TILE, HEAD_DIM), lambda i, at: (late(i), 0)),
                pl.BlockSpec((HEAD_DIM, TILE), lambda i, at: (0, late(i))),
                pl.BlockSpec((1, 1, TILE), lambda i, at: (late(i), 0, 0)),
            ],
            scratch_shapes=[pltpu.VMEM((D, 192), BF), pltpu.VMEM((16, HEAD_DIM), F32)] + [pltpu.VMEM((128, HALF), BF)] * 2,
        ),
        compiler_params=params(60),
        cost_estimate=cost(1),
        name="project_attend",
    )(at, near, far, rows, sv, ids)


def attend_kernel(half, at, q, kv_a, kv_b, ids, att, o_out, lse_out, vt_a, vt_b):
    @pl.when(pl.program_id(0) == 0)
    def _():
        vt_a[...] = kv_a[...].T
        vt_b[...] = kv_b[...].T

    run = functools.partial(attend_tile, at, half, q[...], (kv_a, kv_b), (vt_a, vt_b), ids, att, o_out, lse_out)
    by_tile(at, half, pl.program_id(0), run)


def attend(at, half, q, kv, ids):
    tiles = HALF // TILE
    pairs = whole(HALF, 128)
    return pl.pallas_call(
        functools.partial(attend_kernel, half),
        out_shape=(
            jax.ShapeDtypeStruct((HALF, HEAD_DIM), BF),
            jax.ShapeDtypeStruct((HEAD_DIM, HALF), F32),
            jax.ShapeDtypeStruct((tiles, 1, TILE), F32),
        ),
        grid_spec=pltpu.PrefetchScalarGridSpec(
            num_scalar_prefetch=1,
            grid=(tiles,),
            in_specs=[
                pl.BlockSpec((TILE, 128), lambda i, at: (i, 0)),
                pairs,
                pairs,
                pl.BlockSpec((1, 1, TILE), lambda i, at: ((at[0] + half) % 2, 0, i)),
            ],
            out_specs=[
                pl.BlockSpec((TILE, HEAD_DIM), lambda i, at: (i, 0)),
                pl.BlockSpec((HEAD_DIM, TILE), lambda i, at: (0, i)),
                pl.BlockSpec((1, 1, TILE), lambda i, at: (i, 0, 0)),
            ],
            scratch_shapes=[pltpu.VMEM((128, HALF), BF)] * 2,
        ),
        compiler_params=params(60),
        cost_estimate=cost(1),
        name="attend",
    )(at, q, *kv, ids)


def attend_back_kernel(at, q_a, q_b, kv_a, kv_b, do_in, o_a, o_b, lse_a, lse_b, ids, g_abs, g_a, g_b, q, kv, do, kt, dq, dkv):
    tile = pl.program_id(0)
    yh = at[0]

    @pl.when(tile == 0)
    def _():
        for ref, one, two in ((q, q_a, q_b), (kv, kv_a, kv_b)):
            ref[0:HALF, :] = one[...]
            ref[HALF:GROUP, :] = two[...]
        kt[...] = kv[...].T
        for half in range(2):
            start = ((half + yh) % 2) * HALF
            for s in range(8):
                packed = do_in[half * 8 + s]
                block = jnp.concatenate([packed[:, 0:64], packed[:, 64:128]], 0)
                block = jnp.concatenate([jnp.zeros_like(block), block], 1)
                do[pl.ds(pl.multiple_of(start + s * TOK, TOK), TOK), :] = block
        dkv[...] = jnp.zeros_like(dkv)

    near = tile < TILES // 2

    def run(whole_tile):
        first, length = image_range(at, ids[0])
        o_tile = jnp.where(near, o_a[...], o_b[...])
        lse = jnp.where(near, lse_a[0], lse_b[0])
        rows = pl.ds(pl.multiple_of(tile * TILE, TILE), TILE)
        queries = q[rows, :]
        grads = do[rows, :]
        delta = jnp.sum(o_tile * grads[:, 64:128].astype(F32).T, 0, keepdims=True)
        dq_tile = 0.0
        for half in range(2):
            here = slice(half * HALF, half * HALF + HALF)
            scores = dot(kv[here, :], queries, ((1,), (1,)))
            base = ((half + yh) % 2) * HALF
            probs = jnp.exp(masked(scores, base, first, length, whole_tile, NEGATIVE) - lse)
            probs_grad = dot(kv[here, :], grads, ((1,), (1,)))
            scores_grad = (probs * (probs_grad - delta)).astype(BF)
            dkv[here, :] += dot(scores_grad, queries) + dot(probs.astype(BF), grads)
            dq_tile = dq_tile + dot(kt[0:64, here], scores_grad)
        dq[rows, :] = (dq_tile.T * 0.125).astype(BF)

    place = jnp.where(near, tile, tile - TILES // 2)
    at_end = place == jnp.where((yh + jnp.where(near, 0, 1)) % 2 == 0, 0, TILES // 2 - 1)
    pl.when(at_end)(lambda: run(True))
    pl.when(jnp.logical_not(at_end))(lambda: run(False))

    @pl.when(tile == TILES - 1)
    def _():
        for ref, half in ((g_a, 0), (g_b, 1)):
            here = slice(half * HALF, half * HALF + HALF)
            ref[:, 0:64] = dq[here, :]
            ref[:, 64:192] = dkv[here, :].astype(BF)
            for s in range(8):
                block = ref[s * TOK : s * TOK + TOK, :]
                to = ((half + yh) % 2) * 8 + s
                g_abs[to, 0:TOK, :] = block[:, 0:128]
                g_abs[to, TOK : TOK + 80, :] = jnp.concatenate([block[0:80, 128:192], block[80:TOK, 128:192]], 1)


def attend_back(at, q, kv, do, o, lse, ids):
    pairs = whole(HALF, 128)
    last = TILES // 2 - 1
    one = lambda i: jnp.minimum(i, last)
    two = lambda i: jnp.maximum(i - last - 1, 0)
    wide = pltpu.VMEM((GROUP, 128), BF)
    return pl.pallas_call(
        attend_back_kernel,
        out_shape=(
            jax.ShapeDtypeStruct((HEADS, 240, 128), BF),
            jax.ShapeDtypeStruct((HALF, 192), BF),
            jax.ShapeDtypeStruct((HALF, 192), BF),
        ),
        grid_spec=pltpu.PrefetchScalarGridSpec(
            num_scalar_prefetch=1,
            grid=(TILES,),
            in_specs=[pairs] * 4
            + [whole(HEADS, TOK // 2, 128)]
            + [pl.BlockSpec((HEAD_DIM, TILE), lambda i, at, f=f: (0, f(i))) for f in (one, two)]
            + [pl.BlockSpec((1, 1, TILE), lambda i, at, f=f: (f(i), 0, 0)) for f in (one, two)]
            + [pl.BlockSpec((1, 1, TILE), lambda i, at: ((at[0] + i // (last + 1)) % 2, 0, i % (last + 1)))],
            out_specs=[whole(HEADS, 240, 128), whole(HALF, 192), whole(HALF, 192)],
            scratch_shapes=[
                wide,
                wide,
                wide,
                pltpu.VMEM((128, GROUP), BF),
                pltpu.VMEM((GROUP, HEAD_DIM), BF),
                pltpu.VMEM((GROUP, 128), F32),
            ],
        ),
        compiler_params=params(60),
        cost_estimate=cost(20),
        name="attend_back",
    )(at, *q, *kv, do, *o, *lse, ids)


def feed_kernel(at, *refs):
    blocks, refs = refs[:8], refs[8:]
    x, w_out, sv, rows, bias, dy, resid_out, att_out, y_out, dn2_other, dn2_own, w1_out, w2_out, b1_out = refs[:14]
    wide, w1, w2, b1, w1_grad, w2_grad = refs[14:]
    step = pl.program_id(0)
    z, core = at[1], at[2]
    own = step >= 1

    @pl.when(step == 0)
    def _():
        for j in range(16):
            w1[j * 64 : j * 64 + 32, :] = rows[j, 0:32, 0:512]
            w1[j * 64 + 32 : j * 64 + 64, :] = rows[j, 0:32, 512:1024]
            w2[j * 32 : j * 32 + 32, :] = rows[j, 32:64, :]
            b1[0:1, j * 32 : j * 32 + 32] = bias[j, 0:1, 0:32].astype(F32)
        b1_out[...] = jnp.zeros_like(b1_out)
        w1_grad[...] = jnp.zeros_like(w1_grad)
        w2_grad[...] = jnp.zeros_like(w2_grad)

    for k in range(4):
        mine, theirs = (block[:, 0].reshape(4 * TOK, 128) for block in (blocks[k], blocks[4 + k]))
        one = jnp.where(core == 0, mine, theirs)
        two = jnp.where(core == 0, theirs, mine)
        for h in range(2):
            lane = pl.multiple_of(h * 512 + ((z + k) % 4) * 128, 128)
            here = slice(h * 64, h * 64 + 64)
            wide[:, pl.ds(lane, 128)] = jnp.concatenate([one[:, here], two[:, here]], 1)
    resid = x[:, 0].reshape(4 * TOK, D).astype(F32) + dot(wide[...], w_out[...]) + sv[4:5, :].astype(F32)

    for k in range(4):

        @pl.when(jnp.logical_and(own, z == k))
        def _(k=k):
            resid_out[...] = resid[k * TOK : k * TOK + TOK]
            att_out[...] = wide[k * TOK : k * TOK + TOK, :]

    center = resid - jnp.mean(resid, -1, keepdims=True)
    spread = jnp.mean(center * center, -1, keepdims=True)
    normed = (center * lax.rsqrt(spread + EPSILON) * sv[5:6, :].astype(F32) + sv[6:7, :].astype(F32)).astype(BF)
    pre = dot(normed, w1[...]) + b1[0:1, :]
    cdf = 0.5 * (1.0 + lax.erf(pre * (0.5**0.5)))
    hidden = (pre * cdf).astype(BF)
    slope = cdf + pre * jnp.exp(-0.5 * pre * pre) * 0.3989422804014327
    dy_rows = dy[:, 0].reshape(4 * TOK, D)
    hidden_grad = dot(dy_rows, w2[...], ((1,), (1,)))
    pre_grad = (hidden_grad * slope).astype(BF)
    normed_grad = dot(pre_grad, w1[...], ((1,), (1,))).astype(BF).reshape(4, TOK, D)
    y_out[:, 0] = dot(hidden, w2[...]).astype(BF).reshape(4, TOK, D)
    w2_grad[...] += dot(hidden, dy_rows, ((0,), (0,)))
    w1_grad[...] += dot(normed, pre_grad, ((0,), (0,)))
    b1_out[...] += jnp.sum(pre_grad.astype(F32), 0, keepdims=True)

    @pl.when(own)
    def _():
        dn2_own[...] = normed_grad

    @pl.when(jnp.logical_not(own))
    def _():
        dn2_other[...] = normed_grad

    @pl.when(step == 1)
    def _():
        w1_out[...] = w1_grad[...].astype(BF).reshape(16, 64, 512)
        w2_out[...] = w2_grad[...].astype(BF).reshape(16, 32, D)


def feed(at, att_own, att_other, x, w_out, sv, rows, dy):
    core_of = lambda i, at: jnp.where(i >= 1, at[2], 1 - at[2])
    tok_spec = lambda width: pl.BlockSpec((4, 1, TOK, width), lambda i, at: (0, core_of(i, at), 0, 0))
    return pl.pallas_call(
        feed_kernel,
        out_shape=(
            jax.ShapeDtypeStruct((TOK, D), F32),
            jax.ShapeDtypeStruct((TOK, D), BF),
            jax.ShapeDtypeStruct((4, 2, TOK, D), BF),
            jax.ShapeDtypeStruct((4, TOK, D), BF),
            jax.ShapeDtypeStruct((4, TOK, D), BF),
            jax.ShapeDtypeStruct((16, 64, 512), BF),
            jax.ShapeDtypeStruct((16, 32, D), BF),
            jax.ShapeDtypeStruct((1, 512), F32),
        ),
        grid_spec=pltpu.PrefetchScalarGridSpec(
            num_scalar_prefetch=1,
            grid=(2,),
            in_specs=[tok_spec(128)] * 8
            + [
                tok_spec(D),
                whole(D, D),
                whole(8, D),
                whole(16, 64, D),
                pl.BlockSpec((16, 8, D), lambda i, at: (0, 8, 0)),
                tok_spec(D),
            ],
            out_specs=[
                whole(TOK, D),
                whole(TOK, D),
                tok_spec(D),
                whole(4, TOK, D),
                whole(4, TOK, D),
                whole(16, 64, 512),
                whole(16, 32, D),
                whole(1, 512),
            ],
            scratch_shapes=[
                pltpu.VMEM((4 * TOK, D), BF),
                pltpu.VMEM((D, 512), BF),
                pltpu.VMEM((512, D), BF),
                pltpu.VMEM((8, 512), F32),
                pltpu.VMEM((D, 512), F32),
                pltpu.VMEM((512, D), F32),
            ],
        ),
        compiler_params=params(56),
        cost_estimate=cost(20),
        name="out_feed",
    )(at, *att_own, *att_other, x, w_out, sv, rows, rows, dy)


def mix_kernel(at, own, came, *outs):
    for k in range(4):
        here = pl.ds((at[1] + k) % 4, 1)
        outs[k][...] = (own[here][0].astype(F32) + came[here][0].astype(F32)).astype(BF)


def mix(at, own, came):
    return pl.pallas_call(
        mix_kernel,
        out_shape=[jax.ShapeDtypeStruct((TOK, D), BF)] * 4,
        grid_spec=pltpu.PrefetchScalarGridSpec(
            num_scalar_prefetch=1,
            grid=(1,),
            in_specs=[whole(4, TOK, D)] * 2,
            out_specs=[whole(TOK, D)] * 4,
        ),
        compiler_params=params(60),
        cost_estimate=cost(2),
        name="mix",
    )(at, own, came)


def norm_back(values, gain, grad):
    center = values - jnp.mean(values, -1, keepdims=True)
    spread = jnp.mean(center * center, -1, keepdims=True)
    r = lax.rsqrt(spread + EPSILON)
    n = center * r
    e = grad * gain
    inner = r * (e - jnp.mean(e, -1, keepdims=True) - n * jnp.mean(e * n, -1, keepdims=True))
    return inner, jnp.sum(grad * n, 0, keepdims=True), jnp.sum(grad, 0, keepdims=True)


def middle_kernel(m0, m1, m2, m3, resid, dy, sv, w_out, resid_grad_out, branch_out, att_grad_out, sums):
    grad = m0[...].astype(F32) + m1[...].astype(F32) + m2[...].astype(F32) + m3[...].astype(F32)
    dy_f = dy[...].astype(F32)
    part, gain_grad, shift_grad = norm_back(resid[...], sv[5:6, :].astype(F32), grad)
    resid_grad = dy_f + part
    resid_grad_out[...] = resid_grad
    branch = resid_grad.astype(BF)
    branch_out[...] = branch
    sums[0:1, :] = jnp.sum(branch.astype(F32), 0, keepdims=True)
    sums[1:2, :] = gain_grad
    sums[2:3, :] = shift_grad
    sums[3:4, :] = jnp.sum(dy_f, 0, keepdims=True)
    att_grad = dot(branch, w_out[...], ((1,), (1,))).astype(BF)
    for h in range(HEADS):
        lane = h * 64
        att_grad_out[h] = jnp.concatenate(
            [att_grad[0:80, lane : lane + 64], att_grad[80:160, lane : lane + 64]], 1
        )


def middle(parts, resid, dy, sv, w_out):
    return pl.pallas_call(
        middle_kernel,
        out_shape=(
            jax.ShapeDtypeStruct((TOK, D), F32),
            jax.ShapeDtypeStruct((TOK, D), BF),
            jax.ShapeDtypeStruct((HEADS, TOK // 2, 128), BF),
            jax.ShapeDtypeStruct((4, D), F32),
        ),
        grid=(1,),
        in_specs=[whole(TOK, D)] * 6 + [whole(8, D), whole(D, D)],
        out_specs=[whole(TOK, D), whole(TOK, D), whole(HEADS, TOK // 2, 128), whole(4, D)],
        compiler_params=params(16),
        cost_estimate=cost(5),
        name="middle",
    )(*parts, resid, dy, sv, w_out)


def last_kernel(g_a, g_b, w, x, resid_grad, sv, out, sums, biases, total):
    step = pl.program_id(0)

    @pl.when(step == 0)
    def _():
        total[...] = jnp.zeros_like(total)

    for k in range(4):
        pair = []
        for packed in (g_a[k], g_b[k]):
            values = jnp.concatenate([packed[160:240, 0:64], packed[160:240, 64:128]], 0)
            pair += [packed[0:160, :], values]
        pair = jnp.concatenate(pair, 1)
        total[...] += dot(pair, w[k], ((1,), (1,)))
        biases[k] = jnp.sum(pair.astype(F32), 0, keepdims=True)

    @pl.when(step == 1)
    def _():
        part, gain_grad, shift_grad = norm_back(x[...].astype(F32), sv[0:1, :].astype(F32), total[...])
        out[...] = (resid_grad[...] + part).astype(BF)
        sums[0:1, :] = gain_grad
        sums[1:2, :] = shift_grad


def last(g, w, x, resid_grad, sv):
    return pl.pallas_call(
        last_kernel,
        out_shape=(
            jax.ShapeDtypeStruct((TOK, D), BF),
            jax.ShapeDtypeStruct((2, D), F32),
            jax.ShapeDtypeStruct((8, 1, 384), F32),
        ),
        grid=(2,),
        in_specs=[
            pl.BlockSpec((4, 240, 128), lambda i: (i, 0, 0)),
            pl.BlockSpec((4, 240, 128), lambda i: (i + 2, 0, 0)),
            pl.BlockSpec((4, D, 384), lambda i: (i, 0, 0)),
            whole(TOK, D),
            whole(TOK, D),
            whole(8, D),
        ],
        out_specs=[whole(TOK, D), whole(2, D), pl.BlockSpec((4, 1, 384), lambda i: (i, 0, 0))],
        scratch_shapes=[pltpu.VMEM((TOK, D), F32)],
        compiler_params=params(48),
        cost_estimate=cost(15),
        name="last",
    )(g, g, w, x, resid_grad, sv)


def body(
    inputs,
    image_ids,
    ln1_gain,
    ln1_shift,
    qkv_weight,
    query_bias,
    value_bias,
    out_weight,
    out_bias,
    ln2_gain,
    ln2_shift,
    fc1_weight,
    fc1_bias,
    fc2_weight,
    fc2_bias,
    out_grad,
):
    xi, yl, yh, zi, ci = (lax.axis_index(name) for name in ALL)
    zc = zi * 2 + ci
    where_at = jnp.arange(16)
    starts = jnp.sum((image_ids[:, None] < where_at[None, :] - 4).astype(jnp.int32), 0)
    at = jnp.where(where_at == 0, yh, jnp.where(where_at == 1, zi, jnp.where(where_at == 2, ci, yh * 8 + zc)))
    at = jnp.where(where_at < 4, at, starts).astype(jnp.int32)

    near = lax.all_gather(inputs, TP, axis=0, tiled=True).reshape(4, 2, TOK, D)
    crossed = along(inputs, "yh", 1)

    qkv = qkv_weight.reshape(8, 3, 2, 8, HEAD_DIM).transpose(3, 0, 2, 1, 4).reshape(8, 8, 384)
    small = jnp.stack(
        [ln1_gain, ln1_shift, query_bias, value_bias, out_bias, ln2_gain, ln2_shift, fc2_bias], 1
    )
    small = jnp.broadcast_to(jnp.pad(small, ((0, 0), (0, 120)))[None], (8, 8, 128))
    fc1 = fc1_weight.reshape(8, 16, 8, 32).transpose(2, 0, 1, 3).reshape(8, 8, 512)
    columns = exchange(jnp.concatenate([qkv, small, fc1], 2), TP)
    far = lax.all_gather(after(crossed, columns), TP, axis=0, tiled=True).reshape(4, 2, TOK, D)
    dy_all = lax.all_gather(after(out_grad, crossed, columns), TP, axis=0, tiled=True).reshape(4, 2, TOK, D)
    columns = columns.reshape(64, D)

    fc1 = jnp.concatenate([columns[0:32, 512:], columns[32:64, 512:]], 1)
    columns = jnp.concatenate([columns[0:32, 0:512], columns[32:64, 0:512]], 1)
    spread = lambda v: exchange(jnp.broadcast_to(v[None], (16, *v.shape)), XY)
    first = spread(jnp.concatenate([columns, out_weight], 0))
    bias = jnp.pad(fc1_bias[None], ((0, 7), (0, D - 32)))
    rows = spread(after(jnp.concatenate([fc1, fc2_weight, bias], 0), first))
    sv = jnp.concatenate([first[:, 0:32, 384:392], first[:, 0:32, 896:904]], 1).reshape(D, 8).T
    w_out = lax.all_gather(first[:, 32:40], TP, axis=1, tiled=True).reshape(D, D)

    ids = image_ids.reshape(2, 1, HALF)
    n1_near, n1_far, q_near, kv_near, q_far, kv_far, heads, att_far, o_far, lse_far = project(
        at, near, far, first, sv, ids
    )
    q, kv = (q_near, q_far), (kv_near, kv_far)
    theirs = along(att_far, "yh", 1)
    att_near, o_near, lse_near = attend(at, 0, after(q[0], att_far), kv, ids)
    att_two = jnp.where(
        yh == 0, jnp.concatenate([att_near, theirs], 1), jnp.concatenate([theirs, att_near], 1)
    )
    att_two = after(att_two, rows)
    att_own = [att_two] + [from_up(att_two, k) for k in (1, 2, 3)]
    att_other = [along(block, "c", 1) for block in att_own]
    w_qkv = lax.all_gather(after(heads, *att_other), TP, axis=0, tiled=False)
    split = lambda blocks: [block.reshape(4, 2, TOK, 128) for block in blocks]
    resid, att_tok, y_part, dn2_other, dn2_own, fc1_grad, fc2_grad, b1_grad = feed(
        at, split(att_own), split(att_other), near, w_out, sv, rows, dy_all
    )

    mixed = mix(at, dn2_own, along(dn2_other, "c", 1))
    parts = [mixed[0]] + [along(mixed[k], "z", k) for k in (1, 2, 3)]
    fc2_grad = exchange(fc2_grad, XY)
    parts = [after(parts[0], fc2_grad)] + parts[1:]
    resid_grad, branch_grad, att_grad, mid_sums = middle(parts, resid, out_grad, sv, w_out)
    do = exchange(after(att_grad, w_qkv), SEQ)
    turn = ((0,), (0,))

    g, g_near, g_far = attend_back(
        at, q, kv, do, (o_near, o_far), (lse_near, lse_far), ids
    )

    out_w = dot(att_tok, branch_grad, turn).astype(BF)
    out_w = lax.psum_scatter(after(out_w, do), TP, scatter_dimension=0, tiled=True)

    fc1_grad = exchange(after(fc1_grad, do), XY)
    g_tok = exchange(after(g, fc1_grad), SEQ)
    fc2_grad = jnp.sum(fc2_grad.astype(F32), 0)
    fc1_grad = jnp.sum(fc1_grad.astype(F32), 0).reshape(8, 8, 512)
    fc1_grad = exchange(after(fc1_grad, g_tok), TP)
    fc1_grad = fc1_grad.reshape(8, 8, 16, 32).transpose(1, 2, 0, 3).reshape(8, FF)

    summed = lax.psum_scatter(after(y_part, *parts).reshape(HALF, D), TP, scatter_dimension=0, tiled=True)
    outputs = resid + summed.astype(F32) + sv[7].astype(F32)

    qkv_grad = dot(n1_near.reshape(HALF, D), g_near, turn) + dot(n1_far.reshape(HALF, D), g_far, turn)
    qkv_grad = qkv_grad.astype(BF)
    pick = lambda v, axis, place: lax.dynamic_index_in_dim(v, place, axis, keepdims=False)
    out_w = after(out_w, qkv_grad).reshape(4, 2, 2, 8, D)
    total = pick(out_w, 0, xi).astype(F32)
    for k in (1, 2, 3):
        total = total + along(pick(out_w, 0, (xi + k) % 4), "x", k).astype(F32)
    out_w = total.astype(BF)
    g_tok = after(g_tok, out_w)
    input_grad, norm_sums, biases = last(g_tok, w_qkv, inputs, resid_grad, sv)
    biases = biases.reshape(8, 2, 3, HEAD_DIM).transpose(2, 1, 0, 3).reshape(3, D)
    vectors = jnp.concatenate([norm_sums, biases[0:1], biases[2:3], mid_sums])
    vectors = vectors.reshape(8, 128, 8).transpose(1, 0, 2)
    mine = jnp.arange(8)[None, :, None] == zc
    b1_part = jnp.where(mine, b1_grad.reshape(16, 1, 32), 0.0).reshape(128, 4, 8)
    b1_part = jnp.pad(b1_part, ((0, 0), (0, 4), (0, 0)))
    vectors = jnp.concatenate([vectors, b1_part], 2)
    high = vectors.astype(BF)
    low = (vectors - high.astype(F32)).astype(BF)

    final = jnp.concatenate([qkv_grad.reshape(128, 8, 192), high, low], 2)
    final = after(final, out_w)
    out_w = after(out_w, norm_sums)
    by_y = lambda y: pick(pick(out_w, 0, y % 2), 0, y // 2)
    yi = yh * 2 + yl
    total = by_y(yi).astype(F32)
    for k in (1, 2, 3):
        total = total + along_y(by_y((yi + k) % 4), k).astype(F32)
    out_w = lax.ppermute(total, ALL, [(j * 8 + s, (2 * s + j // 8) * 8 + j % 8) for j in range(16) for s in range(8)])
    final = exchange(final, ALL).astype(F32)
    qkv_grad = jnp.sum(final[:, :, 0:192].reshape(8, HEADS, 8, 192), 0)
    qkv_grad = qkv_grad.reshape(HEADS, 8, 3, HEAD_DIM).transpose(1, 2, 0, 3).reshape(8, 3 * D)
    vectors = jnp.sum(final[:, :, 192:208] + final[:, :, 208:224], 0)
    fc1_bias_grad = vectors[0:4, 8:16].reshape(32)
    vectors = vectors[:, 0:8]
    return (
        outputs.astype(BF),
        input_grad,
        vectors[0],
        vectors[1],
        qkv_grad,
        vectors[2],
        vectors[3],
        out_w,
        vectors[4],
        vectors[5],
        vectors[6],
        fc1_grad,
        fc1_bias_grad,
        fc2_grad,
        vectors[7],
    )


def solution(mesh):
    fine = Mesh(mesh.devices.reshape(4, 2, 2, 4, 2), ALL)
    rows = P(ALL, None)
    vec = P(ALL)
    return jax.shard_map(
        body,
        mesh=fine,
        in_specs=(rows, P(("x", "yl")), vec, vec, rows, vec, vec, rows, vec, vec, vec, rows, vec, rows, vec, rows),
        out_specs=(rows, rows, vec, vec, rows, vec, vec, rows, vec, vec, vec, rows, vec, rows, vec),
        check_vma=False,
    )
```

```python
import functools

import jax
import jax.numpy as jnp
from jax import lax
from jax.experimental import pallas as pl
from jax.experimental.pallas import tpu as pltpu
from jax.sharding import Mesh
from jax.sharding import PartitionSpec as P

HEADS = 16
HEAD_DIM = 64
D = 1024
FF = 4096
TOK = 160
GROUP = 2560
HALF = 1280
EPSILON = 1e-06
NEGATIVE = -1e30
TILE = 256
TILES = GROUP // TILE
ALL = ("x", "yl", "yh", "z", "c")
TP = ("z", "c")
XY = ("x", "yl", "yh")
SEQ = ("yh", "z", "c")
BF = jnp.bfloat16
F32 = jnp.float32


def dot(left, right, dims=((1,), (0,))):
    return lax.dot_general(left, right, (dims, ((), ())), preferred_element_type=F32)


def params(mebibytes):
    return pltpu.CompilerParams(vmem_limit_bytes=mebibytes * 1024 * 1024)


def cost(micros):
    return pl.CostEstimate(flops=int(micros * 1e9), bytes_accessed=1 << 20, transcendentals=0)


def whole(*shape):
    return pl.BlockSpec(shape, lambda *_: (0,) * len(shape))


def along(value, axis, by):
    size = 4 if axis in ("x", "z") else 2
    return lax.ppermute(value, axis, [(i, (i + by) % size) for i in range(size)])


def along_y(value, by):
    pairs = []
    for yl in range(2):
        for yh in range(2):
            to = (yh * 2 + yl + by) % 4
            pairs.append((yl * 2 + yh, (to % 2) * 2 + to // 2))
    return lax.ppermute(value, ("yl", "yh"), pairs)


def from_up(value, k):
    return along(value, "z", 4 - k)


def after(value, *done):
    return lax.optimization_barrier((value, *done))[0]


def exchange(value, axes):
    return lax.all_to_all(value, axes, split_axis=0, concat_axis=0, tiled=True)


def project_rows(raw, sv, wh, bias):
    rows = raw.astype(F32)
    center = rows - jnp.mean(rows, -1, keepdims=True)
    spread = jnp.mean(center * center, -1, keepdims=True)
    gain = sv[0:1, :].astype(F32)
    shift = sv[1:2, :].astype(F32)
    normed = (center * lax.rsqrt(spread + EPSILON) * gain + shift).astype(BF)
    mixed = dot(normed, wh[...])
    queries = (mixed[:, 0:64] + bias[0:1, :]).astype(BF) * jnp.asarray(0.125, BF)
    keys = mixed[:, 64:128].astype(BF)
    values = (mixed[:, 128:192] + bias[8:9, :]).astype(BF)
    return normed, jnp.concatenate([queries, jnp.zeros_like(queries)], 1), jnp.concatenate([keys, values], 1)


def choose_head(at, w, sv, heads, wh, bias):
    @pl.when(pl.program_id(0) == 0)
    def _():
        for j in range(16):
            for part in range(2):
                lane = part * 512
                rows = jnp.where(at[0] == 0, w[j, :, lane : lane + 192], w[j, :, lane + 192 : lane + 384])
                wh[j * 64 + part * 32 : j * 64 + part * 32 + 32, :] = rows
                heads[j * 64 + part * 32 : j * 64 + part * 32 + 32, :] = w[j, :, lane : lane + 384]
        for row, place in ((2, 0), (3, 8)):
            value = sv[row : row + 1, 0:64]
            for h in range(1, HEADS):
                value = jnp.where(at[3] == h, sv[row : row + 1, h * 64 : h * 64 + 64], value)
            bias[place : place + 1, :] = value.astype(F32)


def image_range(at, ids):
    first = jnp.zeros_like(ids)
    length = jnp.zeros_like(ids)
    for m in range(4):
        first = jnp.where(ids == m, at[4 + m], first)
        length = jnp.where(ids == m, at[5 + m] - at[4 + m], length)
    return first, length


def masked(values, base, first, length, fill):
    place = lax.broadcasted_iota(jnp.int32, values.shape, 0) - (first - base)
    return jnp.where(jnp.logical_and(place >= 0, place < length), values, fill)


def attend_tile(at, queries, kv, vt, ids, att, o_out, lse_out):
    first, length = image_range(at, ids[0])
    scores = []
    for key_half, keys in enumerate(kv):
        raw = dot(keys[...], queries, ((1,), (1,)))
        base = ((key_half + at[0]) % 2) * HALF
        scores.append(masked(raw, base, first, length, NEGATIVE))
    top = jnp.maximum(jnp.max(scores[0], 0, keepdims=True), jnp.max(scores[1], 0, keepdims=True))
    total = 0.0
    out = 0.0
    for part, values in zip(scores, vt, strict=True):
        part = jnp.exp(part - top)
        total = total + jnp.sum(part, 0, keepdims=True)
        out = out + dot(values[64:128, :], part.astype(BF))
    out = out / total
    o_out[...] = out
    att[...] = out.T.astype(BF)
    lse_out[0] = top + jnp.log(total)


def project_kernel(at, x_a, x_b, w, sv, ids, n1_a, n1_b, q_a, kv_a, q_b, kv_b, heads, att, o_out, lse_out, wh, bias, vt_a, vt_b):
    step = pl.program_id(0)
    choose_head(at, w, sv, heads, wh, bias)

    @pl.when(step < 4)
    def _():
        raw = jnp.where(step < 2, x_a[...], x_b[...]).reshape(4 * TOK, D)
        normed, queries, pairs = project_rows(raw, sv, wh, bias)
        rows = pl.ds(pl.multiple_of((step % 2) * 4 * TOK, 4 * TOK), 4 * TOK)

        def put(n1, q_out, kv_out):
            n1[...] = normed.reshape(2, 2, TOK, D)
            q_out[rows, :] = queries
            kv_out[rows, :] = pairs

        pl.when(step < 2)(lambda: put(n1_a, q_a, kv_a))
        pl.when(step >= 2)(lambda: put(n1_b, q_b, kv_b))

    @pl.when(step == 4)
    def _():
        vt_a[...] = kv_a[...].T
        vt_b[...] = kv_b[...].T

    @pl.when(step >= 4)
    def _():
        tile = step - 4
        queries = q_b[pl.ds(pl.multiple_of(tile * TILE, TILE), TILE), :]
        attend_tile(at, queries, (kv_a, kv_b), (vt_a, vt_b), ids, att, o_out, lse_out)


def project(at, near, far, rows, sv, ids):
    tiles = HALF // TILE
    one = lambda i, at: (jnp.minimum(i, 1), 0, 0, 0)
    two = lambda i, at: (jnp.clip(i - 2, 0, 1), 0, 0, 0)
    late = lambda i: jnp.maximum(i - 4, 0)
    block = lambda index: pl.BlockSpec((2, 2, TOK, D), index)
    tokens = jax.ShapeDtypeStruct((4, 2, TOK, D), BF)
    pairs = jax.ShapeDtypeStruct((HALF, 128), BF)
    return pl.pallas_call(
        project_kernel,
        out_shape=[tokens] * 2
        + [pairs] * 4
        + [
            jax.ShapeDtypeStruct((D, 384), BF),
            jax.ShapeDtypeStruct((HALF, HEAD_DIM), BF),
            jax.ShapeDtypeStruct((HEAD_DIM, HALF), F32),
            jax.ShapeDtypeStruct((tiles, 1, TILE), F32),
        ],
        grid_spec=pltpu.PrefetchScalarGridSpec(
            num_scalar_prefetch=1,
            grid=(4 + tiles,),
            in_specs=[
                block(one),
                block(two),
                whole(16, 32, D),
                whole(8, D),
                pl.BlockSpec((1, 1, TILE), lambda i, at: (1 - at[0], 0, late(i))),
            ],
            out_specs=[block(one), block(two)]
            + [whole(HALF, 128)] * 4
            + [
                whole(D, 384),
                pl.BlockSpec((TILE, HEAD_DIM), lambda i, at: (late(i), 0)),
                pl.BlockSpec((HEAD_DIM, TILE), lambda i, at: (0, late(i))),
                pl.BlockSpec((1, 1, TILE), lambda i, at: (late(i), 0, 0)),
            ],
            scratch_shapes=[pltpu.VMEM((D, 192), BF), pltpu.VMEM((16, HEAD_DIM), F32)] + [pltpu.VMEM((128, HALF), BF)] * 2,
        ),
        compiler_params=params(60),
        cost_estimate=cost(1),
        name="project_attend",
    )(at, near, far, rows, sv, ids)


def attend_kernel(at, q, kv_a, kv_b, ids, att, o_out, lse_out, vt_a, vt_b):
    @pl.when(pl.program_id(0) == 0)
    def _():
        vt_a[...] = kv_a[...].T
        vt_b[...] = kv_b[...].T

    attend_tile(at, q[...], (kv_a, kv_b), (vt_a, vt_b), ids, att, o_out, lse_out)


def attend(at, half, q, kv, ids):
    tiles = HALF // TILE
    pairs = whole(HALF, 128)
    return pl.pallas_call(
        attend_kernel,
        out_shape=(
            jax.ShapeDtypeStruct((HALF, HEAD_DIM), BF),
            jax.ShapeDtypeStruct((HEAD_DIM, HALF), F32),
            jax.ShapeDtypeStruct((tiles, 1, TILE), F32),
        ),
        grid_spec=pltpu.PrefetchScalarGridSpec(
            num_scalar_prefetch=1,
            grid=(tiles,),
            in_specs=[
                pl.BlockSpec((TILE, 128), lambda i, at: (i, 0)),
                pairs,
                pairs,
                pl.BlockSpec((1, 1, TILE), lambda i, at: ((at[0] + half) % 2, 0, i)),
            ],
            out_specs=[
                pl.BlockSpec((TILE, HEAD_DIM), lambda i, at: (i, 0)),
                pl.BlockSpec((HEAD_DIM, TILE), lambda i, at: (0, i)),
                pl.BlockSpec((1, 1, TILE), lambda i, at: (i, 0, 0)),
            ],
            scratch_shapes=[pltpu.VMEM((128, HALF), BF)] * 2,
        ),
        compiler_params=params(60),
        cost_estimate=cost(1),
        name="attend",
    )(at, q, *kv, ids)


def attend_back_kernel(at, q_a, q_b, kv_a, kv_b, do_in, o_a, o_b, lse_a, lse_b, ids, g_abs, g_a, g_b, q, kv, do, kt, dq, dkv):
    tile = pl.program_id(0)
    yh = at[0]

    @pl.when(tile == 0)
    def _():
        for ref, one, two in ((q, q_a, q_b), (kv, kv_a, kv_b)):
            ref[0:HALF, :] = one[...]
            ref[HALF:GROUP, :] = two[...]
        kt[...] = kv[...].T
        for half in range(2):
            start = ((half + yh) % 2) * HALF
            for s in range(8):
                packed = do_in[half * 8 + s]
                block = jnp.concatenate([packed[:, 0:64], packed[:, 64:128]], 0)
                block = jnp.concatenate([jnp.zeros_like(block), block], 1)
                do[pl.ds(pl.multiple_of(start + s * TOK, TOK), TOK), :] = block
        dkv[...] = jnp.zeros_like(dkv)

    near = tile < TILES // 2

    first, length = image_range(at, ids[0])
    o_tile = jnp.where(near, o_a[...], o_b[...])
    lse = jnp.where(near, lse_a[0], lse_b[0])
    rows = pl.ds(pl.multiple_of(tile * TILE, TILE), TILE)
    queries = q[rows, :]
    grads = do[rows, :]
    delta = jnp.sum(o_tile * grads[:, 64:128].astype(F32).T, 0, keepdims=True)
    dq_tile = 0.0
    for half in range(2):
        here = slice(half * HALF, half * HALF + HALF)
        scores = dot(kv[here, :], queries, ((1,), (1,)))
        base = ((half + yh) % 2) * HALF
        probs = jnp.exp(masked(scores, base, first, length, NEGATIVE) - lse)
        probs_grad = dot(kv[here, :], grads, ((1,), (1,)))
        scores_grad = (probs * (probs_grad - delta)).astype(BF)
        dkv[here, :] += dot(scores_grad, queries) + dot(probs.astype(BF), grads)
        dq_tile = dq_tile + dot(kt[0:64, here], scores_grad)
    dq[rows, :] = (dq_tile.T * 0.125).astype(BF)

    @pl.when(tile == TILES - 1)
    def _():
        for ref, half in ((g_a, 0), (g_b, 1)):
            here = slice(half * HALF, half * HALF + HALF)
            ref[:, 0:64] = dq[here, :]
            ref[:, 64:192] = dkv[here, :].astype(BF)
            for s in range(8):
                block = ref[s * TOK : s * TOK + TOK, :]
                to = ((half + yh) % 2) * 8 + s
                g_abs[to, 0:TOK, :] = block[:, 0:128]
                g_abs[to, TOK : TOK + 80, :] = jnp.concatenate([block[0:80, 128:192], block[80:TOK, 128:192]], 1)


def attend_back(at, q, kv, do, o, lse, ids):
    pairs = whole(HALF, 128)
    last = TILES // 2 - 1
    one = lambda i: jnp.minimum(i, last)
    two = lambda i: jnp.maximum(i - last - 1, 0)
    wide = pltpu.VMEM((GROUP, 128), BF)
    return pl.pallas_call(
        attend_back_kernel,
        out_shape=(
            jax.ShapeDtypeStruct((HEADS, 240, 128), BF),
            jax.ShapeDtypeStruct((HALF, 192), BF),
            jax.ShapeDtypeStruct((HALF, 192), BF),
        ),
        grid_spec=pltpu.PrefetchScalarGridSpec(
            num_scalar_prefetch=1,
            grid=(TILES,),
            in_specs=[pairs] * 4
            + [whole(HEADS, TOK // 2, 128)]
            + [pl.BlockSpec((HEAD_DIM, TILE), lambda i, at, f=f: (0, f(i))) for f in (one, two)]
            + [pl.BlockSpec((1, 1, TILE), lambda i, at, f=f: (f(i), 0, 0)) for f in (one, two)]
            + [pl.BlockSpec((1, 1, TILE), lambda i, at: ((at[0] + i // (last + 1)) % 2, 0, i % (last + 1)))],
            out_specs=[whole(HEADS, 240, 128), whole(HALF, 192), whole(HALF, 192)],
            scratch_shapes=[
                wide,
                wide,
                wide,
                pltpu.VMEM((128, GROUP), BF),
                pltpu.VMEM((GROUP, HEAD_DIM), BF),
                pltpu.VMEM((GROUP, 128), F32),
            ],
        ),
        compiler_params=params(60),
        cost_estimate=cost(20),
        name="attend_back",
    )(at, *q, *kv, do, *o, *lse, ids)


def feed_kernel(at, *refs):
    blocks, refs = refs[:8], refs[8:]
    x, w_out, sv, rows, bias, dy, resid_out, att_out, y_out, dn2_other, dn2_own, w1_out, w2_out, b1_out = refs[:14]
    wide, w1, w2, b1, w1_grad, w2_grad = refs[14:]
    step = pl.program_id(0)
    z, core = at[1], at[2]
    own = step >= 1

    @pl.when(step == 0)
    def _():
        for j in range(16):
            w1[j * 64 : j * 64 + 32, :] = rows[j, 0:32, 0:512]
            w1[j * 64 + 32 : j * 64 + 64, :] = rows[j, 0:32, 512:1024]
            w2[j * 32 : j * 32 + 32, :] = rows[j, 32:64, :]
            b1[0:1, j * 32 : j * 32 + 32] = bias[j, 0:1, 0:32].astype(F32)
        b1_out[...] = jnp.zeros_like(b1_out)
        w1_grad[...] = jnp.zeros_like(w1_grad)
        w2_grad[...] = jnp.zeros_like(w2_grad)

    for k in range(4):
        mine, theirs = (block[:, 0].reshape(4 * TOK, 128) for block in (blocks[k], blocks[4 + k]))
        one = jnp.where(core == 0, mine, theirs)
        two = jnp.where(core == 0, theirs, mine)
        for h in range(2):
            lane = pl.multiple_of(h * 512 + ((z + k) % 4) * 128, 128)
            here = slice(h * 64, h * 64 + 64)
            wide[:, pl.ds(lane, 128)] = jnp.concatenate([one[:, here], two[:, here]], 1)
    resid = x[:, 0].reshape(4 * TOK, D).astype(F32) + dot(wide[...], w_out[...]) + sv[4:5, :].astype(F32)

    for k in range(4):

        @pl.when(jnp.logical_and(own, z == k))
        def _(k=k):
            resid_out[...] = resid[k * TOK : k * TOK + TOK]
            att_out[...] = wide[k * TOK : k * TOK + TOK, :]

    center = resid - jnp.mean(resid, -1, keepdims=True)
    spread = jnp.mean(center * center, -1, keepdims=True)
    normed = (center * lax.rsqrt(spread + EPSILON) * sv[5:6, :].astype(F32) + sv[6:7, :].astype(F32)).astype(BF)
    pre = dot(normed, w1[...]) + b1[0:1, :]
    cdf = 0.5 * (1.0 + lax.erf(pre * (0.5**0.5)))
    hidden = (pre * cdf).astype(BF)
    slope = cdf + pre * jnp.exp(-0.5 * pre * pre) * 0.3989422804014327
    dy_rows = dy[:, 0].reshape(4 * TOK, D)
    hidden_grad = dot(dy_rows, w2[...], ((1,), (1,)))
    pre_grad = (hidden_grad * slope).astype(BF)
    normed_grad = dot(pre_grad, w1[...], ((1,), (1,))).astype(BF).reshape(4, TOK, D)
    y_out[:, 0] = dot(hidden, w2[...]).astype(BF).reshape(4, TOK, D)
    w2_grad[...] += dot(hidden, dy_rows, ((0,), (0,)))
    w1_grad[...] += dot(normed, pre_grad, ((0,), (0,)))
    b1_out[...] += jnp.sum(pre_grad.astype(F32), 0, keepdims=True)

    @pl.when(own)
    def _():
        dn2_own[...] = normed_grad

    @pl.when(jnp.logical_not(own))
    def _():
        dn2_other[...] = normed_grad

    @pl.when(step == 1)
    def _():
        w1_out[...] = w1_grad[...].astype(BF).reshape(16, 64, 512)
        w2_out[...] = w2_grad[...].astype(BF).reshape(16, 32, D)


def feed(at, att_own, att_other, x, w_out, sv, rows, dy):
    core_of = lambda i, at: jnp.where(i >= 1, at[2], 1 - at[2])
    tok_spec = lambda width: pl.BlockSpec((4, 1, TOK, width), lambda i, at: (0, core_of(i, at), 0, 0))
    return pl.pallas_call(
        feed_kernel,
        out_shape=(
            jax.ShapeDtypeStruct((TOK, D), F32),
            jax.ShapeDtypeStruct((TOK, D), BF),
            jax.ShapeDtypeStruct((4, 2, TOK, D), BF),
            jax.ShapeDtypeStruct((4, TOK, D), BF),
            jax.ShapeDtypeStruct((4, TOK, D), BF),
            jax.ShapeDtypeStruct((16, 64, 512), BF),
            jax.ShapeDtypeStruct((16, 32, D), BF),
            jax.ShapeDtypeStruct((1, 512), F32),
        ),
        grid_spec=pltpu.PrefetchScalarGridSpec(
            num_scalar_prefetch=1,
            grid=(2,),
            in_specs=[tok_spec(128)] * 8
            + [
                tok_spec(D),
                whole(D, D),
                whole(8, D),
                whole(16, 64, D),
                pl.BlockSpec((16, 8, D), lambda i, at: (0, 8, 0)),
                tok_spec(D),
            ],
            out_specs=[
                whole(TOK, D),
                whole(TOK, D),
                tok_spec(D),
                whole(4, TOK, D),
                whole(4, TOK, D),
                whole(16, 64, 512),
                whole(16, 32, D),
                whole(1, 512),
            ],
            scratch_shapes=[
                pltpu.VMEM((4 * TOK, D), BF),
                pltpu.VMEM((D, 512), BF),
                pltpu.VMEM((512, D), BF),
                pltpu.VMEM((8, 512), F32),
                pltpu.VMEM((D, 512), F32),
                pltpu.VMEM((512, D), F32),
            ],
        ),
        compiler_params=params(56),
        cost_estimate=cost(20),
        name="out_feed",
    )(at, *att_own, *att_other, x, w_out, sv, rows, rows, dy)


def mix_kernel(at, own, came, *outs):
    for k in range(4):
        here = pl.ds((at[1] + k) % 4, 1)
        outs[k][...] = (own[here][0].astype(F32) + came[here][0].astype(F32)).astype(BF)


def mix(at, own, came):
    return pl.pallas_call(
        mix_kernel,
        out_shape=[jax.ShapeDtypeStruct((TOK, D), BF)] * 4,
        grid_spec=pltpu.PrefetchScalarGridSpec(
            num_scalar_prefetch=1,
            grid=(1,),
            in_specs=[whole(4, TOK, D)] * 2,
            out_specs=[whole(TOK, D)] * 4,
        ),
        compiler_params=params(60),
        cost_estimate=cost(2),
        name="mix",
    )(at, own, came)


def norm_back(values, gain, grad):
    center = values - jnp.mean(values, -1, keepdims=True)
    spread = jnp.mean(center * center, -1, keepdims=True)
    r = lax.rsqrt(spread + EPSILON)
    n = center * r
    e = grad * gain
    inner = r * (e - jnp.mean(e, -1, keepdims=True) - n * jnp.mean(e * n, -1, keepdims=True))
    return inner, jnp.sum(grad * n, 0, keepdims=True), jnp.sum(grad, 0, keepdims=True)


def middle_kernel(m0, m1, m2, m3, resid, dy, sv, w_out, resid_grad_out, branch_out, att_grad_out, sums):
    grad = m0[...].astype(F32) + m1[...].astype(F32) + m2[...].astype(F32) + m3[...].astype(F32)
    dy_f = dy[...].astype(F32)
    part, gain_grad, shift_grad = norm_back(resid[...], sv[5:6, :].astype(F32), grad)
    resid_grad = dy_f + part
    resid_grad_out[...] = resid_grad
    branch = resid_grad.astype(BF)
    branch_out[...] = branch
    sums[0:1, :] = jnp.sum(branch.astype(F32), 0, keepdims=True)
    sums[1:2, :] = gain_grad
    sums[2:3, :] = shift_grad
    sums[3:4, :] = jnp.sum(dy_f, 0, keepdims=True)
    att_grad = dot(branch, w_out[...], ((1,), (1,))).astype(BF)
    for h in range(HEADS):
        lane = h * 64
        att_grad_out[h] = jnp.concatenate(
            [att_grad[0:80, lane : lane + 64], att_grad[80:160, lane : lane + 64]], 1
        )


def middle(parts, resid, dy, sv, w_out):
    return pl.pallas_call(
        middle_kernel,
        out_shape=(
            jax.ShapeDtypeStruct((TOK, D), F32),
            jax.ShapeDtypeStruct((TOK, D), BF),
            jax.ShapeDtypeStruct((HEADS, TOK // 2, 128), BF),
            jax.ShapeDtypeStruct((4, D), F32),
        ),
        grid=(1,),
        in_specs=[whole(TOK, D)] * 6 + [whole(8, D), whole(D, D)],
        out_specs=[whole(TOK, D), whole(TOK, D), whole(HEADS, TOK // 2, 128), whole(4, D)],
        compiler_params=params(16),
        cost_estimate=cost(5),
        name="middle",
    )(*parts, resid, dy, sv, w_out)


def last_kernel(g_a, g_b, w, x, resid_grad, sv, out, sums, biases, total):
    step = pl.program_id(0)

    @pl.when(step == 0)
    def _():
        total[...] = jnp.zeros_like(total)

    for k in range(2):
        pair = []
        for packed in (g_a[k], g_b[k]):
            values = jnp.concatenate([packed[160:240, 0:64], packed[160:240, 64:128]], 0)
            pair += [packed[0:160, :], values]
        pair = jnp.concatenate(pair, 1)
        total[...] += dot(pair, w[k], ((1,), (1,)))
        biases[k] = jnp.sum(pair.astype(F32), 0, keepdims=True)

    @pl.when(step == 3)
    def _():
        part, gain_grad, shift_grad = norm_back(x[...].astype(F32), sv[0:1, :].astype(F32), total[...])
        out[...] = (resid_grad[...] + part).astype(BF)
        sums[0:1, :] = gain_grad
        sums[1:2, :] = shift_grad


def last(g, w, x, resid_grad, sv):
    return pl.pallas_call(
        last_kernel,
        out_shape=(
            jax.ShapeDtypeStruct((TOK, D), BF),
            jax.ShapeDtypeStruct((2, D), F32),
            jax.ShapeDtypeStruct((8, 1, 384), F32),
        ),
        grid=(4,),
        in_specs=[
            pl.BlockSpec((2, 240, 128), lambda i: (i, 0, 0)),
            pl.BlockSpec((2, 240, 128), lambda i: (i + 4, 0, 0)),
            pl.BlockSpec((2, D, 384), lambda i: (i, 0, 0)),
            whole(TOK, D),
            whole(TOK, D),
            whole(8, D),
        ],
        out_specs=[whole(TOK, D), whole(2, D), pl.BlockSpec((2, 1, 384), lambda i: (i, 0, 0))],
        scratch_shapes=[pltpu.VMEM((TOK, D), F32)],
        compiler_params=params(48),
        cost_estimate=cost(15),
        name="last",
    )(g, g, w, x, resid_grad, sv)


def body(
    inputs,
    image_ids,
    ln1_gain,
    ln1_shift,
    qkv_weight,
    query_bias,
    value_bias,
    out_weight,
    out_bias,
    ln2_gain,
    ln2_shift,
    fc1_weight,
    fc1_bias,
    fc2_weight,
    fc2_bias,
    out_grad,
):
    xi, yl, yh, zi, ci = (lax.axis_index(name) for name in ALL)
    zc = zi * 2 + ci
    where_at = jnp.arange(16)
    starts = jnp.sum((image_ids[:, None] < where_at[None, :] - 4).astype(jnp.int32), 0)
    at = jnp.where(where_at == 0, yh, jnp.where(where_at == 1, zi, jnp.where(where_at == 2, ci, yh * 8 + zc)))
    at = jnp.where(where_at < 4, at, starts).astype(jnp.int32)

    near = lax.all_gather(inputs, TP, axis=0, tiled=True).reshape(4, 2, TOK, D)
    crossed = along(inputs, "yh", 1)

    qkv = qkv_weight.reshape(8, 3, 2, 8, HEAD_DIM).transpose(3, 0, 2, 1, 4).reshape(8, 8, 384)
    small = jnp.stack(
        [ln1_gain, ln1_shift, query_bias, value_bias, out_bias, ln2_gain, ln2_shift, fc2_bias], 1
    )
    small = jnp.broadcast_to(jnp.pad(small, ((0, 0), (0, 120)))[None], (8, 8, 128))
    fc1 = fc1_weight.reshape(8, 16, 8, 32).transpose(2, 0, 1, 3).reshape(8, 8, 512)
    columns = exchange(jnp.concatenate([qkv, small, fc1], 2), TP)
    far = lax.all_gather(after(crossed, columns), TP, axis=0, tiled=True).reshape(4, 2, TOK, D)
    columns = columns.reshape(64, D)

    fc1 = jnp.concatenate([columns[0:32, 512:], columns[32:64, 512:]], 1)
    columns = jnp.concatenate([columns[0:32, 0:512], columns[32:64, 0:512]], 1)
    spread = lambda v: exchange(jnp.broadcast_to(v[None], (16, *v.shape)), XY)
    first = spread(jnp.concatenate([columns, out_weight], 0))
    bias = jnp.pad(fc1_bias[None], ((0, 7), (0, D - 32)))
    rows = spread(after(jnp.concatenate([fc1, fc2_weight, bias], 0), first))
    sv = jnp.concatenate([first[:, 0:32, 384:392], first[:, 0:32, 896:904]], 1).reshape(D, 8).T
    sent = jnp.concatenate([out_grad, first[:, 32:40].reshape(128, D)], 0)
    sent = lax.all_gather(sent, TP, axis=0, tiled=False)
    w_out = sent[:, TOK:].reshape(8, 16, 8, D).transpose(1, 0, 2, 3).reshape(D, D)
    dy_all = sent.reshape(4, 2, TOK + 128, D)

    ids = image_ids.reshape(2, 1, HALF)
    n1_near, n1_far, q_near, kv_near, q_far, kv_far, heads, att_far, o_far, lse_far = project(
        at, near, far, first, sv, ids
    )
    q, kv = (q_near, q_far), (kv_near, kv_far)
    theirs = along(att_far, "yh", 1)
    att_near, o_near, lse_near = attend(at, 0, after(q[0], att_far), kv, ids)
    att_two = jnp.where(
        yh == 0, jnp.concatenate([att_near, theirs], 1), jnp.concatenate([theirs, att_near], 1)
    )
    att_two = after(att_two, rows)
    att_own = [att_two] + [from_up(att_two, k) for k in (1, 2, 3)]
    att_other = [along(block, "c", 1) for block in att_own]
    w_qkv = lax.all_gather(after(heads, *att_other), TP, axis=0, tiled=False)
    split = lambda blocks: [block.reshape(4, 2, TOK, 128) for block in blocks]
    resid, att_tok, y_part, dn2_other, dn2_own, fc1_grad, fc2_grad, b1_grad = feed(
        at, split(att_own), split(att_other), near, w_out, sv, rows, dy_all
    )

    mixed = mix(at, dn2_own, along(dn2_other, "c", 1))
    parts = [mixed[0]] + [along(mixed[k], "z", k) for k in (1, 2, 3)]
    fc2_grad = exchange(fc2_grad, XY)
    parts = [after(parts[0], fc2_grad)] + parts[1:]
    resid_grad, branch_grad, att_grad, mid_sums = middle(parts, resid, out_grad, sv, w_out)
    do = exchange(after(att_grad, w_qkv), SEQ)
    turn = ((0,), (0,))

    g, g_near, g_far = attend_back(
        at, q, kv, do, (o_near, o_far), (lse_near, lse_far), ids
    )

    out_w = dot(att_tok, branch_grad, turn).astype(BF)
    out_w = lax.psum_scatter(after(out_w, do), TP, scatter_dimension=0, tiled=True)

    fc1_grad = exchange(after(fc1_grad, do), XY)
    g_tok = exchange(after(g, fc1_grad), SEQ)
    fc2_grad = jnp.sum(fc2_grad.astype(F32), 0)
    fc1_grad = jnp.sum(fc1_grad.astype(F32), 0).reshape(8, 8, 512)
    fc1_grad = exchange(after(fc1_grad, g_tok), TP)
    fc1_grad = fc1_grad.reshape(8, 8, 16, 32).transpose(1, 2, 0, 3).reshape(8, FF)

    summed = lax.psum_scatter(after(y_part, *parts).reshape(HALF, D), TP, scatter_dimension=0, tiled=True)
    outputs = resid + summed.astype(F32) + sv[7].astype(F32)

    qkv_grad = dot(n1_near.reshape(HALF, D), g_near, turn) + dot(n1_far.reshape(HALF, D), g_far, turn)
    qkv_grad = qkv_grad.astype(BF)
    pick = lambda v, axis, place: lax.dynamic_index_in_dim(v, place, axis, keepdims=False)
    out_w = after(out_w, qkv_grad).reshape(4, 2, 2, 8, D)
    total = pick(out_w, 0, xi).astype(F32)
    for k in (1, 2, 3):
        total = total + along(pick(out_w, 0, (xi + k) % 4), "x", k).astype(F32)
    out_w = total.astype(BF)
    g_tok = after(g_tok, out_w)
    input_grad, norm_sums, biases = last(g_tok, w_qkv, inputs, resid_grad, sv)
    biases = biases.reshape(8, 2, 3, HEAD_DIM).transpose(2, 1, 0, 3).reshape(3, D)
    vectors = jnp.concatenate([norm_sums, biases[0:1], biases[2:3], mid_sums])
    vectors = vectors.reshape(8, 128, 8).transpose(1, 0, 2)
    mine = jnp.arange(8)[None, :, None] == zc
    b1_part = jnp.where(mine, b1_grad.reshape(16, 1, 32), 0.0).reshape(128, 4, 8)
    b1_part = jnp.pad(b1_part, ((0, 0), (0, 4), (0, 0)))
    vectors = jnp.concatenate([vectors, b1_part], 2)
    high = vectors.astype(BF)
    low = (vectors - high.astype(F32)).astype(BF)

    final = jnp.concatenate([qkv_grad.reshape(128, 8, 192), high, low], 2)
    final = after(final, out_w)
    out_w = after(out_w, norm_sums)
    by_y = lambda y: pick(pick(out_w, 0, y % 2), 0, y // 2)
    yi = yh * 2 + yl
    total = by_y(yi).astype(F32)
    for k in (1, 2, 3):
        total = total + along_y(by_y((yi + k) % 4), k).astype(F32)
    out_w = lax.ppermute(total, ALL, [(j * 8 + s, (2 * s + j // 8) * 8 + j % 8) for j in range(16) for s in range(8)])
    final = exchange(final, ALL).astype(F32)
    qkv_grad = jnp.sum(final[:, :, 0:192].reshape(8, HEADS, 8, 192), 0)
    qkv_grad = qkv_grad.reshape(HEADS, 8, 3, HEAD_DIM).transpose(1, 2, 0, 3).reshape(8, 3 * D)
    vectors = jnp.sum(final[:, :, 192:208] + final[:, :, 208:224], 0)
    fc1_bias_grad = vectors[0:4, 8:16].reshape(32)
    vectors = vectors[:, 0:8]
    return (
        outputs.astype(BF),
        input_grad,
        vectors[0],
        vectors[1],
        qkv_grad,
        vectors[2],
        vectors[3],
        out_w,
        vectors[4],
        vectors[5],
        vectors[6],
        fc1_grad,
        fc1_bias_grad,
        fc2_grad,
        vectors[7],
    )


def solution(mesh):
    fine = Mesh(mesh.devices.reshape(4, 2, 2, 4, 2), ALL)
    rows = P(ALL, None)
    vec = P(ALL)
    return jax.shard_map(
        body,
        mesh=fine,
        in_specs=(rows, P(("x", "yl")), vec, vec, rows, vec, vec, rows, vec, vec, vec, rows, vec, rows, vec, rows),
        out_specs=(rows, rows, vec, vec, rows, vec, vec, rows, vec, vec, vec, rows, vec, rows, vec),
        check_vma=False,
    )
```

```python
import functools

import jax
import jax.numpy as jnp
from jax import lax
from jax.experimental import pallas as pl
from jax.experimental.pallas import tpu as pltpu
from jax.sharding import Mesh
from jax.sharding import PartitionSpec as P

HEADS = 16
HEAD_DIM = 64
D = 1024
FF = 4096
TOK = 160
GROUP = 2560
HALF = 1280
EPSILON = 1e-06
NEGATIVE = -1e30
TILE = 256
TILES = GROUP // TILE
ALL = ("x", "yl", "yh", "z", "c")
TP = ("z", "c")
XY = ("x", "yl", "yh")
SEQ = ("yh", "z", "c")
BF = jnp.bfloat16
F32 = jnp.float32


def dot(left, right, dims=((1,), (0,))):
    return lax.dot_general(left, right, (dims, ((), ())), preferred_element_type=F32)


def params(mebibytes):
    return pltpu.CompilerParams(vmem_limit_bytes=mebibytes * 1024 * 1024)


def cost(micros):
    return pl.CostEstimate(flops=int(micros * 1e9), bytes_accessed=1 << 20, transcendentals=0)


def whole(*shape):
    return pl.BlockSpec(shape, lambda *_: (0,) * len(shape))


def along(value, axis, by):
    size = 4 if axis in ("x", "z") else 2
    return lax.ppermute(value, axis, [(i, (i + by) % size) for i in range(size)])


def along_y(value, by):
    pairs = []
    for yl in range(2):
        for yh in range(2):
            to = (yh * 2 + yl + by) % 4
            pairs.append((yl * 2 + yh, (to % 2) * 2 + to // 2))
    return lax.ppermute(value, ("yl", "yh"), pairs)


def from_up(value, k):
    return along(value, "z", 4 - k)


def after(value, *done):
    return lax.optimization_barrier((value, *done))[0]


def exchange(value, axes):
    return lax.all_to_all(value, axes, split_axis=0, concat_axis=0, tiled=True)


def project_rows(raw, sv, wh, bias):
    rows = raw.astype(F32)
    center = rows - jnp.mean(rows, -1, keepdims=True)
    spread = jnp.mean(center * center, -1, keepdims=True)
    gain = sv[0:1, :].astype(F32)
    shift = sv[1:2, :].astype(F32)
    normed = (center * lax.rsqrt(spread + EPSILON) * gain + shift).astype(BF)
    mixed = dot(normed, wh[...])
    queries = (mixed[:, 0:64] + bias[0:1, :]).astype(BF) * jnp.asarray(0.125, BF)
    keys = mixed[:, 64:128].astype(BF)
    values = (mixed[:, 128:192] + bias[8:9, :]).astype(BF)
    return normed, jnp.concatenate([queries, jnp.zeros_like(queries)], 1), jnp.concatenate([keys, values], 1)


def choose_head(at, w, sv, heads, wh, bias):
    @pl.when(pl.program_id(0) == 0)
    def _():
        for j in range(16):
            for part in range(2):
                lane = part * 512
                rows = jnp.where(at[0] == 0, w[j, :, lane : lane + 192], w[j, :, lane + 192 : lane + 384])
                wh[j * 64 + part * 32 : j * 64 + part * 32 + 32, :] = rows
                heads[j * 64 + part * 32 : j * 64 + part * 32 + 32, :] = w[j, :, lane : lane + 384]
        for row, place in ((2, 0), (3, 8)):
            value = sv[row : row + 1, 0:64]
            for h in range(1, HEADS):
                value = jnp.where(at[3] == h, sv[row : row + 1, h * 64 : h * 64 + 64], value)
            bias[place : place + 1, :] = value.astype(F32)


def image_range(at, ids):
    first = jnp.zeros_like(ids)
    length = jnp.zeros_like(ids)
    for m in range(4):
        first = jnp.where(ids == m, at[4 + m], first)
        length = jnp.where(ids == m, at[5 + m] - at[4 + m], length)
    return first, length


def masked(values, base, first, length, fill):
    place = lax.broadcasted_iota(jnp.int32, values.shape, 0) - (first - base)
    return jnp.where(jnp.logical_and(place >= 0, place < length), values, fill)


def attend_tile(at, queries, kv, vt, ids, att, o_out, lse_out):
    first, length = image_range(at, ids[0])
    scores = []
    for key_half, keys in enumerate(kv):
        raw = dot(keys[...], queries, ((1,), (1,)))
        base = ((key_half + at[0]) % 2) * HALF
        scores.append(masked(raw, base, first, length, NEGATIVE))
    top = jnp.maximum(jnp.max(scores[0], 0, keepdims=True), jnp.max(scores[1], 0, keepdims=True))
    total = 0.0
    out = 0.0
    for part, values in zip(scores, vt, strict=True):
        part = jnp.exp(part - top)
        total = total + jnp.sum(part, 0, keepdims=True)
        out = out + dot(values[64:128, :], part.astype(BF))
    out = out / total
    o_out[...] = out
    att[...] = out.T.astype(BF)
    lse_out[0] = top + jnp.log(total)


def project_kernel(at, x_a, x_b, w, sv, ids, n1_a, n1_b, q_a, kv_a, q_b, kv_b, heads, att, o_out, lse_out, wh, bias, vt_a, vt_b):
    step = pl.program_id(0)
    choose_head(at, w, sv, heads, wh, bias)

    @pl.when(step < 4)
    def _():
        raw = jnp.where(step < 2, x_a[...], x_b[...]).reshape(4 * TOK, D)
        normed, queries, pairs = project_rows(raw, sv, wh, bias)
        rows = pl.ds(pl.multiple_of((step % 2) * 4 * TOK, 4 * TOK), 4 * TOK)

        def put(n1, q_out, kv_out):
            n1[...] = normed.reshape(2, 2, TOK, D)
            q_out[rows, :] = queries
            kv_out[rows, :] = pairs

        pl.when(step < 2)(lambda: put(n1_a, q_a, kv_a))
        pl.when(step >= 2)(lambda: put(n1_b, q_b, kv_b))

    @pl.when(step == 4)
    def _():
        vt_a[...] = kv_a[...].T
        vt_b[...] = kv_b[...].T

    @pl.when(step >= 4)
    def _():
        tile = step - 4
        queries = q_b[pl.ds(pl.multiple_of(tile * TILE, TILE), TILE), :]
        attend_tile(at, queries, (kv_a, kv_b), (vt_a, vt_b), ids, att, o_out, lse_out)


def project(at, near, far, rows, sv, ids):
    tiles = HALF // TILE
    one = lambda i, at: (jnp.minimum(i, 1), 0, 0, 0)
    two = lambda i, at: (jnp.clip(i - 2, 0, 1), 0, 0, 0)
    late = lambda i: jnp.maximum(i - 4, 0)
    block = lambda index: pl.BlockSpec((2, 2, TOK, D), index)
    tokens = jax.ShapeDtypeStruct((4, 2, TOK, D), BF)
    pairs = jax.ShapeDtypeStruct((HALF, 128), BF)
    return pl.pallas_call(
        project_kernel,
        out_shape=[tokens] * 2
        + [pairs] * 4
        + [
            jax.ShapeDtypeStruct((D, 384), BF),
            jax.ShapeDtypeStruct((HALF, HEAD_DIM), BF),
            jax.ShapeDtypeStruct((HEAD_DIM, HALF), F32),
            jax.ShapeDtypeStruct((tiles, 1, TILE), F32),
        ],
        grid_spec=pltpu.PrefetchScalarGridSpec(
            num_scalar_prefetch=1,
            grid=(4 + tiles,),
            in_specs=[
                block(one),
                block(two),
                whole(16, 32, D),
                whole(8, D),
                pl.BlockSpec((1, 1, TILE), lambda i, at: (1 - at[0], 0, late(i))),
            ],
            out_specs=[block(one), block(two)]
            + [whole(HALF, 128)] * 4
            + [
                whole(D, 384),
                pl.BlockSpec((TILE, HEAD_DIM), lambda i, at: (late(i), 0)),
                pl.BlockSpec((HEAD_DIM, TILE), lambda i, at: (0, late(i))),
                pl.BlockSpec((1, 1, TILE), lambda i, at: (late(i), 0, 0)),
            ],
            scratch_shapes=[pltpu.VMEM((D, 192), BF), pltpu.VMEM((16, HEAD_DIM), F32)] + [pltpu.VMEM((128, HALF), BF)] * 2,
        ),
        compiler_params=params(60),
        cost_estimate=cost(1),
        name="project_attend",
    )(at, near, far, rows, sv, ids)


def attend_kernel(at, q, kv_a, kv_b, ids, att, o_out, lse_out, vt_a, vt_b):
    @pl.when(pl.program_id(0) == 0)
    def _():
        vt_a[...] = kv_a[...].T
        vt_b[...] = kv_b[...].T

    attend_tile(at, q[...], (kv_a, kv_b), (vt_a, vt_b), ids, att, o_out, lse_out)


def attend(at, half, q, kv, ids):
    tiles = HALF // TILE
    pairs = whole(HALF, 128)
    return pl.pallas_call(
        attend_kernel,
        out_shape=(
            jax.ShapeDtypeStruct((HALF, HEAD_DIM), BF),
            jax.ShapeDtypeStruct((HEAD_DIM, HALF), F32),
            jax.ShapeDtypeStruct((tiles, 1, TILE), F32),
        ),
        grid_spec=pltpu.PrefetchScalarGridSpec(
            num_scalar_prefetch=1,
            grid=(tiles,),
            in_specs=[
                pl.BlockSpec((TILE, 128), lambda i, at: (i, 0)),
                pairs,
                pairs,
                pl.BlockSpec((1, 1, TILE), lambda i, at: ((at[0] + half) % 2, 0, i)),
            ],
            out_specs=[
                pl.BlockSpec((TILE, HEAD_DIM), lambda i, at: (i, 0)),
                pl.BlockSpec((HEAD_DIM, TILE), lambda i, at: (0, i)),
                pl.BlockSpec((1, 1, TILE), lambda i, at: (i, 0, 0)),
            ],
            scratch_shapes=[pltpu.VMEM((128, HALF), BF)] * 2,
        ),
        compiler_params=params(60),
        cost_estimate=cost(1),
        name="attend",
    )(at, q, *kv, ids)


def attend_back_kernel(at, q_a, q_b, kv_a, kv_b, do_in, o_a, o_b, lse_a, lse_b, ids, g_abs, g_a, g_b, q, kv, do, kt, dq, dkv):
    tile = pl.program_id(0)
    yh = at[0]

    @pl.when(tile == 0)
    def _():
        for ref, one, two in ((q, q_a, q_b), (kv, kv_a, kv_b)):
            ref[0:HALF, :] = one[...]
            ref[HALF:GROUP, :] = two[...]
        kt[...] = kv[...].T
        for half in range(2):
            start = ((half + yh) % 2) * HALF
            for s in range(8):
                packed = do_in[half * 8 + s]
                block = jnp.concatenate([packed[:, 0:64], packed[:, 64:128]], 0)
                block = jnp.concatenate([jnp.zeros_like(block), block], 1)
                do[pl.ds(pl.multiple_of(start + s * TOK, TOK), TOK), :] = block
        dkv[...] = jnp.zeros_like(dkv)

    near = tile < TILES // 2

    first, length = image_range(at, ids[0])
    o_tile = jnp.where(near, o_a[...], o_b[...])
    lse = jnp.where(near, lse_a[0], lse_b[0])
    rows = pl.ds(pl.multiple_of(tile * TILE, TILE), TILE)
    queries = q[rows, :]
    grads = do[rows, :]
    delta = jnp.sum(o_tile * grads[:, 64:128].astype(F32).T, 0, keepdims=True)
    dq_tile = 0.0
    for half in range(2):
        here = slice(half * HALF, half * HALF + HALF)
        scores = dot(kv[here, :], queries, ((1,), (1,)))
        base = ((half + yh) % 2) * HALF
        probs = jnp.exp(masked(scores, base, first, length, NEGATIVE) - lse)
        probs_grad = dot(kv[here, :], grads, ((1,), (1,)))
        scores_grad = (probs * (probs_grad - delta)).astype(BF)
        dkv[here, :] += dot(scores_grad, queries) + dot(probs.astype(BF), grads)
        dq_tile = dq_tile + dot(kt[0:64, here], scores_grad)
    dq[rows, :] = (dq_tile.T * 0.125).astype(BF)

    @pl.when(tile == TILES - 1)
    def _():
        for ref, half in ((g_a, 0), (g_b, 1)):
            here = slice(half * HALF, half * HALF + HALF)
            ref[:, 0:64] = dq[here, :]
            ref[:, 64:192] = dkv[here, :].astype(BF)
            for s in range(8):
                block = ref[s * TOK : s * TOK + TOK, :]
                to = ((half + yh) % 2) * 8 + s
                g_abs[to, 0:TOK, :] = block[:, 0:128]
                g_abs[to, TOK : TOK + 80, :] = jnp.concatenate([block[0:80, 128:192], block[80:TOK, 128:192]], 1)


def attend_back(at, q, kv, do, o, lse, ids):
    pairs = whole(HALF, 128)
    last = TILES // 2 - 1
    one = lambda i: jnp.minimum(i, last)
    two = lambda i: jnp.maximum(i - last - 1, 0)
    wide = pltpu.VMEM((GROUP, 128), BF)
    return pl.pallas_call(
        attend_back_kernel,
        out_shape=(
            jax.ShapeDtypeStruct((HEADS, 240, 128), BF),
            jax.ShapeDtypeStruct((HALF, 192), BF),
            jax.ShapeDtypeStruct((HALF, 192), BF),
        ),
        grid_spec=pltpu.PrefetchScalarGridSpec(
            num_scalar_prefetch=1,
            grid=(TILES,),
            in_specs=[pairs] * 4
            + [whole(HEADS, TOK // 2, 128)]
            + [pl.BlockSpec((HEAD_DIM, TILE), lambda i, at, f=f: (0, f(i))) for f in (one, two)]
            + [pl.BlockSpec((1, 1, TILE), lambda i, at, f=f: (f(i), 0, 0)) for f in (one, two)]
            + [pl.BlockSpec((1, 1, TILE), lambda i, at: ((at[0] + i // (last + 1)) % 2, 0, i % (last + 1)))],
            out_specs=[whole(HEADS, 240, 128), whole(HALF, 192), whole(HALF, 192)],
            scratch_shapes=[
                wide,
                wide,
                wide,
                pltpu.VMEM((128, GROUP), BF),
                pltpu.VMEM((GROUP, HEAD_DIM), BF),
                pltpu.VMEM((GROUP, 128), F32),
            ],
        ),
        compiler_params=params(60),
        cost_estimate=cost(20),
        name="attend_back",
    )(at, *q, *kv, do, *o, *lse, ids)


def feed_kernel(at, *refs):
    blocks, refs = refs[:8], refs[8:]
    x, w_out, sv, rows, bias, dy, resid_out, att_out, y_out, dn2_other, dn2_own, w1_out, w2_out, b1_out = refs[:14]
    wide, w1, w2, b1, w1_grad, w2_grad = refs[14:]
    step = pl.program_id(0)
    z, core = at[1], at[2]
    own = step >= 1

    @pl.when(step == 0)
    def _():
        for j in range(16):
            w1[j * 64 : j * 64 + 32, :] = rows[j, 0:32, 0:512]
            w1[j * 64 + 32 : j * 64 + 64, :] = rows[j, 0:32, 512:1024]
            w2[j * 32 : j * 32 + 32, :] = rows[j, 32:64, :]
            b1[0:1, j * 32 : j * 32 + 32] = bias[j, 0:1, 0:32].astype(F32)
        b1_out[...] = jnp.zeros_like(b1_out)
        w1_grad[...] = jnp.zeros_like(w1_grad)
        w2_grad[...] = jnp.zeros_like(w2_grad)

    for k in range(4):
        mine, theirs = (block[:, 0].reshape(4 * TOK, 128) for block in (blocks[k], blocks[4 + k]))
        one = jnp.where(core == 0, mine, theirs)
        two = jnp.where(core == 0, theirs, mine)
        for h in range(2):
            lane = pl.multiple_of(h * 512 + ((z + k) % 4) * 128, 128)
            here = slice(h * 64, h * 64 + 64)
            wide[:, pl.ds(lane, 128)] = jnp.concatenate([one[:, here], two[:, here]], 1)
    resid = x[:, 0].reshape(4 * TOK, D).astype(F32) + dot(wide[...], w_out[...]) + sv[4:5, :].astype(F32)

    for k in range(4):

        @pl.when(jnp.logical_and(own, z == k))
        def _(k=k):
            resid_out[...] = resid[k * TOK : k * TOK + TOK]
            att_out[...] = wide[k * TOK : k * TOK + TOK, :]

    center = resid - jnp.mean(resid, -1, keepdims=True)
    spread = jnp.mean(center * center, -1, keepdims=True)
    normed = (center * lax.rsqrt(spread + EPSILON) * sv[5:6, :].astype(F32) + sv[6:7, :].astype(F32)).astype(BF)
    pre = dot(normed, w1[...]) + b1[0:1, :]
    cdf = 0.5 * (1.0 + lax.erf(pre * (0.5**0.5)))
    hidden = (pre * cdf).astype(BF)
    slope = cdf + pre * jnp.exp(-0.5 * pre * pre) * 0.3989422804014327
    dy_rows = dy[:, 0].reshape(4 * TOK, D)
    hidden_grad = dot(dy_rows, w2[...], ((1,), (1,)))
    pre_grad = (hidden_grad * slope).astype(BF)
    normed_grad = dot(pre_grad, w1[...], ((1,), (1,))).astype(BF).reshape(4, TOK, D)
    y_out[:, 0] = dot(hidden, w2[...]).astype(BF).reshape(4, TOK, D)
    w2_grad[...] += dot(hidden, dy_rows, ((0,), (0,)))
    w1_grad[...] += dot(normed, pre_grad, ((0,), (0,)))
    b1_out[...] += jnp.sum(pre_grad.astype(F32), 0, keepdims=True)

    @pl.when(own)
    def _():
        dn2_own[...] = normed_grad

    @pl.when(jnp.logical_not(own))
    def _():
        dn2_other[...] = normed_grad

    @pl.when(step == 1)
    def _():
        w1_out[...] = w1_grad[...].astype(BF).reshape(16, 64, 512)
        w2_out[...] = w2_grad[...].astype(BF).reshape(16, 32, D)


def feed(at, att_own, att_other, x, w_out, sv, rows, dy):
    core_of = lambda i, at: jnp.where(i >= 1, at[2], 1 - at[2])
    tok_spec = lambda width: pl.BlockSpec((4, 1, TOK, width), lambda i, at: (0, core_of(i, at), 0, 0))
    return pl.pallas_call(
        feed_kernel,
        out_shape=(
            jax.ShapeDtypeStruct((TOK, D), F32),
            jax.ShapeDtypeStruct((TOK, D), BF),
            jax.ShapeDtypeStruct((4, 2, TOK, D), BF),
            jax.ShapeDtypeStruct((4, TOK, D), BF),
            jax.ShapeDtypeStruct((4, TOK, D), BF),
            jax.ShapeDtypeStruct((16, 64, 512), BF),
            jax.ShapeDtypeStruct((16, 32, D), BF),
            jax.ShapeDtypeStruct((1, 512), F32),
        ),
        grid_spec=pltpu.PrefetchScalarGridSpec(
            num_scalar_prefetch=1,
            grid=(2,),
            in_specs=[tok_spec(128)] * 8
            + [
                tok_spec(D),
                whole(D, D),
                whole(8, D),
                whole(16, 64, D),
                pl.BlockSpec((16, 8, D), lambda i, at: (0, 8, 0)),
                tok_spec(D),
            ],
            out_specs=[
                whole(TOK, D),
                whole(TOK, D),
                tok_spec(D),
                whole(4, TOK, D),
                whole(4, TOK, D),
                whole(16, 64, 512),
                whole(16, 32, D),
                whole(1, 512),
            ],
            scratch_shapes=[
                pltpu.VMEM((4 * TOK, D), BF),
                pltpu.VMEM((D, 512), BF),
                pltpu.VMEM((512, D), BF),
                pltpu.VMEM((8, 512), F32),
                pltpu.VMEM((D, 512), F32),
                pltpu.VMEM((512, D), F32),
            ],
        ),
        compiler_params=params(56),
        cost_estimate=cost(20),
        name="out_feed",
    )(at, *att_own, *att_other, x, w_out, sv, rows, rows, dy)


def mix_kernel(at, own, came, *outs):
    for k in range(4):
        here = pl.ds((at[1] + k) % 4, 1)
        outs[k][...] = (own[here][0].astype(F32) + came[here][0].astype(F32)).astype(BF)


def mix(at, own, came):
    return pl.pallas_call(
        mix_kernel,
        out_shape=[jax.ShapeDtypeStruct((TOK, D), BF)] * 4,
        grid_spec=pltpu.PrefetchScalarGridSpec(
            num_scalar_prefetch=1,
            grid=(1,),
            in_specs=[whole(4, TOK, D)] * 2,
            out_specs=[whole(TOK, D)] * 4,
        ),
        compiler_params=params(60),
        cost_estimate=cost(2),
        name="mix",
    )(at, own, came)


def norm_back(values, gain, grad):
    center = values - jnp.mean(values, -1, keepdims=True)
    spread = jnp.mean(center * center, -1, keepdims=True)
    r = lax.rsqrt(spread + EPSILON)
    n = center * r
    e = grad * gain
    inner = r * (e - jnp.mean(e, -1, keepdims=True) - n * jnp.mean(e * n, -1, keepdims=True))
    return inner, jnp.sum(grad * n, 0, keepdims=True), jnp.sum(grad, 0, keepdims=True)


def middle_kernel(m0, m1, m2, m3, resid, dy, sv, w_out, resid_grad_out, branch_out, att_grad_out, sums):
    grad = m0[...].astype(F32) + m1[...].astype(F32) + m2[...].astype(F32) + m3[...].astype(F32)
    dy_f = dy[...].astype(F32)
    part, gain_grad, shift_grad = norm_back(resid[...], sv[5:6, :].astype(F32), grad)
    resid_grad = dy_f + part
    resid_grad_out[...] = resid_grad
    branch = resid_grad.astype(BF)
    branch_out[...] = branch
    sums[0:1, :] = jnp.sum(branch.astype(F32), 0, keepdims=True)
    sums[1:2, :] = gain_grad
    sums[2:3, :] = shift_grad
    sums[3:4, :] = jnp.sum(dy_f, 0, keepdims=True)
    att_grad = dot(branch, w_out[...], ((1,), (1,))).astype(BF)
    for h in range(HEADS):
        lane = h * 64
        att_grad_out[h] = jnp.concatenate(
            [att_grad[0:80, lane : lane + 64], att_grad[80:160, lane : lane + 64]], 1
        )


def middle(parts, resid, dy, sv, w_out):
    return pl.pallas_call(
        middle_kernel,
        out_shape=(
            jax.ShapeDtypeStruct((TOK, D), F32),
            jax.ShapeDtypeStruct((TOK, D), BF),
            jax.ShapeDtypeStruct((HEADS, TOK // 2, 128), BF),
            jax.ShapeDtypeStruct((4, D), F32),
        ),
        grid=(1,),
        in_specs=[whole(TOK, D)] * 6 + [whole(8, D), whole(D, D)],
        out_specs=[whole(TOK, D), whole(TOK, D), whole(HEADS, TOK // 2, 128), whole(4, D)],
        compiler_params=params(16),
        cost_estimate=cost(5),
        name="middle",
    )(*parts, resid, dy, sv, w_out)


def last_kernel(g_a, g_b, w, x, resid_grad, sv, out, sums, biases, total):
    step = pl.program_id(0)

    @pl.when(step == 0)
    def _():
        total[...] = jnp.zeros_like(total)

    for k in range(2):
        pair = []
        for packed in (g_a[k], g_b[k]):
            values = jnp.concatenate([packed[160:240, 0:64], packed[160:240, 64:128]], 0)
            pair += [packed[0:160, :], values]
        pair = jnp.concatenate(pair, 1)
        total[...] += dot(pair, w[k], ((1,), (1,)))
        biases[k] = jnp.sum(pair.astype(F32), 0, keepdims=True)

    @pl.when(step == 3)
    def _():
        part, gain_grad, shift_grad = norm_back(x[...].astype(F32), sv[0:1, :].astype(F32), total[...])
        out[...] = (resid_grad[...] + part).astype(BF)
        sums[0:1, :] = gain_grad
        sums[1:2, :] = shift_grad


def last(g, w, x, resid_grad, sv):
    return pl.pallas_call(
        last_kernel,
        out_shape=(
            jax.ShapeDtypeStruct((TOK, D), BF),
            jax.ShapeDtypeStruct((2, D), F32),
            jax.ShapeDtypeStruct((8, 1, 384), F32),
        ),
        grid=(4,),
        in_specs=[
            pl.BlockSpec((2, 240, 128), lambda i: (i, 0, 0)),
            pl.BlockSpec((2, 240, 128), lambda i: (i + 4, 0, 0)),
            pl.BlockSpec((2, D, 384), lambda i: (i, 0, 0)),
            whole(TOK, D),
            whole(TOK, D),
            whole(8, D),
        ],
        out_specs=[whole(TOK, D), whole(2, D), pl.BlockSpec((2, 1, 384), lambda i: (i, 0, 0))],
        scratch_shapes=[pltpu.VMEM((TOK, D), F32)],
        compiler_params=params(48),
        cost_estimate=cost(15),
        name="last",
    )(g, g, w, x, resid_grad, sv)


def body(
    inputs,
    image_ids,
    ln1_gain,
    ln1_shift,
    qkv_weight,
    query_bias,
    value_bias,
    out_weight,
    out_bias,
    ln2_gain,
    ln2_shift,
    fc1_weight,
    fc1_bias,
    fc2_weight,
    fc2_bias,
    out_grad,
):
    xi, yl, yh, zi, ci = (lax.axis_index(name) for name in ALL)
    zc = zi * 2 + ci
    where_at = jnp.arange(16)
    starts = jnp.sum((image_ids[:, None] < where_at[None, :] - 4).astype(jnp.int32), 0)
    at = jnp.where(where_at == 0, yh, jnp.where(where_at == 1, zi, jnp.where(where_at == 2, ci, yh * 8 + zc)))
    at = jnp.where(where_at < 4, at, starts).astype(jnp.int32)

    near = lax.all_gather(inputs, TP, axis=0, tiled=True).reshape(4, 2, TOK, D)
    crossed = along(inputs, "yh", 1)

    qkv = qkv_weight.reshape(8, 3, 2, 8, HEAD_DIM).transpose(3, 0, 2, 1, 4).reshape(8, 8, 384)
    small = jnp.stack(
        [ln1_gain, ln1_shift, query_bias, value_bias, out_bias, ln2_gain, ln2_shift, fc2_bias], 1
    )
    small = jnp.broadcast_to(jnp.pad(small, ((0, 0), (0, 120)))[None], (8, 8, 128))
    fc1 = fc1_weight.reshape(8, 16, 8, 32).transpose(2, 0, 1, 3).reshape(8, 8, 512)
    columns = exchange(jnp.concatenate([qkv, small, fc1], 2), TP)
    far = lax.all_gather(after(crossed, columns), TP, axis=0, tiled=True).reshape(4, 2, TOK, D)
    columns = columns.reshape(64, D)

    fc1 = jnp.concatenate([columns[0:32, 512:], columns[32:64, 512:]], 1)
    columns = jnp.concatenate([columns[0:32, 0:512], columns[32:64, 0:512]], 1)
    spread = lambda v: exchange(jnp.broadcast_to(v[None], (16, *v.shape)), XY)
    first = spread(jnp.concatenate([columns, out_weight], 0))
    bias = jnp.pad(fc1_bias[None], ((0, 7), (0, D - 32)))
    rows = spread(after(jnp.concatenate([fc1, fc2_weight, bias], 0), first))
    sv = jnp.concatenate([first[:, 0:32, 384:392], first[:, 0:32, 896:904]], 1).reshape(D, 8).T
    sent = jnp.concatenate([out_grad, first[:, 32:40].reshape(128, D)], 0)
    sent = lax.all_gather(sent, TP, axis=0, tiled=False)
    w_out = sent[:, TOK:].reshape(8, 16, 8, D).transpose(1, 0, 2, 3).reshape(D, D)
    dy_all = sent.reshape(4, 2, TOK + 128, D)

    ids = image_ids.reshape(2, 1, HALF)
    n1_near, n1_far, q_near, kv_near, q_far, kv_far, heads, att_far, o_far, lse_far = project(
        at, near, far, first, sv, ids
    )
    q, kv = (q_near, q_far), (kv_near, kv_far)
    theirs = along(att_far, "yh", 1)
    att_near, o_near, lse_near = attend(at, 0, after(q[0], att_far), kv, ids)
    att_two = jnp.where(
        yh == 0, jnp.concatenate([att_near, theirs], 1), jnp.concatenate([theirs, att_near], 1)
    )
    att_two = after(att_two, rows)
    att_own = [att_two] + [from_up(att_two, k) for k in (1, 2, 3)]
    att_other = [along(after(block, w_out), "c", 1) for block in att_own]
    w_qkv = lax.all_gather(after(heads, *att_other), TP, axis=0, tiled=False)
    split = lambda blocks: [block.reshape(4, 2, TOK, 128) for block in blocks]
    resid, att_tok, y_part, dn2_other, dn2_own, fc1_grad, fc2_grad, b1_grad = feed(
        at, split(att_own), split(att_other), near, w_out, sv, rows, dy_all
    )

    mixed = mix(at, dn2_own, along(dn2_other, "c", 1))
    parts = [mixed[0]] + [along(mixed[k], "z", k) for k in (1, 2, 3)]
    fc2_grad = exchange(fc2_grad, XY)
    parts = [after(parts[0], fc2_grad)] + parts[1:]
    resid_grad, branch_grad, att_grad, mid_sums = middle(parts, resid, out_grad, sv, w_out)
    do = exchange(after(att_grad, w_qkv), SEQ)
    turn = ((0,), (0,))

    g, g_near, g_far = attend_back(
        at, q, kv, do, (o_near, o_far), (lse_near, lse_far), ids
    )

    out_w = dot(att_tok, branch_grad, turn).astype(BF)
    out_w = lax.psum_scatter(after(out_w, do), TP, scatter_dimension=0, tiled=True)

    fc1_grad = exchange(after(fc1_grad, do), XY)
    g_tok = exchange(after(g, fc1_grad), SEQ)
    fc1_grad = jnp.sum(fc1_grad.astype(F32), 0).reshape(8, 8, 512)
    fc1_grad = exchange(after(fc1_grad, g_tok), TP)
    fc1_grad = fc1_grad.reshape(8, 8, 16, 32).transpose(1, 2, 0, 3).reshape(8, FF)

    summed = lax.psum_scatter(after(y_part, *parts).reshape(HALF, D), TP, scatter_dimension=0, tiled=True)
    outputs = resid + summed.astype(F32) + sv[7].astype(F32)

    qkv_grad = dot(n1_near.reshape(HALF, D), g_near, turn) + dot(n1_far.reshape(HALF, D), g_far, turn)
    qkv_grad = qkv_grad.astype(BF)
    pick = lambda v, axis, place: lax.dynamic_index_in_dim(v, place, axis, keepdims=False)
    out_w = after(out_w, qkv_grad).reshape(4, 2, 2, 8, D)
    total = pick(out_w, 0, xi).astype(F32)
    for k in (1, 2, 3):
        total = total + along(pick(out_w, 0, (xi + k) % 4), "x", k).astype(F32)
    out_w = total.astype(BF)
    g_tok = after(g_tok, out_w)
    input_grad, norm_sums, biases = last(g_tok, w_qkv, inputs, resid_grad, sv)
    fc2_grad = jnp.sum(after(fc2_grad, norm_sums).astype(F32), 0)
    biases = biases.reshape(8, 2, 3, HEAD_DIM).transpose(2, 1, 0, 3).reshape(3, D)
    vectors = jnp.concatenate([norm_sums, biases[0:1], biases[2:3], mid_sums])
    vectors = vectors.reshape(8, 128, 8).transpose(1, 0, 2)
    mine = jnp.arange(8)[None, :, None] == zc
    b1_part = jnp.where(mine, b1_grad.reshape(16, 1, 32), 0.0).reshape(128, 4, 8)
    b1_part = jnp.pad(b1_part, ((0, 0), (0, 4), (0, 0)))
    vectors = jnp.concatenate([vectors, b1_part], 2)
    high = vectors.astype(BF)
    low = (vectors - high.astype(F32)).astype(BF)

    final = jnp.concatenate([qkv_grad.reshape(128, 8, 192), high, low], 2)
    final = after(final, out_w)
    out_w = after(out_w, norm_sums)
    by_y = lambda y: pick(pick(out_w, 0, y % 2), 0, y // 2)
    yi = yh * 2 + yl
    total = by_y(yi).astype(F32)
    for k in (1, 2, 3):
        total = total + along_y(by_y((yi + k) % 4), k).astype(F32)
    out_w = lax.ppermute(total, ALL, [(j * 8 + s, (2 * s + j // 8) * 8 + j % 8) for j in range(16) for s in range(8)])
    final = exchange(final, ALL).astype(F32)
    qkv_grad = jnp.sum(final[:, :, 0:192].reshape(8, HEADS, 8, 192), 0)
    qkv_grad = qkv_grad.reshape(HEADS, 8, 3, HEAD_DIM).transpose(1, 2, 0, 3).reshape(8, 3 * D)
    vectors = jnp.sum(final[:, :, 192:208] + final[:, :, 208:224], 0)
    fc1_bias_grad = vectors[0:4, 8:16].reshape(32)
    vectors = vectors[:, 0:8]
    return (
        outputs.astype(BF),
        input_grad,
        vectors[0],
        vectors[1],
        qkv_grad,
        vectors[2],
        vectors[3],
        out_w,
        vectors[4],
        vectors[5],
        vectors[6],
        fc1_grad,
        fc1_bias_grad,
        fc2_grad,
        vectors[7],
    )


def solution(mesh):
    fine = Mesh(mesh.devices.reshape(4, 2, 2, 4, 2), ALL)
    rows = P(ALL, None)
    vec = P(ALL)
    return jax.shard_map(
        body,
        mesh=fine,
        in_specs=(rows, P(("x", "yl")), vec, vec, rows, vec, vec, rows, vec, vec, vec, rows, vec, rows, vec, rows),
        out_specs=(rows, rows, vec, vec, rows, vec, vec, rows, vec, vec, vec, rows, vec, rows, vec),
        check_vma=False,
    )
```

```python
import functools

import jax
import jax.numpy as jnp
from jax import lax
from jax.experimental import pallas as pl
from jax.experimental.pallas import tpu as pltpu
from jax.sharding import Mesh
from jax.sharding import PartitionSpec as P

HEADS = 16
HEAD_DIM = 64
D = 1024
FF = 4096
TOK = 160
GROUP = 2560
HALF = 1280
EPSILON = 1e-06
NEGATIVE = -1e30
TILE = 256
TILES = GROUP // TILE
ALL = ("x", "yl", "yh", "z", "c")
TP = ("z", "c")
XY = ("x", "yl", "yh")
SEQ = ("yh", "z", "c")
BF = jnp.bfloat16
F32 = jnp.float32


def dot(left, right, dims=((1,), (0,))):
    return lax.dot_general(left, right, (dims, ((), ())), preferred_element_type=F32)


def params(mebibytes):
    return pltpu.CompilerParams(vmem_limit_bytes=mebibytes * 1024 * 1024)


def cost(micros):
    return pl.CostEstimate(flops=int(micros * 1e9), bytes_accessed=1 << 20, transcendentals=0)


def whole(*shape):
    return pl.BlockSpec(shape, lambda *_: (0,) * len(shape))


def along(value, axis, by):
    size = 4 if axis in ("x", "z") else 2
    return lax.ppermute(value, axis, [(i, (i + by) % size) for i in range(size)])


def along_y(value, by):
    pairs = []
    for yl in range(2):
        for yh in range(2):
            to = (yh * 2 + yl + by) % 4
            pairs.append((yl * 2 + yh, (to % 2) * 2 + to // 2))
    return lax.ppermute(value, ("yl", "yh"), pairs)


def from_up(value, k):
    return along(value, "z", 4 - k)


def after(value, *done):
    return lax.optimization_barrier((value, *done))[0]


def exchange(value, axes):
    return lax.all_to_all(value, axes, split_axis=0, concat_axis=0, tiled=True)


def project_rows(raw, sv, wh, bias):
    rows = raw.astype(F32)
    center = rows - jnp.mean(rows, -1, keepdims=True)
    spread = jnp.mean(center * center, -1, keepdims=True)
    gain = sv[0:1, :].astype(F32)
    shift = sv[1:2, :].astype(F32)
    normed = (center * lax.rsqrt(spread + EPSILON) * gain + shift).astype(BF)
    mixed = dot(normed, wh[...])
    queries = (mixed[:, 0:64] + bias[0:1, :]).astype(BF) * jnp.asarray(0.125, BF)
    keys = mixed[:, 64:128].astype(BF)
    values = (mixed[:, 128:192] + bias[8:9, :]).astype(BF)
    return normed, jnp.concatenate([queries, jnp.zeros_like(queries)], 1), jnp.concatenate([keys, values], 1)


def choose_head(at, w, sv, heads, wh, bias):
    @pl.when(pl.program_id(0) == 0)
    def _():
        for j in range(16):
            for part in range(2):
                lane = part * 512
                rows = jnp.where(at[0] == 0, w[j, :, lane : lane + 192], w[j, :, lane + 192 : lane + 384])
                wh[j * 64 + part * 32 : j * 64 + part * 32 + 32, :] = rows
                heads[j * 64 + part * 32 : j * 64 + part * 32 + 32, :] = w[j, :, lane : lane + 384]
        for row, place in ((2, 0), (3, 8)):
            value = sv[row : row + 1, 0:64]
            for h in range(1, HEADS):
                value = jnp.where(at[3] == h, sv[row : row + 1, h * 64 : h * 64 + 64], value)
            bias[place : place + 1, :] = value.astype(F32)


def image_range(at, ids):
    first = jnp.zeros_like(ids)
    length = jnp.zeros_like(ids)
    for m in range(4):
        first = jnp.where(ids == m, at[4 + m], first)
        length = jnp.where(ids == m, at[5 + m] - at[4 + m], length)
    return first, length


def masked(values, base, first, length, fill):
    place = lax.broadcasted_iota(jnp.int32, values.shape, 0) - (first - base)
    return jnp.where(jnp.logical_and(place >= 0, place < length), values, fill)


def attend_tile(at, queries, kv, vt, ids, att, o_out, lse_out):
    first, length = image_range(at, ids[0])
    scores = []
    for key_half, keys in enumerate(kv):
        raw = dot(keys[...], queries, ((1,), (1,)))
        base = ((key_half + at[0]) % 2) * HALF
        scores.append(masked(raw, base, first, length, NEGATIVE))
    top = jnp.maximum(jnp.max(scores[0], 0, keepdims=True), jnp.max(scores[1], 0, keepdims=True))
    total = 0.0
    out = 0.0
    for part, values in zip(scores, vt, strict=True):
        part = jnp.exp(part - top)
        total = total + jnp.sum(part, 0, keepdims=True)
        out = out + dot(values[64:128, :], part.astype(BF))
    out = out / total
    o_out[...] = out
    att[...] = out.T.astype(BF)
    lse_out[0] = top + jnp.log(total)


def project_kernel(at, x_a, x_b, w, sv, ids, n1_a, n1_b, q_a, kv_a, q_b, kv_b, heads, att, o_out, lse_out, wh, bias, vt_a, vt_b):
    step = pl.program_id(0)
    choose_head(at, w, sv, heads, wh, bias)

    @pl.when(step < 4)
    def _():
        raw = jnp.where(step < 2, x_a[...], x_b[...]).reshape(4 * TOK, D)
        normed, queries, pairs = project_rows(raw, sv, wh, bias)
        rows = pl.ds(pl.multiple_of((step % 2) * 4 * TOK, 4 * TOK), 4 * TOK)

        def put(n1, q_out, kv_out):
            n1[...] = normed.reshape(2, 2, TOK, D)
            q_out[rows, :] = queries
            kv_out[rows, :] = pairs

        pl.when(step < 2)(lambda: put(n1_a, q_a, kv_a))
        pl.when(step >= 2)(lambda: put(n1_b, q_b, kv_b))

    @pl.when(step == 4)
    def _():
        vt_a[...] = kv_a[...].T
        vt_b[...] = kv_b[...].T

    @pl.when(step >= 4)
    def _():
        tile = step - 4
        queries = q_b[pl.ds(pl.multiple_of(tile * TILE, TILE), TILE), :]
        attend_tile(at, queries, (kv_a, kv_b), (vt_a, vt_b), ids, att, o_out, lse_out)


def project(at, near, far, rows, sv, ids):
    tiles = HALF // TILE
    one = lambda i, at: (jnp.minimum(i, 1), 0, 0, 0)
    two = lambda i, at: (jnp.clip(i - 2, 0, 1), 0, 0, 0)
    late = lambda i: jnp.maximum(i - 4, 0)
    block = lambda index: pl.BlockSpec((2, 2, TOK, D), index)
    tokens = jax.ShapeDtypeStruct((4, 2, TOK, D), BF)
    pairs = jax.ShapeDtypeStruct((HALF, 128), BF)
    return pl.pallas_call(
        project_kernel,
        out_shape=[tokens] * 2
        + [pairs] * 4
        + [
            jax.ShapeDtypeStruct((D, 384), BF),
            jax.ShapeDtypeStruct((HALF, HEAD_DIM), BF),
            jax.ShapeDtypeStruct((HEAD_DIM, HALF), F32),
            jax.ShapeDtypeStruct((tiles, 1, TILE), F32),
        ],
        grid_spec=pltpu.PrefetchScalarGridSpec(
            num_scalar_prefetch=1,
            grid=(4 + tiles,),
            in_specs=[
                block(one),
                block(two),
                whole(16, 32, D),
                whole(8, D),
                pl.BlockSpec((1, 1, TILE), lambda i, at: (1 - at[0], 0, late(i))),
            ],
            out_specs=[block(one), block(two)]
            + [whole(HALF, 128)] * 4
            + [
                whole(D, 384),
                pl.BlockSpec((TILE, HEAD_DIM), lambda i, at: (late(i), 0)),
                pl.BlockSpec((HEAD_DIM, TILE), lambda i, at: (0, late(i))),
                pl.BlockSpec((1, 1, TILE), lambda i, at: (late(i), 0, 0)),
            ],
            scratch_shapes=[pltpu.VMEM((D, 192), BF), pltpu.VMEM((16, HEAD_DIM), F32)] + [pltpu.VMEM((128, HALF), BF)] * 2,
        ),
        compiler_params=params(60),
        cost_estimate=cost(1),
        name="project_attend",
    )(at, near, far, rows, sv, ids)


def attend_kernel(at, q, kv_a, kv_b, ids, att, o_out, lse_out, vt_a, vt_b):
    @pl.when(pl.program_id(0) == 0)
    def _():
        vt_a[...] = kv_a[...].T
        vt_b[...] = kv_b[...].T

    attend_tile(at, q[...], (kv_a, kv_b), (vt_a, vt_b), ids, att, o_out, lse_out)


def attend(at, half, q, kv, ids):
    tiles = HALF // TILE
    pairs = whole(HALF, 128)
    return pl.pallas_call(
        attend_kernel,
        out_shape=(
            jax.ShapeDtypeStruct((HALF, HEAD_DIM), BF),
            jax.ShapeDtypeStruct((HEAD_DIM, HALF), F32),
            jax.ShapeDtypeStruct((tiles, 1, TILE), F32),
        ),
        grid_spec=pltpu.PrefetchScalarGridSpec(
            num_scalar_prefetch=1,
            grid=(tiles,),
            in_specs=[
                pl.BlockSpec((TILE, 128), lambda i, at: (i, 0)),
                pairs,
                pairs,
                pl.BlockSpec((1, 1, TILE), lambda i, at: ((at[0] + half) % 2, 0, i)),
            ],
            out_specs=[
                pl.BlockSpec((TILE, HEAD_DIM), lambda i, at: (i, 0)),
                pl.BlockSpec((HEAD_DIM, TILE), lambda i, at: (0, i)),
                pl.BlockSpec((1, 1, TILE), lambda i, at: (i, 0, 0)),
            ],
            scratch_shapes=[pltpu.VMEM((128, HALF), BF)] * 2,
        ),
        compiler_params=params(60),
        cost_estimate=cost(1),
        name="attend",
    )(at, q, *kv, ids)


def attend_back_kernel(at, q_a, q_b, kv_a, kv_b, do_in, o_a, o_b, lse_a, lse_b, ids, g_abs, g_a, g_b, q, kv, do, kt, dq, dkv):
    tile = pl.program_id(0)
    yh = at[0]

    @pl.when(tile == 0)
    def _():
        for ref, one, two in ((q, q_a, q_b), (kv, kv_a, kv_b)):
            ref[0:HALF, :] = one[...]
            ref[HALF:GROUP, :] = two[...]
        kt[...] = kv[...].T
        for half in range(2):
            start = ((half + yh) % 2) * HALF
            for s in range(8):
                packed = do_in[half * 8 + s]
                block = jnp.concatenate([packed[:, 0:64], packed[:, 64:128]], 0)
                block = jnp.concatenate([jnp.zeros_like(block), block], 1)
                do[pl.ds(pl.multiple_of(start + s * TOK, TOK), TOK), :] = block
        dkv[...] = jnp.zeros_like(dkv)

    near = tile < TILES // 2

    first, length = image_range(at, ids[0])
    o_tile = jnp.where(near, o_a[...], o_b[...])
    lse = jnp.where(near, lse_a[0], lse_b[0])
    rows = pl.ds(pl.multiple_of(tile * TILE, TILE), TILE)
    queries = q[rows, :]
    grads = do[rows, :]
    delta = jnp.sum(o_tile * grads[:, 64:128].astype(F32).T, 0, keepdims=True)
    dq_tile = 0.0
    for half in range(2):
        here = slice(half * HALF, half * HALF + HALF)
        scores = dot(kv[here, :], queries, ((1,), (1,)))
        base = ((half + yh) % 2) * HALF
        probs = jnp.exp(masked(scores, base, first, length, NEGATIVE) - lse)
        probs_grad = dot(kv[here, :], grads, ((1,), (1,)))
        scores_grad = (probs * (probs_grad - delta)).astype(BF)
        dkv[here, :] += dot(scores_grad, queries) + dot(probs.astype(BF), grads)
        dq_tile = dq_tile + dot(kt[0:64, here], scores_grad)
    dq[rows, :] = (dq_tile.T * 0.125).astype(BF)

    @pl.when(tile == TILES - 1)
    def _():
        for ref, half in ((g_a, 0), (g_b, 1)):
            here = slice(half * HALF, half * HALF + HALF)
            ref[:, 0:64] = dq[here, :]
            ref[:, 64:192] = dkv[here, :].astype(BF)
            for s in range(8):
                block = ref[s * TOK : s * TOK + TOK, :]
                to = ((half + yh) % 2) * 8 + s
                g_abs[to, 0:TOK, :] = block[:, 0:128]
                g_abs[to, TOK : TOK + 80, :] = jnp.concatenate([block[0:80, 128:192], block[80:TOK, 128:192]], 1)


def attend_back(at, q, kv, do, o, lse, ids):
    pairs = whole(HALF, 128)
    last = TILES // 2 - 1
    one = lambda i: jnp.minimum(i, last)
    two = lambda i: jnp.maximum(i - last - 1, 0)
    wide = pltpu.VMEM((GROUP, 128), BF)
    return pl.pallas_call(
        attend_back_kernel,
        out_shape=(
            jax.ShapeDtypeStruct((HEADS, 240, 128), BF),
            jax.ShapeDtypeStruct((HALF, 192), BF),
            jax.ShapeDtypeStruct((HALF, 192), BF),
        ),
        grid_spec=pltpu.PrefetchScalarGridSpec(
            num_scalar_prefetch=1,
            grid=(TILES,),
            in_specs=[pairs] * 4
            + [whole(HEADS, TOK // 2, 128)]
            + [pl.BlockSpec((HEAD_DIM, TILE), lambda i, at, f=f: (0, f(i))) for f in (one, two)]
            + [pl.BlockSpec((1, 1, TILE), lambda i, at, f=f: (f(i), 0, 0)) for f in (one, two)]
            + [pl.BlockSpec((1, 1, TILE), lambda i, at: ((at[0] + i // (last + 1)) % 2, 0, i % (last + 1)))],
            out_specs=[whole(HEADS, 240, 128), whole(HALF, 192), whole(HALF, 192)],
            scratch_shapes=[
                wide,
                wide,
                wide,
                pltpu.VMEM((128, GROUP), BF),
                pltpu.VMEM((GROUP, HEAD_DIM), BF),
                pltpu.VMEM((GROUP, 128), F32),
            ],
        ),
        compiler_params=params(60),
        cost_estimate=cost(20),
        name="attend_back",
    )(at, *q, *kv, do, *o, *lse, ids)


def feed_kernel(at, *refs):
    blocks, refs = refs[:8], refs[8:]
    x, w_out, sv, rows, bias, dy, resid_out, att_out, y_out, dn2_other, dn2_own, w1_out, w2_out, b1_out = refs[:14]
    wide, w1, w2, b1, w1_grad, w2_grad = refs[14:]
    step = pl.program_id(0)
    z, core = at[1], at[2]
    own = step >= 1

    @pl.when(step == 0)
    def _():
        for j in range(16):
            w1[j * 64 : j * 64 + 32, :] = rows[j, 0:32, 0:512]
            w1[j * 64 + 32 : j * 64 + 64, :] = rows[j, 0:32, 512:1024]
            w2[j * 32 : j * 32 + 32, :] = rows[j, 32:64, :]
            b1[0:1, j * 32 : j * 32 + 32] = bias[j, 0:1, 0:32].astype(F32)
        b1_out[...] = jnp.zeros_like(b1_out)
        w1_grad[...] = jnp.zeros_like(w1_grad)
        w2_grad[...] = jnp.zeros_like(w2_grad)

    for k in range(4):
        mine, theirs = (block[:, 0].reshape(4 * TOK, 128) for block in (blocks[k], blocks[4 + k]))
        one = jnp.where(core == 0, mine, theirs)
        two = jnp.where(core == 0, theirs, mine)
        for h in range(2):
            lane = pl.multiple_of(h * 512 + ((z + k) % 4) * 128, 128)
            here = slice(h * 64, h * 64 + 64)
            wide[:, pl.ds(lane, 128)] = jnp.concatenate([one[:, here], two[:, here]], 1)
    resid = x[:, 0].reshape(4 * TOK, D).astype(F32) + dot(wide[...], w_out[...]) + sv[4:5, :].astype(F32)

    for k in range(4):

        @pl.when(jnp.logical_and(own, z == k))
        def _(k=k):
            resid_out[...] = resid[k * TOK : k * TOK + TOK]
            att_out[...] = wide[k * TOK : k * TOK + TOK, :]

    center = resid - jnp.mean(resid, -1, keepdims=True)
    spread = jnp.mean(center * center, -1, keepdims=True)
    normed = (center * lax.rsqrt(spread + EPSILON) * sv[5:6, :].astype(F32) + sv[6:7, :].astype(F32)).astype(BF)
    pre = dot(normed, w1[...]) + b1[0:1, :]
    cdf = 0.5 * (1.0 + lax.erf(pre * (0.5**0.5)))
    hidden = (pre * cdf).astype(BF)
    slope = cdf + pre * jnp.exp(-0.5 * pre * pre) * 0.3989422804014327
    dy_rows = dy[:, 0].reshape(4 * TOK, D)
    hidden_grad = dot(dy_rows, w2[...], ((1,), (1,)))
    pre_grad = (hidden_grad * slope).astype(BF)
    normed_grad = dot(pre_grad, w1[...], ((1,), (1,))).astype(BF).reshape(4, TOK, D)
    y_out[:, 0] = dot(hidden, w2[...]).astype(BF).reshape(4, TOK, D)
    w2_grad[...] += dot(hidden, dy_rows, ((0,), (0,)))
    w1_grad[...] += dot(normed, pre_grad, ((0,), (0,)))
    sums = jnp.sum(pre_grad.astype(F32), 0, keepdims=True)
    for j in range(16):
        b1_out[j : j + 1, 0:32] += sums[:, j * 32 : j * 32 + 32]

    @pl.when(own)
    def _():
        dn2_own[...] = normed_grad

    @pl.when(jnp.logical_not(own))
    def _():
        dn2_other[...] = normed_grad

    @pl.when(step == 1)
    def _():
        w1_out[...] = w1_grad[...].astype(BF).reshape(16, 64, 512)
        w2_out[...] = w2_grad[...].astype(BF).reshape(16, 32, D)


def feed(at, att_own, att_other, x, w_out, sv, rows, dy):
    core_of = lambda i, at: jnp.where(i >= 1, at[2], 1 - at[2])
    tok_spec = lambda width: pl.BlockSpec((4, 1, TOK, width), lambda i, at: (0, core_of(i, at), 0, 0))
    return pl.pallas_call(
        feed_kernel,
        out_shape=(
            jax.ShapeDtypeStruct((TOK, D), F32),
            jax.ShapeDtypeStruct((TOK, D), BF),
            jax.ShapeDtypeStruct((4, 2, TOK, D), BF),
            jax.ShapeDtypeStruct((4, TOK, D), BF),
            jax.ShapeDtypeStruct((4, TOK, D), BF),
            jax.ShapeDtypeStruct((16, 64, 512), BF),
            jax.ShapeDtypeStruct((16, 32, D), BF),
            jax.ShapeDtypeStruct((16, 32), F32),
        ),
        grid_spec=pltpu.PrefetchScalarGridSpec(
            num_scalar_prefetch=1,
            grid=(2,),
            in_specs=[tok_spec(128)] * 8
            + [
                tok_spec(D),
                whole(D, D),
                whole(8, D),
                whole(16, 64, D),
                pl.BlockSpec((16, 8, D), lambda i, at: (0, 8, 0)),
                tok_spec(D),
            ],
            out_specs=[
                whole(TOK, D),
                whole(TOK, D),
                tok_spec(D),
                whole(4, TOK, D),
                whole(4, TOK, D),
                whole(16, 64, 512),
                whole(16, 32, D),
                whole(16, 32),
            ],
            scratch_shapes=[
                pltpu.VMEM((4 * TOK, D), BF),
                pltpu.VMEM((D, 512), BF),
                pltpu.VMEM((512, D), BF),
                pltpu.VMEM((8, 512), F32),
                pltpu.VMEM((D, 512), F32),
                pltpu.VMEM((512, D), F32),
            ],
        ),
        compiler_params=params(56),
        cost_estimate=cost(20),
        name="out_feed",
    )(at, *att_own, *att_other, x, w_out, sv, rows, rows, dy)


def mix_kernel(at, own, came, *outs):
    for k in range(4):
        here = pl.ds((at[1] + k) % 4, 1)
        outs[k][...] = (own[here][0].astype(F32) + came[here][0].astype(F32)).astype(BF)


def mix(at, own, came):
    return pl.pallas_call(
        mix_kernel,
        out_shape=[jax.ShapeDtypeStruct((TOK, D), BF)] * 4,
        grid_spec=pltpu.PrefetchScalarGridSpec(
            num_scalar_prefetch=1,
            grid=(1,),
            in_specs=[whole(4, TOK, D)] * 2,
            out_specs=[whole(TOK, D)] * 4,
        ),
        compiler_params=params(60),
        cost_estimate=cost(2),
        name="mix",
    )(at, own, came)


def norm_back(values, gain, grad):
    center = values - jnp.mean(values, -1, keepdims=True)
    spread = jnp.mean(center * center, -1, keepdims=True)
    r = lax.rsqrt(spread + EPSILON)
    n = center * r
    e = grad * gain
    inner = r * (e - jnp.mean(e, -1, keepdims=True) - n * jnp.mean(e * n, -1, keepdims=True))
    return inner, jnp.sum(grad * n, 0, keepdims=True), jnp.sum(grad, 0, keepdims=True)


def middle_kernel(m0, m1, m2, m3, resid, dy, sv, w_out, resid_grad_out, branch_out, att_grad_out, sums):
    grad = m0[...].astype(F32) + m1[...].astype(F32) + m2[...].astype(F32) + m3[...].astype(F32)
    dy_f = dy[...].astype(F32)
    part, gain_grad, shift_grad = norm_back(resid[...], sv[5:6, :].astype(F32), grad)
    resid_grad = dy_f + part
    resid_grad_out[...] = resid_grad
    branch = resid_grad.astype(BF)
    branch_out[...] = branch
    sums[0:1, :] = jnp.sum(branch.astype(F32), 0, keepdims=True)
    sums[1:2, :] = gain_grad
    sums[2:3, :] = shift_grad
    sums[3:4, :] = jnp.sum(dy_f, 0, keepdims=True)
    att_grad = dot(branch, w_out[...], ((1,), (1,))).astype(BF)
    for h in range(HEADS):
        lane = h * 64
        att_grad_out[h] = jnp.concatenate(
            [att_grad[0:80, lane : lane + 64], att_grad[80:160, lane : lane + 64]], 1
        )


def middle(parts, resid, dy, sv, w_out):
    return pl.pallas_call(
        middle_kernel,
        out_shape=(
            jax.ShapeDtypeStruct((TOK, D), F32),
            jax.ShapeDtypeStruct((TOK, D), BF),
            jax.ShapeDtypeStruct((HEADS, TOK // 2, 128), BF),
            jax.ShapeDtypeStruct((4, D), F32),
        ),
        grid=(1,),
        in_specs=[whole(TOK, D)] * 6 + [whole(8, D), whole(D, D)],
        out_specs=[whole(TOK, D), whole(TOK, D), whole(HEADS, TOK // 2, 128), whole(4, D)],
        compiler_params=params(60),
        cost_estimate=cost(5),
        name="middle",
    )(*parts, resid, dy, sv, w_out)


def last_kernel(g_a, g_b, w, x, resid_grad, sv, out, sums, biases, total):
    step = pl.program_id(0)

    @pl.when(step == 0)
    def _():
        total[...] = jnp.zeros_like(total)

    for k in range(2):
        pair = []
        for packed in (g_a[k], g_b[k]):
            values = jnp.concatenate([packed[160:240, 0:64], packed[160:240, 64:128]], 0)
            pair += [packed[0:160, :], values]
        pair = jnp.concatenate(pair, 1)
        total[...] += dot(pair, w[k], ((1,), (1,)))
        biases[k] = jnp.sum(pair.astype(F32), 0, keepdims=True)

    @pl.when(step == 3)
    def _():
        part, gain_grad, shift_grad = norm_back(x[...].astype(F32), sv[0:1, :].astype(F32), total[...])
        out[...] = (resid_grad[...] + part).astype(BF)
        sums[0:1, :] = gain_grad
        sums[1:2, :] = shift_grad


def last(g, w, x, resid_grad, sv):
    return pl.pallas_call(
        last_kernel,
        out_shape=(
            jax.ShapeDtypeStruct((TOK, D), BF),
            jax.ShapeDtypeStruct((2, D), F32),
            jax.ShapeDtypeStruct((8, 1, 384), F32),
        ),
        grid=(4,),
        in_specs=[
            pl.BlockSpec((2, 240, 128), lambda i: (i, 0, 0)),
            pl.BlockSpec((2, 240, 128), lambda i: (i + 4, 0, 0)),
            pl.BlockSpec((2, D, 384), lambda i: (i, 0, 0)),
            whole(TOK, D),
            whole(TOK, D),
            whole(8, D),
        ],
        out_specs=[whole(TOK, D), whole(2, D), pl.BlockSpec((2, 1, 384), lambda i: (i, 0, 0))],
        scratch_shapes=[pltpu.VMEM((TOK, D), F32)],
        compiler_params=params(48),
        cost_estimate=cost(15),
        name="last",
    )(g, g, w, x, resid_grad, sv)


def body(
    inputs,
    image_ids,
    ln1_gain,
    ln1_shift,
    qkv_weight,
    query_bias,
    value_bias,
    out_weight,
    out_bias,
    ln2_gain,
    ln2_shift,
    fc1_weight,
    fc1_bias,
    fc2_weight,
    fc2_bias,
    out_grad,
):
    xi, yl, yh, zi, ci = (lax.axis_index(name) for name in ALL)
    zc = zi * 2 + ci
    where_at = jnp.arange(16)
    starts = jnp.sum((image_ids[:, None] < where_at[None, :] - 4).astype(jnp.int32), 0)
    at = jnp.where(where_at == 0, yh, jnp.where(where_at == 1, zi, jnp.where(where_at == 2, ci, yh * 8 + zc)))
    at = jnp.where(where_at < 4, at, starts).astype(jnp.int32)

    near = lax.all_gather(inputs, TP, axis=0, tiled=True).reshape(4, 2, TOK, D)
    crossed = along(inputs, "yh", 1)

    qkv = qkv_weight.reshape(8, 3, 2, 8, HEAD_DIM).transpose(3, 0, 2, 1, 4).reshape(8, 8, 384)
    small = jnp.stack(
        [ln1_gain, ln1_shift, query_bias, value_bias, out_bias, ln2_gain, ln2_shift, fc2_bias], 1
    )
    small = jnp.broadcast_to(jnp.pad(small, ((0, 0), (0, 120)))[None], (8, 8, 128))
    fc1 = fc1_weight.reshape(8, 16, 8, 32).transpose(2, 0, 1, 3).reshape(8, 8, 512)
    columns = exchange(jnp.concatenate([qkv, small, fc1], 2), TP)
    far = lax.all_gather(after(crossed, columns), TP, axis=0, tiled=True).reshape(4, 2, TOK, D)
    columns = columns.reshape(64, D)

    fc1 = jnp.concatenate([columns[0:32, 512:], columns[32:64, 512:]], 1)
    columns = jnp.concatenate([columns[0:32, 0:512], columns[32:64, 0:512]], 1)
    spread = lambda v: exchange(jnp.broadcast_to(v[None], (16, *v.shape)), XY)
    first = spread(jnp.concatenate([columns, out_weight], 0))
    bias = jnp.pad(fc1_bias[None], ((0, 7), (0, D - 32)))
    rows = spread(after(jnp.concatenate([fc1, fc2_weight, bias], 0), first))
    sv = jnp.concatenate([first[:, 0:32, 384:392], first[:, 0:32, 896:904]], 1).reshape(D, 8).T
    sent = jnp.concatenate([out_grad, first[:, 32:40].reshape(128, D)], 0)
    sent = lax.all_gather(sent, TP, axis=0, tiled=False)
    w_out = sent[:, TOK:].reshape(8, 16, 8, D).transpose(1, 0, 2, 3).reshape(D, D)
    dy_all = sent.reshape(4, 2, TOK + 128, D)

    ids = image_ids.reshape(2, 1, HALF)
    n1_near, n1_far, q_near, kv_near, q_far, kv_far, heads, att_far, o_far, lse_far = project(
        at, near, far, first, sv, ids
    )
    q, kv = (q_near, q_far), (kv_near, kv_far)
    theirs = along(att_far, "yh", 1)
    att_near, o_near, lse_near = attend(at, 0, after(q[0], att_far), kv, ids)
    att_two = jnp.where(
        yh == 0, jnp.concatenate([att_near, theirs], 1), jnp.concatenate([theirs, att_near], 1)
    )
    att_two = after(att_two, rows)
    att_own = [att_two] + [from_up(att_two, k) for k in (1, 2, 3)]
    att_other = [along(after(block, w_out), "c", 1) for block in att_own]
    w_qkv = lax.all_gather(after(heads, *att_other), TP, axis=0, tiled=False)
    split = lambda blocks: [block.reshape(4, 2, TOK, 128) for block in blocks]
    resid, att_tok, y_part, dn2_other, dn2_own, fc1_grad, fc2_grad, b1_grad = feed(
        at, split(att_own), split(att_other), near, w_out, sv, rows, dy_all
    )

    mixed = mix(at, dn2_own, along(dn2_other, "c", 1))
    parts = [mixed[0]] + [along(mixed[k], "z", k) for k in (1, 2, 3)]
    fc2_grad = exchange(fc2_grad, XY)
    parts = [after(parts[0], fc2_grad)] + parts[1:]
    resid_grad, branch_grad, att_grad, mid_sums = middle(parts, resid, out_grad, sv, w_out)
    do = exchange(after(att_grad, w_qkv), SEQ)
    turn = ((0,), (0,))

    g, g_near, g_far = attend_back(
        at, q, kv, do, (o_near, o_far), (lse_near, lse_far), ids
    )

    out_w = dot(att_tok, branch_grad, turn).astype(BF)
    out_w = lax.psum_scatter(after(out_w, do), TP, scatter_dimension=0, tiled=True)

    fc1_grad = exchange(after(fc1_grad, do), XY)
    g_tok = exchange(after(g, fc1_grad), SEQ)
    fc1_grad = jnp.sum(fc1_grad.astype(F32), 0).reshape(8, 8, 512)
    fc1_grad = exchange(after(fc1_grad, g_tok), TP)
    fc1_grad = fc1_grad.reshape(8, 8, 16, 32).transpose(1, 2, 0, 3).reshape(8, FF)

    summed = lax.psum_scatter(after(y_part, *parts).reshape(HALF, D), TP, scatter_dimension=0, tiled=True)
    outputs = resid + summed.astype(F32) + sv[7].astype(F32)

    qkv_grad = dot(n1_near.reshape(HALF, D), g_near, turn) + dot(n1_far.reshape(HALF, D), g_far, turn)
    qkv_grad = qkv_grad.astype(BF)
    pick = lambda v, axis, place: lax.dynamic_index_in_dim(v, place, axis, keepdims=False)
    out_w = after(out_w, qkv_grad).reshape(4, 2, 2, 8, D)
    total = pick(out_w, 0, xi).astype(F32)
    for k in (1, 2, 3):
        total = total + along(pick(out_w, 0, (xi + k) % 4), "x", k).astype(F32)
    out_w = total.astype(BF)
    g_tok = after(g_tok, out_w)
    input_grad, norm_sums, biases = last(g_tok, w_qkv, inputs, resid_grad, sv)
    fc2_grad = jnp.sum(after(fc2_grad, norm_sums).astype(F32), 0)
    biases = biases.reshape(8, 2, 3, HEAD_DIM).transpose(2, 1, 0, 3).reshape(3, D)
    vectors = jnp.concatenate([norm_sums, biases[0:1], biases[2:3], mid_sums])
    vectors = vectors.reshape(8, 128, 8).transpose(1, 0, 2)
    mine = jnp.arange(8)[None, :, None] == zc
    b1_part = jnp.where(mine, b1_grad[:, None], 0.0).reshape(128, 4, 8)
    b1_part = jnp.pad(b1_part, ((0, 0), (0, 4), (0, 0)))
    vectors = jnp.concatenate([vectors, b1_part], 2)
    high = vectors.astype(BF)
    low = (vectors - high.astype(F32)).astype(BF)

    final = jnp.concatenate([qkv_grad.reshape(128, 8, 192), high, low], 2)
    final = after(final, out_w)
    out_w = after(out_w, norm_sums)
    by_y = lambda y: pick(pick(out_w, 0, y % 2), 0, y // 2)
    yi = yh * 2 + yl
    total = by_y(yi).astype(F32)
    for k in (1, 2, 3):
        total = total + along_y(by_y((yi + k) % 4), k).astype(F32)
    out_w = lax.ppermute(total, ALL, [(j * 8 + s, (2 * s + j // 8) * 8 + j % 8) for j in range(16) for s in range(8)])
    final = exchange(final, ALL).astype(F32)
    qkv_grad = jnp.sum(final[:, :, 0:192].reshape(8, HEADS, 8, 192), 0)
    qkv_grad = qkv_grad.reshape(HEADS, 8, 3, HEAD_DIM).transpose(1, 2, 0, 3).reshape(8, 3 * D)
    vectors = jnp.sum(final[:, :, 192:208] + final[:, :, 208:224], 0)
    fc1_bias_grad = vectors[0:4, 8:16].reshape(32)
    vectors = vectors[:, 0:8]
    return (
        outputs.astype(BF),
        input_grad,
        vectors[0],
        vectors[1],
        qkv_grad,
        vectors[2],
        vectors[3],
        out_w,
        vectors[4],
        vectors[5],
        vectors[6],
        fc1_grad,
        fc1_bias_grad,
        fc2_grad,
        vectors[7],
    )


def solution(mesh):
    fine = Mesh(mesh.devices.reshape(4, 2, 2, 4, 2), ALL)
    rows = P(ALL, None)
    vec = P(ALL)
    return jax.shard_map(
        body,
        mesh=fine,
        in_specs=(rows, P(("x", "yl")), vec, vec, rows, vec, vec, rows, vec, vec, vec, rows, vec, rows, vec, rows),
        out_specs=(rows, rows, vec, vec, rows, vec, vec, rows, vec, vec, vec, rows, vec, rows, vec),
        check_vma=False,
    )
```
